32 devices in a mesh: seq: 8 (over z, y), ctx: 4 (over x, core).
Axes of the slice: x: 2, y: 2, z: 4, core: 2. Of those that a mesh axis runs over, the one named last changes fastest.
Arguments:
- tokens: bfloat16 [2, 8, 2048, 1088], P(None, 'seq', 'ctx'), may hold values from -6 to 6
- segments: int32 [2, 8, 2048], P(None, 'seq', 'ctx'), may hold values from 0 to 7, as said below
- adapter_index: int32 [2, 8], P(None, 'seq'), may hold values from 0 to 7, as said below
- norm_gains: float32 [2, 1088], replicated, may hold values from 0.25 to 1.75
- norm_shifts: float32 [2, 1088], replicated, may hold values from -4 to 4
- head_biases: float32 [2, 1088], replicated, may hold values from -4 to 4
- expand_bias: float32 [4352], replicated, may hold values from -6 to 6
- exit_biases: float32 [2, 1088], replicated, may hold values from -4 to 4
- mixing_weight: bfloat16 [1088, 3264], P('ctx', 'seq'), may hold values from -0.1875 to 0.1875
- output_weight: bfloat16 [1088, 1088], P('ctx', 'seq'), may hold values from -0.75 to 0.75
- expand_weight: bfloat16 [1088, 4352], P('ctx', 'seq'), may hold values from -0.1875 to 0.1875
- shrink_weight: bfloat16 [4352, 1088], P('ctx', 'seq'), may hold values from -0.09375 to 0.09375
- entry_adapters: bfloat16 [3, 8, 1088, 16], replicated, may hold values from -0.1875 to 0.1875
- mixing_adapters: bfloat16 [8, 16, 3264], replicated, may hold values from -0.75 to 0.75
- expand_adapters: bfloat16 [8, 16, 4352], replicated, may hold values from -0.75 to 0.75
- hidden_adapters: bfloat16 [8, 4352, 16], replicated, may hold values from -0.09375 to 0.09375
- exit_adapters: bfloat16 [2, 8, 16, 1088], replicated, may hold values from -1 to 1
- cotangent: bfloat16 [2, 8, 2048, 1088], P(None, 'seq', 'ctx'), may hold values from -6 to 6
Outputs:
- layer_output: bfloat16 [2, 8, 2048, 1088], P(None, 'seq', 'ctx')
- input_grad: bfloat16 [2, 8, 2048, 1088], P(None, 'seq', 'ctx')
- entry_grads: float32 [3, 8, 1088, 16], replicated
- mixing_grads: float32 [8, 16, 3264], replicated
- expand_grads: float32 [8, 16, 4352], replicated
- hidden_grads: float32 [8, 4352, 16], replicated
- exit_grads: float32 [2, 8, 16, 1088], replicated
The draws below stay inside these ranges and needn't reach their ends.
Inputs may be any that keep to these rules, and one draw needn't show every extreme that they name: `segments`: within each sequence the numbers start at 0 and rise by one at the first token of each document. A sequence holds either a single document or exactly 8 documents. Of the 2 sequences at one index of seq, over all micro-batches together, exactly one is a single document. `adapter_index`: every one of the 8 adapters is used by at least one sequence.
All inputs are finite; a program needn't handle non-finite values.
Results may differ from the reference program's by a relative error of at most 0.015.
Values may be sent and summed in bfloat16 or wider, within the bound.
No kernel may reach another device: no remote copies, remote signals or barrier semaphores. Data moves between devices by JAX's collectives and lax.ppermute only.
A program may use at most 256 MiB of HBM per device.

```python
import math
import jax
import jax.numpy as jnp
from jax import lax

D = 1088
HEADS = 17
HEAD_DIM = 64
FF = 4352
RANK = 16
ADAPTERS = 8
LEN = 2048
MICRO = 2
SEQ_DEV = 1
SEQS = 8


def draw_segments(key, part):
    key = jax.random.fold_in(key, 11)
    key_power, key_extra, key_whole = jax.random.split(key, 3)
    row_count = MICRO * SEQS
    top_power = int(math.log2(LEN)) - 4
    exponent = jax.random.randint(key_power, (row_count, 7), 3, top_power + 1)
    base_len = jnp.left_shift(jnp.ones_like(exponent), exponent)
    extra_len = jax.random.randint(key_extra, (row_count, 7), 0, base_len)
    bounds = jnp.cumsum(base_len + extra_len, axis=1)
    places = jnp.arange(LEN, dtype=jnp.int32)
    numbers = jnp.sum((bounds[:, None, :] <= places[None, :, None]).astype(jnp.int32), axis=-1)
    numbers = numbers.reshape(MICRO, SEQS, LEN)
    pick_member = jax.random.randint(key_whole, (SEQS // SEQ_DEV,), 0, MICRO * SEQ_DEV)
    micro_place = jnp.arange(MICRO, dtype=jnp.int32)[:, None]
    seq_place = jnp.arange(SEQS, dtype=jnp.int32)[None, :]
    member = micro_place * SEQ_DEV + seq_place % SEQ_DEV
    whole_row = member == jnp.repeat(pick_member, SEQ_DEV)[None, :]
    return jnp.where(whole_row[..., None], 0, numbers).astype(jnp.int32)


def draw_adapter_index(key, part):
    key = jax.random.fold_in(key, 23)
    key_order, key_rest, key_place = jax.random.split(key, 3)
    seq_total = MICRO * SEQS
    first_round = jax.random.permutation(key_order, ADAPTERS).astype(jnp.int32)
    remaining = jax.random.randint(key_rest, (seq_total - ADAPTERS,), 0, ADAPTERS).astype(jnp.int32)
    assigned = jnp.concatenate([first_round, remaining])
    assigned = jax.random.permutation(key_place, assigned)
    return assigned.reshape(MICRO, SEQS).astype(jnp.int32)


def shard_levels(key, extent, pieces, least, high):
    factor_of = 1.0
    for axis_at, shards_of in pieces:
        steps = jax.random.uniform(jax.random.fold_in(jax.random.fold_in(key, 6), axis_at), (shards_of,), jnp.float32, least / len(pieces), high / len(pieces))
        factor_of = factor_of * jnp.repeat(jnp.exp(steps), extent[axis_at] // shards_of).reshape((-1,) + (1,) * (len(extent) - 1 - axis_at))
    return factor_of


def gaussian(own_key, shape, scale, reach, cuts=(), held_as=jnp.bfloat16):
    gain = shard_levels(own_key, shape, cuts, -0.22, 0.18) if cuts else 1.0
    array = jax.random.normal(own_key, shape, jnp.float32) * scale * gain
    return jnp.minimum(jnp.maximum(array, -reach), reach).astype(held_as)


def setup_inputs(seed: int = 0) -> dict:
    arg_keys = jax.random.split(jax.random.key(seed), 19)
    return {
        "tokens": gaussian(arg_keys[0], (MICRO, SEQS, LEN, D), 1.0, 6.0, ((1, 8), (2, 4))),
        "segments": draw_segments(jax.random.fold_in(arg_keys[18], 71), 0),
        "adapter_index": draw_adapter_index(jax.random.fold_in(arg_keys[18], 71), 0),
        "norm_gains": jnp.clip(1.0 + 0.15 * jax.random.normal(arg_keys[3], (2, D), jnp.float32), 0.25, 1.75),
        "norm_shifts": gaussian(arg_keys[4], (2, D), 0.3, 4.0, (), jnp.float32),
        "head_biases": gaussian(arg_keys[5], (2, D), 0.3, 4.0, (), jnp.float32),
        "expand_bias": gaussian(arg_keys[6], (FF,), 0.5, 6.0, (), jnp.float32),
        "exit_biases": gaussian(arg_keys[7], (2, D), 0.3, 4.0, (), jnp.float32),
        "mixing_weight": gaussian(arg_keys[8], (D, 3 * D), D ** -0.5, 0.1875, ((0, 4), (1, 8))),
        "output_weight": gaussian(arg_keys[9], (D, D), (D // 16) ** -0.5, 0.75, ((0, 4), (1, 8))),
        "expand_weight": gaussian(arg_keys[10], (D, FF), D ** -0.5, 0.1875, ((0, 4), (1, 8))),
        "shrink_weight": gaussian(arg_keys[11], (FF, D), FF ** -0.5, 0.09375, ((0, 4), (1, 8))),
        "entry_adapters": gaussian(arg_keys[12], (3, ADAPTERS, D, RANK), D ** -0.5, 0.1875),
        "mixing_adapters": gaussian(arg_keys[13], (ADAPTERS, RANK, 3 * D), (4 * RANK) ** -0.5, 0.75),
        "expand_adapters": gaussian(arg_keys[14], (ADAPTERS, RANK, FF), (4 * RANK) ** -0.5, 0.75),
        "hidden_adapters": gaussian(arg_keys[15], (ADAPTERS, FF, RANK), FF ** -0.5, 0.09375),
        "exit_adapters": gaussian(arg_keys[16], (2, ADAPTERS, RANK, D), (2 * RANK) ** -0.5, 1.0),
        "cotangent": gaussian(arg_keys[17], (MICRO, SEQS, LEN, D), 1.0, 6.0, ((1, 8), (2, 4))),
    }


EPS = 1e-05
HIGH = lax.Precision.HIGHEST

@jax.custom_vjp
def low(v):
    return lax.optimization_barrier(v.astype(jnp.bfloat16)).astype(jnp.float32)

@jax.custom_vjp
def low_back(v):
    return v

def low_keep(v):
    return (low(v), None)

def low_pass(kept, grad):
    return (grad,)

def back_keep(v):
    return (v, None)

def back_low(kept, grad):
    return (low(grad),)
low.defvjp(low_keep, low_pass)
low_back.defvjp(back_keep, back_low)

def layer_norm(activations, scale_row, shift_row):
    middle = lax.optimization_barrier(jnp.mean(activations, axis=-1, keepdims=True))
    centred = activations - middle
    spread = lax.optimization_barrier(jnp.mean(centred * centred, axis=-1, keepdims=True))
    return centred * lax.rsqrt(spread + EPS) * scale_row + shift_row

def product(pattern, first_op, second_op):
    return jnp.einsum(pattern, first_op, second_op, precision=HIGH)

def attend(queries, key_heads, value_heads, segment):
    block_width = min(512, LEN)
    block_count = LEN // block_width
    places = jnp.arange(LEN, dtype=jnp.int32)

    def one_block(block_index):
        first_row = block_index * block_width
        query_rows = lax.dynamic_slice_in_dim(queries, first_row, block_width, 1)
        row_segment = lax.dynamic_slice_in_dim(segment, first_row, block_width, 1)
        row_place = lax.dynamic_slice_in_dim(places, first_row, block_width, 0)
        scores = low_back(product('gqhe,gkhe->ghqk', query_rows, key_heads))
        allowed = (row_segment[:, None, :, None] == segment[:, None, None, :]) & (row_place[None, None, :, None] >= places[None, None, None, :])
        weights = low(jax.nn.softmax(jnp.where(allowed, scores, -1e+30), axis=-1))
        return product('ghqk,gkhe->gqhe', weights, value_heads)
    blocks = lax.map(jax.checkpoint(one_block), jnp.arange(block_count, dtype=jnp.int32))
    return jnp.moveaxis(blocks, 0, 1).reshape(queries.shape)

def forward(tokens_in, segment, picked, trained, frozen):
    entry_table, mixing_table, expand_table, hidden_table, exit_table = trained
    norm_gains, norm_shifts, head_biases, expand_bias, exit_biases, w_mix, w_out, w_expand, w_shrink = frozen
    group_size = tokens_in.shape[0]
    chosen = product('ga,kadr->kgdr', picked, entry_table)
    mix_up = product('ga,are->gre', picked, mixing_table)
    expand_up = product('ga,arf->grf', picked, expand_table)
    hidden_down = product('ga,afr->gfr', picked, hidden_table)
    exit_up = product('ga,kard->kgrd', picked, exit_table)
    normed = low(layer_norm(tokens_in, norm_gains[0], norm_shifts[0]))
    narrow = low_back(low(product('gld,gdr->glr', normed, chosen[0])))
    mixed = product('gld,de->gle', normed, w_mix) + product('glr,gre->gle', narrow, mix_up)
    queries = low_back(low((mixed[..., :D] + head_biases[0]) * 0.125))
    key_rows = low_back(low(mixed[..., D:2 * D]))
    value_rows = low_back(low(mixed[..., 2 * D:] + head_biases[1]))
    head_shape = (group_size, LEN, HEADS, HEAD_DIM)
    attended = attend(queries.reshape(head_shape), key_rows.reshape(head_shape), value_rows.reshape(head_shape), segment)
    attended = low(low_back(attended.reshape(group_size, LEN, D)))
    narrow = low_back(low(product('gld,gdr->glr', attended, chosen[1])))
    branch = low_back(product('gld,de->gle', attended, w_out) + product('glr,grd->gld', narrow, exit_up[0]) + exit_biases[0])
    residual = tokens_in + branch
    normed = low(layer_norm(residual, norm_gains[1], norm_shifts[1]))
    narrow = low_back(low(product('gld,gdr->glr', normed, chosen[2])))
    upward = low_back(product('gld,df->glf', normed, w_expand) + product('glr,grf->glf', narrow, expand_up) + expand_bias)
    active = low(jax.nn.gelu(upward))
    narrow = low_back(low(product('glf,gfr->glr', active, hidden_down)))
    branch = low_back(product('glf,fd->gld', active, w_shrink) + product('glr,grd->gld', narrow, exit_up[1]) + exit_biases[1])
    return residual + branch

def reference(tokens, segments, adapter_index, norm_gains, norm_shifts, head_biases, expand_bias, exit_biases, mixing_weight, output_weight, expand_weight, shrink_weight, entry_adapters, mixing_adapters, expand_adapters, hidden_adapters, exit_adapters, cotangent):
    frozen = (norm_gains, norm_shifts, head_biases, expand_bias, exit_biases, mixing_weight.astype(jnp.float32), output_weight.astype(jnp.float32), expand_weight.astype(jnp.float32), shrink_weight.astype(jnp.float32))
    trained = tuple((member.astype(jnp.float32) for member in (entry_adapters, mixing_adapters, expand_adapters, hidden_adapters, exit_adapters)))
    seq_total = MICRO * SEQS
    group_size = math.gcd(max(1, 4096 // LEN), seq_total)
    group_count = seq_total // group_size
    token_groups = tokens.astype(jnp.float32).reshape(group_count, group_size, LEN, D)
    segment_groups = segments.reshape(group_count, group_size, LEN)
    picked = (adapter_index.reshape(group_count, group_size)[..., None] == jnp.arange(ADAPTERS, dtype=jnp.int32)).astype(jnp.float32)
    tangent_groups = cotangent.astype(jnp.float32).reshape(group_count, group_size, LEN, D)

    def one_group(totals, inputs):
        token_rows, segment_rows, pick_rows, tangent_rows = inputs

        def run(token_in, trained_in):
            return forward(token_in, segment_rows, pick_rows, trained_in, frozen)
        outputs, pullback = jax.vjp(run, token_rows, trained)
        token_grad, table_grads = pullback(tangent_rows)
        totals = jax.tree.map(lambda earlier, addition: earlier + addition, totals, table_grads)
        return (totals, (outputs.astype(jnp.bfloat16), token_grad.astype(jnp.bfloat16)))
    initial = jax.tree.map(jnp.zeros_like, trained)
    totals, (output_rows, grad_rows) = lax.scan(one_group, initial, (token_groups, segment_groups, picked, tangent_groups))
    full_shape = (MICRO, SEQS, LEN, D)
    return (output_rows.reshape(full_shape), grad_rows.reshape(full_shape), totals[0], totals[1], totals[2], totals[3], totals[4])
```

```python
import functools

import jax
import jax.numpy as jnp
from jax import lax
from jax.experimental import pallas as pl
from jax.experimental.pallas import tpu as pltpu
from jax.sharding import PartitionSpec as P

HEADS = 17
EPS = 1e-05
NEG = -1e30
BF = jnp.bfloat16
F32 = jnp.float32
BOTH = ("seq", "ctx")


def dotg(a,b,ca,cb):
    return lax.dot_general(a,b,(((ca,),(cb,)),((),())),preferred_element_type=jnp.float32)

def ranges(meta_ref, r, qi, qn, QB, KB, ctx, L):
    smin=meta_ref[1+(r*qn+qi)*2]; smax=meta_ref[2+(r*qn+qi)*2]
    q0=ctx*L+qi*QB
    lo=smin//KB
    hi=(q0+QB-1)//KB+1
    f0=jnp.minimum((smax+KB-1)//KB,hi)
    f1=jnp.maximum((q0+1)//KB,f0)
    return lo,f0,f1,hi,q0

def fwd_kernel(meta_ref, start_ref, q_ref, k_ref, v_ref, o_ref, l_ref, vt_ref, acc_ref, st_ref, *, QB, KB, L, xorder):
    r=pl.program_id(0)
    ctx=meta_ref[0]
    qn=L//QB; per=L//KB
    vt_ref[...]=v_ref[0].T
    lane=lax.broadcasted_iota(jnp.int32,(1,128),1)
    for qi in range(qn):
        lo,f0,f1,hi,q0=ranges(meta_ref,r,qi,qn,QB,KB,ctx,L)
        q2=q_ref[0,qi*QB:(qi+1)*QB,:]
        qh=[jnp.where(lane<64,q2,0).astype(q2.dtype),jnp.where(lane>=64,q2,0).astype(q2.dtype)]
        start=start_ref[0,:,qi*QB:(qi+1)*QB]
        acc_ref[...]=jnp.zeros_like(acc_ref)
        st_ref[0:2,:]=jnp.full((2,QB),NEG,jnp.float32)
        st_ref[2:4,:]=jnp.zeros((2,QB),jnp.float32)
        def body(t,_,masked):
            b=t//per
            rel=(b^ctx) if xorder else b
            off=pl.multiple_of(rel*L+(t-b*per)*KB,KB)
            kt=k_ref[0,pl.ds(off,KB),:]
            if masked:
                kpos=lax.broadcasted_iota(jnp.int32,(KB,1),0)+t*KB
                qpos=lax.broadcasted_iota(jnp.int32,(1,QB),1)+q0
                ok=(kpos<=qpos)&(kpos>=start)
            for h in range(2):
                s=dotg(kt,qh[h],1,1)
                if masked: s=jnp.where(ok,s,NEG)
                m=st_ref[h:h+1,:]
                mn=jnp.maximum(m,jnp.max(s,axis=0,keepdims=True))
                al=jnp.exp(m-mn)
                p=jnp.exp(s-mn)
                if masked: p=jnp.where(ok,p,0.0)
                st_ref[2+h:3+h,:]=st_ref[2+h:3+h,:]*al+jnp.sum(p,axis=0,keepdims=True)
                st_ref[h:h+1,:]=mn
                vt=vt_ref[h*64:(h+1)*64,pl.ds(off,KB)]
                acc_ref[h*64:(h+1)*64,:]=acc_ref[h*64:(h+1)*64,:]*al+dotg(vt,p.astype(jnp.bfloat16),1,0)
            return 0
        lax.fori_loop(lo,f0,lambda t,c: body(t,c,True),0)
        lax.fori_loop(f0,f1,lambda t,c: body(t,c,False),0)
        lax.fori_loop(f1,hi,lambda t,c: body(t,c,True),0)
        for h in range(2):
            l=st_ref[2+h:3+h,:]
            l_ref[0,0,h:h+1,qi*QB:(qi+1)*QB]=st_ref[h:h+1,:]+jnp.log(l)
            acc_ref[h*64:(h+1)*64,:]=acc_ref[h*64:(h+1)*64,:]/l
        o_ref[0,qi*QB:(qi+1)*QB,:]=acc_ref[...].T.astype(o_ref.dtype)

def attn_fwd(meta,start,q,k,v,*,QB=256,KB=256,xorder=True):
    R,L,W=q.shape; T=k.shape[1]; NP=W//128
    kern=functools.partial(fwd_kernel,QB=QB,KB=KB,L=L,xorder=xorder)
    return pl.pallas_call(kern,
        grid_spec=pltpu.PrefetchScalarGridSpec(num_scalar_prefetch=1,grid=(R,NP),
            in_specs=[pl.BlockSpec((1,1,L),lambda r,p,m:(r,0,0)),
                      pl.BlockSpec((1,L,128),lambda r,p,m:(r,0,p)),
                      pl.BlockSpec((1,T,128),lambda r,p,m:(r,0,p)),
                      pl.BlockSpec((1,T,128),lambda r,p,m:(r,0,p))],
            out_specs=[pl.BlockSpec((1,L,128),lambda r,p,m:(r,0,p)),
                       pl.BlockSpec((1,1,2,L),lambda r,p,m:(r,p,0,0))],
            scratch_shapes=[pltpu.VMEM((128,T),jnp.bfloat16),pltpu.VMEM((128,QB),jnp.float32),pltpu.VMEM((8,QB),jnp.float32)]),
        out_shape=[jax.ShapeDtypeStruct((R,L,1088),jnp.bfloat16),jax.ShapeDtypeStruct((R,NP,2,L),jnp.float32)],
        compiler_params=pltpu.CompilerParams(dimension_semantics=("arbitrary","arbitrary"),vmem_limit_bytes=48<<20),
        cost_estimate=pl.CostEstimate(flops=R*4*L*T*W,bytes_accessed=R*(2*L+2*T)*W*2,transcendentals=R*L*T*18),
        name="attn_fwd")(meta,start,q,k,v)

def bwd_kernel(meta_ref, start_ref, q_ref, k_ref, v_ref, do_ref, o_ref, l_ref, dq_ref, dk_ref, dv_ref,
               kt_ref, dqt_ref, dkt_ref, dvt_ref, *, QB, KB, L, xorder, nheads, r0):
    r=pl.program_id(0)+r0
    ctx=meta_ref[0]
    qn=L//QB; per=L//KB
    kt_ref[...]=k_ref[0].T
    lane=lax.broadcasted_iota(jnp.int32,(1,128),1)
    lane_lim=nheads*64-pl.program_id(1)*128
    dkt_ref[...]=jnp.zeros_like(dkt_ref)
    dvt_ref[...]=jnp.zeros_like(dvt_ref)
    for qi in range(qn):
        lo,f0,f1,hi,q0=ranges(meta_ref,r,qi,qn,QB,KB,ctx,L)
        q2=q_ref[0,qi*QB:(qi+1)*QB,:]
        do2=do_ref[0,qi*QB:(qi+1)*QB,:]
        do2=jnp.where(lane<lane_lim,do2,0).astype(do2.dtype)
        o2=o_ref[0,qi*QB:(qi+1)*QB,:]
        o2=jnp.where(lane<lane_lim,o2,0).astype(o2.dtype)
        qh=[jnp.where(lane<64,q2,0).astype(q2.dtype),jnp.where(lane>=64,q2,0).astype(q2.dtype)]
        dh=[jnp.where(lane<64,do2,0).astype(q2.dtype),jnp.where(lane>=64,do2,0).astype(q2.dtype)]
        qt=q2.T; dot_=do2.T
        prod=(do2.astype(jnp.float32)*o2.astype(jnp.float32)).T
        dl=[jnp.sum(prod[h*64:(h+1)*64],axis=0,keepdims=True) for h in range(2)]
        lrow=[l_ref[0,0,h:h+1,qi*QB:(qi+1)*QB] for h in range(2)]
        start=start_ref[0,:,qi*QB:(qi+1)*QB]
        dqt_ref[...]=jnp.zeros_like(dqt_ref)
        def body(t,_,masked):
            b=t//per
            rel=(b^ctx) if xorder else b
            off=pl.multiple_of(rel*L+(t-b*per)*KB,KB)
            kt=k_ref[0,pl.ds(off,KB),:]
            vt=v_ref[0,pl.ds(off,KB),:]
            if masked:
                kpos=lax.broadcasted_iota(jnp.int32,(KB,1),0)+t*KB
                qpos=lax.broadcasted_iota(jnp.int32,(1,QB),1)+q0
                ok=(kpos<=qpos)&(kpos>=start)
            for h in range(2):
                hs=slice(h*64,(h+1)*64)
                s=dotg(kt,qh[h],1,1)
                dp=dotg(vt,dh[h],1,1)
                p=jnp.exp(s-lrow[h])
                if masked: p=jnp.where(ok,p,0.0)
                pb=p.astype(jnp.bfloat16)
                ds=(p*(dp-dl[h])).astype(jnp.bfloat16)
                dvt_ref[hs,pl.ds(off,KB)]+=dotg(dot_[hs],pb,1,1)
                dkt_ref[hs,pl.ds(off,KB)]+=dotg(qt[hs],ds,1,1)
                dqt_ref[hs,:]+=dotg(kt_ref[hs,pl.ds(off,KB)],ds,1,0)
            return 0
        lax.fori_loop(lo,f0,lambda t,c: body(t,c,True),0)
        lax.fori_loop(f0,f1,lambda t,c: body(t,c,False),0)
        lax.fori_loop(f1,hi,lambda t,c: body(t,c,True),0)
        dq_ref[0,qi*QB:(qi+1)*QB,:]=(dqt_ref[...].T).astype(dq_ref.dtype)*jnp.bfloat16(0.125)
    dk_ref[0]=dkt_ref[...].T.astype(dk_ref.dtype)
    dv_ref[0]=dvt_ref[...].T.astype(dv_ref.dtype)

def attn_bwd(meta,start,q,k,v,do,o,lse,*,QB=256,KB=256,xorder=True,nheads=17,r0=0):
    _,L,W=q.shape; T=k.shape[1]; NP=W//128; R=1
    kern=functools.partial(bwd_kernel,QB=QB,KB=KB,L=L,xorder=xorder,nheads=nheads,r0=r0)
    full=lambda r,p,m:(r+r0,0,p)
    return pl.pallas_call(kern,
        grid_spec=pltpu.PrefetchScalarGridSpec(num_scalar_prefetch=1,grid=(R,NP),
            in_specs=[pl.BlockSpec((1,1,L),lambda r,p,m:(r+r0,0,0)),
                      pl.BlockSpec((1,L,128),full),
                      pl.BlockSpec((1,T,128),full),
                      pl.BlockSpec((1,T,128),full),
                      pl.BlockSpec((1,L,128),full),
                      pl.BlockSpec((1,L,128),full),
                      pl.BlockSpec((1,1,2,L),lambda r,p,m:(r+r0,p,0,0))],
            out_specs=[pl.BlockSpec((1,L,128),lambda r,p,m:(r,0,p)),
                       pl.BlockSpec((1,T,128),lambda r,p,m:(r,0,p)),
                       pl.BlockSpec((1,T,128),lambda r,p,m:(r,0,p))],
            scratch_shapes=[pltpu.VMEM((128,T),jnp.bfloat16),pltpu.VMEM((128,QB),jnp.float32),
                            pltpu.VMEM((128,T),jnp.float32),pltpu.VMEM((128,T),jnp.float32)]),
        out_shape=[jax.ShapeDtypeStruct((R,L,W),jnp.bfloat16),jax.ShapeDtypeStruct((R,T,W),jnp.bfloat16),jax.ShapeDtypeStruct((R,T,W),jnp.bfloat16)],
        compiler_params=pltpu.CompilerParams(dimension_semantics=("arbitrary","arbitrary"),vmem_limit_bytes=48<<20),
        cost_estimate=pl.CostEstimate(flops=R*10*L*T*W,bytes_accessed=R*(3*L+4*T)*W*2,transcendentals=R*L*T*18),
        name="attn_bwd")(meta,start,q,k,v,do,o,lse)


def mm(pattern, a, b):
    return jnp.einsum(pattern, a, b, preferred_element_type=F32)


def unpack_kernel(w_ref, *outs, pieces, rows, halves):
    for half in range(halves):
        for out, (first, width, places, pad) in zip(outs, pieces):
            whole = [
                w_ref[s, 0, :, half * (w_ref.shape[3] // halves) + first : half * (w_ref.shape[3] // halves) + first + width]
                for s in range(w_ref.shape[0])
            ]
            joined = jnp.concatenate(whole, axis=1)
            if pad:
                zero = jnp.zeros((rows, pad), joined.dtype)
                step = joined.shape[1] // places
                joined = jnp.concatenate(
                    [x for i in range(places) for x in (joined[:, i * step : (i + 1) * step], zero)], axis=1
                )
            out[0, half] = joined


def layer_stats(v):
    middle = jnp.mean(v, axis=-1, keepdims=True)
    centred = v - middle
    inv = lax.rsqrt(jnp.mean(centred * centred, axis=-1, keepdims=True) + EPS)
    return centred * inv, inv


def norm_back(e, z, inv):
    return (e - jnp.mean(e, -1, keepdims=True) - z * jnp.mean(e * z, -1, keepdims=True)) * inv


def swap(x, axis, bit, needed):
    n = lax.axis_size(axis)
    return lax.ppermute(x, axis, [(d ^ bit, d) for d in range(n) if needed(d)])


def blocks_of(x, bits):
    found = {0: x}
    for bit in reversed(bits):
        for j in sorted(found):
            found[j | bit] = swap(found[j], "ctx", bit, lambda d, k=j | bit: (d ^ k) < d)
    return [found[j] for j in sorted(found)]


def blocks_back(parts, bits):
    held = dict(enumerate(parts))
    for bit in bits:
        for j in sorted(held):
            if j & bit:
                sent = held.pop(j)
                got = swap(sent, "ctx", bit, lambda d, k=j, b=bit: ((d ^ b) ^ k) < (d ^ b))
                held[j ^ bit] = held[j ^ bit] + got
    return held[0]


def ctx_sum_rows(g, bits):
    n = lax.axis_size("ctx")
    me = lax.axis_index("ctx")
    for bit in reversed(bits):
        half = g.shape[0] // 2
        mine = (me & bit) != 0
        low, high = g[:half], g[half:]
        got = lax.ppermute(jnp.where(mine, low, high), "ctx", [(d, d ^ bit) for d in range(n)])
        g = jnp.where(mine, high, low) + got
    return g


def slots_kernel(index_ref, g_ref, *refs, count, spans):
    outs, total = refs[:-1], refs[-1]
    total[...] = jnp.zeros_like(total)

    def one(i, carry):
        a = index_ref[i]
        total[a] = total[a] + g_ref[i].astype(F32)
        return carry

    lax.fori_loop(0, count, one, 0)
    for out, (first, width) in zip(outs, spans):
        out[...] = total[:, :, first : first + width]


def to_slots(index, g, adapters, widths):
    count, rank, wide = g.shape
    rows = 8
    spans, at = [], 0
    for w in widths:
        spans.append((at, w))
        at += w
    return pl.pallas_call(
        functools.partial(slots_kernel, count=count, spans=spans),
        grid_spec=pltpu.PrefetchScalarGridSpec(
            num_scalar_prefetch=1,
            grid=(rank // rows,),
            in_specs=[pl.BlockSpec((count, rows, wide), lambda i, m: (0, i, 0))],
            out_specs=[pl.BlockSpec((adapters, rows, w), lambda i, m: (0, i, 0)) for w in widths],
            scratch_shapes=[pltpu.VMEM((adapters, rows, wide), F32)],
        ),
        out_shape=[jax.ShapeDtypeStruct((adapters, rank, w), F32) for w in widths],
        compiler_params=pltpu.CompilerParams(vmem_limit_bytes=48 << 20),
        cost_estimate=pl.CostEstimate(
            flops=count * rank * wide, bytes_accessed=count * rank * wide * 2 + adapters * rank * wide * 4, transcendentals=0
        ),
        name="to_slots",
    )(index, g)


def per_device(
    tokens, segments, adapter_index, norm_gains, norm_shifts, head_biases, expand_bias, exit_biases,
    mixing_weight, output_weight, expand_weight, shrink_weight,
    entry_adapters, mixing_adapters, expand_adapters, hidden_adapters, exit_adapters, cotangent,
):
    micro, seqs, L, D = tokens.shape
    R = micro * seqs
    adapters, rank = mixing_adapters.shape[:2]
    FF = expand_bias.shape[0]
    C = lax.axis_size("ctx")
    S = lax.axis_size("seq")
    bits = [1 << i for i in range(C.bit_length() - 1)]
    me = lax.axis_index("ctx")
    T = C * L
    W = -(-D // 128) * 128
    pad = W - D

    rows = mixing_weight.shape[0]
    cm, co, ce = mixing_weight.shape[1], output_weight.shape[1], expand_weight.shape[1]
    first = jnp.concatenate([mixing_weight, output_weight], 1)
    first = jnp.concatenate([first[: rows // 2], first[rows // 2 :]], 1)
    second = jnp.concatenate([expand_weight[: rows // 2], expand_weight[rows // 2 :]], 1)
    third = shrink_weight.T
    g1 = lax.all_gather(first, BOTH)
    if second.shape[1] == third.shape[1]:
        g2 = lax.all_gather(jnp.concatenate([second, third], 0), BOTH)
        g2, g3 = g2[:, : rows // 2], g2[:, rows // 2 :]
    else:
        g2, g3 = lax.all_gather(second, BOTH), lax.all_gather(third, BOTH)

    def join(g, width):
        r = g.shape[1]
        g = g.reshape(S, C, r, 2, width).transpose(1, 3, 2, 0, 4)
        return g.reshape(C * 2 * r, S, width)

    w1 = join(g1, cm + co)
    w_mix = w1[:, :, :cm].reshape(D, 3 * D)
    w_out = w1[:, :, cm:].reshape(D, D)
    padded = lambda m: jnp.pad(m, [(0, 0)] * (m.ndim - 1) + [(0, pad)])
    w_q, w_k, w_v = (padded(w_mix[:, i * D : (i + 1) * D]) for i in range(3))
    w_exp = join(g2, ce).reshape(D, FF)
    w_shr_t = g3.reshape(S, C, D // S, FF // C).transpose(0, 2, 1, 3).reshape(D, FF)

    index = adapter_index.reshape(R)
    take = lambda table, axis: jnp.stack(
        [lax.dynamic_index_in_dim(table, index[r], axis, keepdims=False) for r in range(R)], axis
    )
    entry = take(entry_adapters, 1)
    mix_up = take(mixing_adapters, 0)
    exp_up = take(expand_adapters, 0)
    hid = take(hidden_adapters, 0)
    exit_up = take(exit_adapters, 1)
    m_q, m_k, m_v = (padded(mix_up[..., i * D : (i + 1) * D]) for i in range(3))
    all_index = lax.all_gather(index, "seq").reshape(S * R)

    seg = segments.reshape(R, L)
    seg_blocks = blocks_of(seg, bits)
    start = jnp.zeros((R, L), jnp.int32)
    for j, other in enumerate(seg_blocks):
        ok = (me ^ j) <= me
        start = start + jnp.sum(((other[:, None, :] < seg[:, :, None]) & ok).astype(jnp.int32), -1)
    QB = KB = min(512, L)
    meta = jnp.concatenate(
        [me[None].astype(jnp.int32)]
        + [start[r, (qi + e) * QB - e][None] for r in range(R) for qi in range(L // QB) for e in (0, 1)]
    )
    start = start[:, None, :]

    x = tokens.reshape(R, L, D).astype(F32)
    dy = cotangent.reshape(R, L, D)
    z1, inv1 = layer_stats(x)
    n1 = (z1 * norm_gains[0] + norm_shifts[0]).astype(BF)
    n1_all = jnp.concatenate(blocks_of(n1, bits), 1)
    l1_all = mm("rtd,rdk->rtk", n1_all, entry[0]).astype(BF)
    l1 = l1_all[:, :L]
    q = ((mm("rtd,de->rte", n1, w_q) + mm("rtk,rke->rte", l1, m_q) + padded(head_biases[0])) * 0.125).astype(BF)
    k = (mm("rtd,de->rte", n1_all, w_k) + mm("rtk,rke->rte", l1_all, m_k)).astype(BF)
    v = (mm("rtd,de->rte", n1_all, w_v) + mm("rtk,rke->rte", l1_all, m_v) + padded(head_biases[1])).astype(BF)

    o, lse = attn_fwd(meta, start, q, k, v, QB=QB, KB=KB)

    lo = mm("rtd,rdk->rtk", o, entry[1]).astype(BF)
    res = x + mm("rtd,de->rte", o, w_out) + mm("rtk,rke->rte", lo, exit_up[0]) + exit_biases[0]
    z2, inv2 = layer_stats(res)
    n2 = (z2 * norm_gains[1] + norm_shifts[1]).astype(BF)
    l3 = mm("rtd,rdk->rtk", n2, entry[2]).astype(BF)
    h = mm("rtd,df->rtf", n2, w_exp) + mm("rtk,rkf->rtf", l3, exp_up) + expand_bias
    c0 = 0.7978845608028654
    hh = h * h
    th = jnp.tanh(c0 * h * (1.0 + 0.044715 * hh))
    g = (0.5 * h * (1.0 + th)).astype(BF)
    slope = 0.5 * (1.0 + th) + 0.5 * h * (1.0 - th * th) * (c0 * (1.0 + 3 * 0.044715 * hh))
    l4 = mm("rtf,rfk->rtk", g, hid).astype(BF)
    out = res + mm("rtf,df->rtd", g, w_shr_t) + mm("rtk,rkd->rtd", l4, exit_up[1]) + exit_biases[1]
    layer_output = out.astype(BF).reshape(tokens.shape)

    dl4 = mm("rtd,rkd->rtk", dy, exit_up[1]).astype(BF)
    dg = mm("rtd,df->rtf", dy, w_shr_t) + mm("rtk,rfk->rtf", dl4, hid)
    dh = (dg * slope).astype(BF)
    dl3 = mm("rtf,rkf->rtk", dh, exp_up).astype(BF)
    dn2 = mm("rtf,df->rtd", dh, w_exp) + mm("rtk,rdk->rtd", dl3, entry[2])
    dr = dy.astype(F32) + norm_back(norm_gains[1] * dn2, z2, inv2)
    drb = dr.astype(BF)
    dl2 = mm("rtd,rkd->rtk", drb, exit_up[0]).astype(BF)
    do = (mm("rtd,ed->rte", drb, w_out) + mm("rtk,rdk->rtd", dl2, entry[1])).astype(BF)

    early = jnp.concatenate(
        [
            mm("rtk,rtd->rkd", dl2, o),
            mm("rtk,rtd->rkd", dl3, n2),
            mm("rtk,rtf->rkf", l3, dh),
            mm("rtk,rtf->rkf", dl4, g),
            mm("rtk,rtd->rkd", lo, drb),
            mm("rtk,rtd->rkd", l4, dy),
        ],
        -1,
    ).reshape(R * rank, -1)
    early = ctx_sum_rows(early, bits).astype(BF)
    early = lax.all_gather(early, BOTH).reshape(S * R, rank, -1)
    entry1_g, entry2_g, expand_g, hidden_g, exit0_g, exit1_g = to_slots(
        all_index, early, adapters, (D, D, FF, FF, D, D)
    )

    own, late = [], []
    for r in range(R):
        dq, dk, dv = attn_bwd(meta, start, q, k, v, do, o, lse, QB=QB, KB=KB, r0=r)
        dq, dk, dv = dq[0], dk[0], dv[0]
        dl1 = mm("te,ke->tk", dk, m_k[r]) + mm("te,ke->tk", dv, m_v[r])
        dl1 = jnp.concatenate([dl1[:L] + mm("te,ke->tk", dq, m_q[r]), dl1[L:]], 0).astype(BF)
        part = mm("te,de->td", dk, w_k) + mm("te,de->td", dv, w_v) + mm("tk,dk->td", dl1, entry[0, r])
        mine = part[:L] + mm("te,de->td", dq, w_q)
        others = part[L:].astype(BF)
        parts = [mine] + [others[(j - 1) * L : j * L] for j in range(1, C)]
        own.append(blocks_back(parts, bits))
        late.append(
            jnp.concatenate(
                [
                    mm("tk,te->ke", l1[r], dq)[:, :D],
                    mm("tk,te->ke", l1_all[r], dk)[:, :D],
                    mm("tk,te->ke", l1_all[r], dv)[:, :D],
                    mm("tk,td->kd", dl1, n1_all[r]),
                ],
                -1,
            )
        )
    late = ctx_sum_rows(jnp.concatenate(late, 0), bits).astype(BF)
    late = lax.all_gather(late, BOTH).reshape(S * R, rank, -1)
    mixing_g, entry0_g = to_slots(all_index, late, adapters, (3 * D, D))

    dn1 = jnp.stack(own)
    input_grad = (dr + norm_back(norm_gains[0] * dn1, z1, inv1)).astype(BF).reshape(tokens.shape)

    flip = lambda m: jnp.swapaxes(m, -1, -2)
    return (
        layer_output,
        input_grad,
        jnp.stack([flip(entry0_g), flip(entry1_g), flip(entry2_g)]),
        mixing_g,
        expand_g,
        flip(hidden_g),
        jnp.stack([exit0_g, exit1_g]),
    )


def solution(mesh):
    rows = P(None, "seq", "ctx", None)
    weight = P("ctx", "seq")
    in_specs = (
        (rows, P(None, "seq", "ctx"), P(None, "seq")) + (P(),) * 5 + (weight,) * 4 + (P(),) * 5 + (rows,)
    )
    out_specs = (rows, rows) + (P(),) * 5
    return jax.shard_map(per_device, mesh=mesh, in_specs=in_specs, out_specs=out_specs, check_vma=False)
```

```python
import functools

import jax
import jax.numpy as jnp
from jax import lax
from jax.experimental import pallas as pl
from jax.experimental.pallas import tpu as pltpu
from jax.sharding import PartitionSpec as P

HEADS = 17
EPS = 1e-05
NEG = -1e30
BF = jnp.bfloat16
F32 = jnp.float32
BOTH = ("seq", "ctx")


def dotg(a,b,ca,cb):
    return lax.dot_general(a,b,(((ca,),(cb,)),((),())),preferred_element_type=jnp.float32)

def ranges(meta_ref, r, qi, qn, QB, KB, ctx, L):
    smin=meta_ref[1+(r*qn+qi)*2]; smax=meta_ref[2+(r*qn+qi)*2]
    q0=ctx*L+qi*QB
    lo=smin//KB
    hi=(q0+QB-1)//KB+1
    f0=jnp.minimum((smax+KB-1)//KB,hi)
    f1=jnp.maximum((q0+1)//KB,f0)
    return lo,f0,f1,hi,q0

def fwd_kernel(meta_ref, start_ref, q_ref, k_ref, v_ref, o_ref, l_ref, vt_ref, acc_ref, st_ref, *, QB, KB, L, xorder):
    r=pl.program_id(0)
    ctx=meta_ref[0]
    qn=L//QB; per=L//KB
    vt_ref[...]=v_ref[0].T
    lane=lax.broadcasted_iota(jnp.int32,(1,128),1)
    for qi in range(qn):
        lo,f0,f1,hi,q0=ranges(meta_ref,r,qi,qn,QB,KB,ctx,L)
        q2=q_ref[0,qi*QB:(qi+1)*QB,:]
        qh=[jnp.where(lane<64,q2,0).astype(q2.dtype),jnp.where(lane>=64,q2,0).astype(q2.dtype)]
        start=start_ref[0,:,qi*QB:(qi+1)*QB]
        acc_ref[...]=jnp.zeros_like(acc_ref)
        st_ref[0:2,:]=jnp.full((2,QB),NEG,jnp.float32)
        st_ref[2:4,:]=jnp.zeros((2,QB),jnp.float32)
        def body(t,_,masked):
            b=t//per
            rel=(b^ctx) if xorder else b
            off=pl.multiple_of(rel*L+(t-b*per)*KB,KB)
            kt=k_ref[0,pl.ds(off,KB),:]
            if masked:
                kpos=lax.broadcasted_iota(jnp.int32,(KB,1),0)+t*KB
                qpos=lax.broadcasted_iota(jnp.int32,(1,QB),1)+q0
                ok=(kpos<=qpos)&(kpos>=start)
            for h in range(2):
                s=dotg(kt,qh[h],1,1)
                if masked: s=jnp.where(ok,s,NEG)
                m=st_ref[h:h+1,:]
                mn=jnp.maximum(m,jnp.max(s,axis=0,keepdims=True))
                al=jnp.exp(m-mn)
                p=jnp.exp(s-mn)
                if masked: p=jnp.where(ok,p,0.0)
                st_ref[2+h:3+h,:]=st_ref[2+h:3+h,:]*al+jnp.sum(p,axis=0,keepdims=True)
                st_ref[h:h+1,:]=mn
                vt=vt_ref[h*64:(h+1)*64,pl.ds(off,KB)]
                acc_ref[h*64:(h+1)*64,:]=acc_ref[h*64:(h+1)*64,:]*al+dotg(vt,p.astype(jnp.bfloat16),1,0)
            return 0
        lax.fori_loop(lo,f0,lambda t,c: body(t,c,True),0)
        lax.fori_loop(f0,f1,lambda t,c: body(t,c,False),0)
        lax.fori_loop(f1,hi,lambda t,c: body(t,c,True),0)
        for h in range(2):
            l=st_ref[2+h:3+h,:]
            l_ref[0,0,h:h+1,qi*QB:(qi+1)*QB]=st_ref[h:h+1,:]+jnp.log(l)
            acc_ref[h*64:(h+1)*64,:]=acc_ref[h*64:(h+1)*64,:]/l
        o_ref[0,qi*QB:(qi+1)*QB,:]=acc_ref[...].T.astype(o_ref.dtype)

def attn_fwd(meta,start,q,k,v,*,QB=256,KB=256,xorder=True):
    R,L,W=q.shape; T=k.shape[1]; NP=W//128
    kern=functools.partial(fwd_kernel,QB=QB,KB=KB,L=L,xorder=xorder)
    return pl.pallas_call(kern,
        grid_spec=pltpu.PrefetchScalarGridSpec(num_scalar_prefetch=1,grid=(R,NP),
            in_specs=[pl.BlockSpec((1,1,L),lambda r,p,m:(r,0,0)),
                      pl.BlockSpec((1,L,128),lambda r,p,m:(r,0,p)),
                      pl.BlockSpec((1,T,128),lambda r,p,m:(r,0,p)),
                      pl.BlockSpec((1,T,128),lambda r,p,m:(r,0,p))],
            out_specs=[pl.BlockSpec((1,L,128),lambda r,p,m:(r,0,p)),
                       pl.BlockSpec((1,1,2,L),lambda r,p,m:(r,p,0,0))],
            scratch_shapes=[pltpu.VMEM((128,T),jnp.bfloat16),pltpu.VMEM((128,QB),jnp.float32),pltpu.VMEM((8,QB),jnp.float32)]),
        out_shape=[jax.ShapeDtypeStruct((R,L,1088),jnp.bfloat16),jax.ShapeDtypeStruct((R,NP,2,L),jnp.float32)],
        compiler_params=pltpu.CompilerParams(dimension_semantics=("arbitrary","arbitrary"),vmem_limit_bytes=48<<20),
        cost_estimate=pl.CostEstimate(flops=R*4*L*T*W,bytes_accessed=R*(2*L+2*T)*W*2,transcendentals=R*L*T*18),
        name="attn_fwd")(meta,start,q,k,v)

def bwd_kernel(meta_ref, start_ref, q_ref, k_ref, v_ref, do_ref, o_ref, l_ref, dq_ref, dk_ref, dv_ref,
               kt_ref, dqt_ref, dkt_ref, dvt_ref, *, QB, KB, L, xorder, nheads, r0):
    r=pl.program_id(0)+r0
    ctx=meta_ref[0]
    qn=L//QB; per=L//KB
    kt_ref[...]=k_ref[0].T
    lane=lax.broadcasted_iota(jnp.int32,(1,128),1)
    lane_lim=nheads*64-pl.program_id(1)*128
    dkt_ref[...]=jnp.zeros_like(dkt_ref)
    dvt_ref[...]=jnp.zeros_like(dvt_ref)
    for qi in range(qn):
        lo,f0,f1,hi,q0=ranges(meta_ref,r,qi,qn,QB,KB,ctx,L)
        q2=q_ref[0,qi*QB:(qi+1)*QB,:]
        do2=do_ref[0,qi*QB:(qi+1)*QB,:]
        do2=jnp.where(lane<lane_lim,do2,0).astype(do2.dtype)
        o2=o_ref[0,qi*QB:(qi+1)*QB,:]
        o2=jnp.where(lane<lane_lim,o2,0).astype(o2.dtype)
        qh=[jnp.where(lane<64,q2,0).astype(q2.dtype),jnp.where(lane>=64,q2,0).astype(q2.dtype)]
        dh=[jnp.where(lane<64,do2,0).astype(q2.dtype),jnp.where(lane>=64,do2,0).astype(q2.dtype)]
        qt=q2.T; dot_=do2.T
        prod=(do2.astype(jnp.float32)*o2.astype(jnp.float32)).T
        dl=[jnp.sum(prod[h*64:(h+1)*64],axis=0,keepdims=True) for h in range(2)]
        lrow=[l_ref[0,0,h:h+1,qi*QB:(qi+1)*QB] for h in range(2)]
        start=start_ref[0,:,qi*QB:(qi+1)*QB]
        dqt_ref[...]=jnp.zeros_like(dqt_ref)
        def body(t,_,masked):
            b=t//per
            rel=(b^ctx) if xorder else b
            off=pl.multiple_of(rel*L+(t-b*per)*KB,KB)
            kt=k_ref[0,pl.ds(off,KB),:]
            vt=v_ref[0,pl.ds(off,KB),:]
            if masked:
                kpos=lax.broadcasted_iota(jnp.int32,(KB,1),0)+t*KB
                qpos=lax.broadcasted_iota(jnp.int32,(1,QB),1)+q0
                ok=(kpos<=qpos)&(kpos>=start)
            for h in range(2):
                hs=slice(h*64,(h+1)*64)
                s=dotg(kt,qh[h],1,1)
                dp=dotg(vt,dh[h],1,1)
                p=jnp.exp(s-lrow[h])
                if masked: p=jnp.where(ok,p,0.0)
                pb=p.astype(jnp.bfloat16)
                ds=(p*(dp-dl[h])).astype(jnp.bfloat16)
                dvt_ref[hs,pl.ds(off,KB)]+=dotg(dot_[hs],pb,1,1)
                dkt_ref[hs,pl.ds(off,KB)]+=dotg(qt[hs],ds,1,1)
                dqt_ref[hs,:]+=dotg(kt_ref[hs,pl.ds(off,KB)],ds,1,0)
            return 0
        lax.fori_loop(lo,f0,lambda t,c: body(t,c,True),0)
        lax.fori_loop(f0,f1,lambda t,c: body(t,c,False),0)
        lax.fori_loop(f1,hi,lambda t,c: body(t,c,True),0)
        dq_ref[0,qi*QB:(qi+1)*QB,:]=(dqt_ref[...].T).astype(dq_ref.dtype)*jnp.bfloat16(0.125)
    dk_ref[0]=dkt_ref[...].T.astype(dk_ref.dtype)
    dv_ref[0]=dvt_ref[...].T.astype(dv_ref.dtype)

def attn_bwd(meta,start,q,k,v,do,o,lse,*,QB=256,KB=256,xorder=True,nheads=17,r0=0):
    _,L,W=q.shape; T=k.shape[1]; NP=W//128; R=1
    kern=functools.partial(bwd_kernel,QB=QB,KB=KB,L=L,xorder=xorder,nheads=nheads,r0=r0)
    full=lambda r,p,m:(r+r0,0,p)
    return pl.pallas_call(kern,
        grid_spec=pltpu.PrefetchScalarGridSpec(num_scalar_prefetch=1,grid=(R,NP),
            in_specs=[pl.BlockSpec((1,1,L),lambda r,p,m:(r+r0,0,0)),
                      pl.BlockSpec((1,L,128),full),
                      pl.BlockSpec((1,T,128),full),
                      pl.BlockSpec((1,T,128),full),
                      pl.BlockSpec((1,L,128),full),
                      pl.BlockSpec((1,L,128),full),
                      pl.BlockSpec((1,1,2,L),lambda r,p,m:(r+r0,p,0,0))],
            out_specs=[pl.BlockSpec((1,L,128),lambda r,p,m:(r,0,p)),
                       pl.BlockSpec((1,T,128),lambda r,p,m:(r,0,p)),
                       pl.BlockSpec((1,T,128),lambda r,p,m:(r,0,p))],
            scratch_shapes=[pltpu.VMEM((128,T),jnp.bfloat16),pltpu.VMEM((128,QB),jnp.float32),
                            pltpu.VMEM((128,T),jnp.float32),pltpu.VMEM((128,T),jnp.float32)]),
        out_shape=[jax.ShapeDtypeStruct((R,L,W),jnp.bfloat16),jax.ShapeDtypeStruct((R,T,W),jnp.bfloat16),jax.ShapeDtypeStruct((R,T,W),jnp.bfloat16)],
        compiler_params=pltpu.CompilerParams(dimension_semantics=("arbitrary","arbitrary"),vmem_limit_bytes=48<<20),
        cost_estimate=pl.CostEstimate(flops=R*10*L*T*W,bytes_accessed=R*(3*L+4*T)*W*2,transcendentals=R*L*T*18),
        name="attn_bwd")(meta,start,q,k,v,do,o,lse)


def dot_nn(a, b):
    return lax.dot_general(a, b, (((1,), (0,)), ((), ())), preferred_element_type=F32)


def dot_nt(a, b):
    return lax.dot_general(a, b, (((1,), (1,)), ((), ())), preferred_element_type=F32)


def turned(x):
    rank = x.shape[1]
    eye = (
        lax.broadcasted_iota(jnp.int32, (rank, rank), 0) == lax.broadcasted_iota(jnp.int32, (rank, rank), 1)
    ).astype(F32).astype(BF)
    return dot_nt(eye, x).astype(BF)


def whole_spec(shape, **kw):
    return pl.BlockSpec(shape, lambda *_: (0,) * len(shape), pipeline_mode=pl.Buffered(1))


def unpack_kernel(g_ref, mix_ref, out_ref, *, cm, co, D, W):
    S = g_ref.shape[0]
    rows = mix_ref.shape[2]
    half_width = cm + co
    for half in range(2):
        at = half * half_width
        mix = jnp.concatenate([g_ref[s, 0, :rows, at : at + cm] for s in range(S)], axis=1)
        out = jnp.concatenate([g_ref[s, 0, :rows, at + cm : at + half_width] for s in range(S)], axis=1)
        zero = jnp.zeros((mix.shape[0], W - D), mix.dtype)
        for i in range(3):
            mix_ref[0, half, :, i * W : (i + 1) * W] = jnp.concatenate([mix[:, i * D : (i + 1) * D], zero], axis=1)
        out_ref[0, half] = out


def unpack(g, S, C, rows2, cm, co, D, W):
    g = g.reshape(S, C, -1, 2 * (cm + co))
    mix, out = pl.pallas_call(
        functools.partial(unpack_kernel, cm=cm, co=co, D=D, W=W),
        grid=(C,),
        in_specs=[pl.BlockSpec((S, 1) + g.shape[2:], lambda c: (0, c, 0, 0))],
        out_specs=[
            pl.BlockSpec((1, 2, rows2, 3 * W), lambda c: (c, 0, 0, 0)),
            pl.BlockSpec((1, 2, rows2, D), lambda c: (c, 0, 0, 0)),
        ],
        out_shape=[
            jax.ShapeDtypeStruct((C, 2, rows2, 3 * W), BF),
            jax.ShapeDtypeStruct((C, 2, rows2, D), BF),
        ],
        compiler_params=pltpu.CompilerParams(vmem_limit_bytes=48 << 20),
        cost_estimate=pl.CostEstimate(flops=0, bytes_accessed=4 * g.size, transcendentals=0),
        name="unpack",
    )(g)
    return mix.reshape(D, 3 * W), out.reshape(D, D)


def qkv_kernel(meta_ref, *refs, W, count):
    n_refs = refs[:count]
    w_ref, e_ref, m_ref, b_ref, q_ref, k_ref, v_ref, l_ref, n_ref = refs[count:]
    j = pl.program_id(1)
    me = meta_ref[0]
    for jj in range(count):

        @pl.when(j == jj)
        def _(jj=jj):
            n_ref[...] = n_refs[jj][0, :, : n_ref.shape[1]]

    @pl.when((me ^ j) <= me)
    def _():
        n = n_ref[...]
        low = dot_nt(n, e_ref[0]).astype(BF)
        l_ref[0] = low

        def part(i):
            s = slice(i * W, (i + 1) * W)
            return dot_nn(n, w_ref[:, s]) + dot_nn(low, m_ref[0, :, s]) + b_ref[:, s]

        k_ref[0] = part(1).astype(BF)
        v_ref[0] = part(2).astype(BF)

        @pl.when(j == 0)
        def _():
            q_ref[0] = (part(0) * 0.125).astype(BF)

    @pl.when((me ^ j) > me)
    def _():
        l_ref[0] = jnp.zeros_like(l_ref[0])


def qkv(meta, n_parts, w, e_t, m, b):
    count = len(n_parts)
    R, L, W = n_parts[0].shape
    D = w.shape[0]
    T = count * L
    rank = m.shape[1]
    row = lambda r, j, _: (r, j, 0)
    one = lambda r, j, _: (r, 0, 0)
    return pl.pallas_call(
        functools.partial(qkv_kernel, W=W, count=count),
        grid_spec=pltpu.PrefetchScalarGridSpec(
            num_scalar_prefetch=1,
            grid=(R, count),
            in_specs=[pl.BlockSpec((1, L, W), one)] * count
            + [
                whole_spec(w.shape),
                pl.BlockSpec((1, rank, D), one),
                pl.BlockSpec((1, rank, 3 * W), one),
                whole_spec(b.shape),
            ],
            out_specs=[
                pl.BlockSpec((1, L, W), one),
                pl.BlockSpec((1, L, W), row),
                pl.BlockSpec((1, L, W), row),
                pl.BlockSpec((1, L, rank), row),
            ],
            scratch_shapes=[pltpu.VMEM((L, D), BF)],
        ),
        out_shape=[
            jax.ShapeDtypeStruct((R, L, W), BF),
            jax.ShapeDtypeStruct((R, T, W), BF),
            jax.ShapeDtypeStruct((R, T, W), BF),
            jax.ShapeDtypeStruct((R, T, rank), BF),
        ],
        compiler_params=pltpu.CompilerParams(vmem_limit_bytes=56 << 20),
        cost_estimate=pl.CostEstimate(
            flops=2 * R * T * D * 2 * W, bytes_accessed=2 * (R * T * D + w.size + 2 * R * T * W), transcendentals=0
        ),
        name="qkv",
    )(meta, *n_parts, w, e_t, m, b)


def ffn_kernel(
    n2_ref, dy_ref, res_ref, o_ref, lo_ref, l3_ref, wexp_ref, wshr_ref, rexp_ref, rshr_ref, eu_ref, eur_ref,
    hd_ref, hdr_ref, b_ref, br_ref, x0_ref, x1_ref, e1_ref, e2_ref, wout_ref, gain_ref, xb_ref,
    y_ref, dr_ref, do_ref, g1_ref, g2_ref, gx0_ref, gx1_ref, ge_ref, ger_ref, gh_ref, ghr_ref,
    out_acc, dn_acc, l4_acc, dl3_acc, dl4_ref, dl4t_ref, l3t_ref, shr_ref, *, R, per, co,
):
    f = pl.program_id(0)
    last = pl.num_programs(0) - 1
    D = dy_ref.shape[2]

    def block(r, wexp, wshr, eu, hd, b, ge, gh):
        n2, dy = n2_ref[r], dy_ref[r]
        h = dot_nn(n2, wexp) + dot_nn(l3_ref[r], eu) + b
        hh = h * h
        th = jnp.tanh(h * (0.7978845608028654 + (0.7978845608028654 * 0.044715) * hh))
        half = 0.5 * (1.0 + th)
        g = (h * half).astype(BF)
        slope = half + (0.5 * h) * (1.0 - th * th) * (0.7978845608028654 + (3 * 0.7978845608028654 * 0.044715) * hh)
        dg = dot_nn(dy, wshr) + dot_nn(dl4_ref[r], hd)
        dh = (dg * slope).astype(BF)
        out_acc[r] += dot_nt(g, wshr)
        dn_acc[r] += dot_nt(dh, wexp)
        l4_acc[r] += dot_nt(g, hd)
        dl3_acc[r] += dot_nt(dh, eu)
        gh[r] = dot_nn(dl4t_ref[r], g)
        ge[r] = dot_nn(l3t_ref[r], dh)

    if per:
        for part in range(per):

            @pl.when(lax.rem(f, per) == part)
            def _(part=part):
                for s in range(wshr_ref.shape[0]):
                    shr_ref[s * co : (s + 1) * co] = wshr_ref[s, 0, part * co : (part + 1) * co]

    else:
        shr_ref = wshr_ref.at[0]

    def rows(r, carry):
        @pl.when(f == 0)
        def _():
            dl4 = dot_nt(dy_ref[r], x1_ref[r]).astype(BF)
            dl4_ref[r] = dl4
            dl4t_ref[r] = turned(dl4)
            l3t_ref[r] = turned(l3_ref[r])
            out_acc[r] = jnp.zeros_like(out_acc[r])
            dn_acc[r] = jnp.zeros_like(dn_acc[r])
            l4_acc[r] = jnp.zeros_like(l4_acc[r])
            dl3_acc[r] = jnp.zeros_like(dl3_acc[r])

        block(r, wexp_ref[...].reshape(D, -1), shr_ref[...], eu_ref[r], hd_ref[r], b_ref[...], ge_ref, gh_ref)

        @pl.when(f == last)
        def _():
            block(r, rexp_ref[...], rshr_ref[...], eur_ref[r], hdr_ref[r], br_ref[...], ger_ref, ghr_ref)
            l4 = l4_acc[r].astype(BF)
            res = res_ref[r]
            y_ref[r] = (res + out_acc[r] + dot_nn(l4, x1_ref[r]) + xb_ref[...]).astype(BF).T
            gx1_ref[r] = dot_nn(turned(l4), dy_ref[r])
            dl3 = dl3_acc[r].astype(BF)
            g2_ref[r] = dot_nn(turned(dl3), n2_ref[r])
            e = (dn_acc[r] + dot_nn(dl3, e2_ref[r])) * gain_ref[...]
            z, inv = layer_stats(res)
            dr = dy_ref[r].astype(F32) + norm_back(e, z, inv)
            dr_ref[r] = dr
            drb = dr.astype(BF)
            dl2 = dot_nt(drb, x0_ref[r]).astype(BF)
            do_ref[r] = (dot_nt(drb, wout_ref[...]) + dot_nn(dl2, e1_ref[r])).astype(BF)
            g1_ref[r] = dot_nn(turned(dl2), o_ref[r])
            gx0_ref[r] = dot_nn(turned(lo_ref[r]), drb)

        return carry

    lax.fori_loop(0, R, rows, 0)


def ffn(n2, dy, res, o, lo, l3, wexp, wshr, rexp, rshr, eu, eur, hd, hdr, b, br, x0, x1, e1, e2, wout, gain, xb):
    R, L, D = n2.shape
    rank = x0.shape[1]
    width, rem = wexp.shape[-1], rexp.shape[1]
    blocks = eu.shape[2] // width
    cols = lambda *lead: pl.BlockSpec(lead + (width,), lambda f: (0,) * len(lead) + (f,))
    if wexp.ndim == 4:
        S, C = wexp.shape[:2]
        per, co = S // C, D // S
        wexp_spec = pl.BlockSpec((1, C, D // C, width), lambda f: (f, 0, 0, 0))
        wshr_spec = pl.BlockSpec((S, 1, D // C, width), lambda f: (0, f // per, 1, 0))
    else:
        per = co = 0
        wexp_spec = wshr_spec = pl.BlockSpec((1, D, width), lambda f: (f, 0, 0))
    shapes = [
        ((R, D, L), BF), ((R, L, D), F32), ((R, L, D), BF),
        ((R, rank, D), F32), ((R, rank, D), F32), ((R, rank, D), F32), ((R, rank, D), F32),
        ((R, rank, blocks * width), F32), ((R, rank, rem), F32), ((R, rank, blocks * width), F32), ((R, rank, rem), F32),
    ]
    out_specs = [whole_spec(s) for s, _ in shapes]
    out_specs[7] = out_specs[9] = cols(R, rank)
    ff = blocks * width + rem
    return pl.pallas_call(
        functools.partial(ffn_kernel, R=R, per=per, co=co),
        grid=(blocks,),
        in_specs=[whole_spec(a.shape) for a in (n2, dy, res, o, lo, l3)]
        + [wexp_spec, wshr_spec, whole_spec(rexp.shape), whole_spec(rshr.shape)]
        + [cols(R, rank), whole_spec(eur.shape), cols(R, rank), whole_spec(hdr.shape), cols(1), whole_spec(br.shape)]
        + [whole_spec(a.shape) for a in (x0, x1, e1, e2, wout, gain, xb)],
        out_specs=out_specs,
        out_shape=[jax.ShapeDtypeStruct(s, d) for s, d in shapes],
        scratch_shapes=[
            pltpu.VMEM((R, L, D), F32), pltpu.VMEM((R, L, D), F32), pltpu.VMEM((R, L, rank), F32),
            pltpu.VMEM((R, L, rank), F32), pltpu.VMEM((R, L, rank), BF), pltpu.VMEM((R, rank, L), BF),
            pltpu.VMEM((R, rank, L), BF), pltpu.VMEM((D, width), BF),
        ],
        compiler_params=pltpu.CompilerParams(vmem_limit_bytes=60 << 20),
        cost_estimate=pl.CostEstimate(
            flops=8 * R * L * D * ff, bytes_accessed=4 * D * ff + 24 * R * L * D, transcendentals=R * L * ff
        ),
        name="ffn",
    )(n2, dy, res, o, lo, l3, wexp, wshr, rexp, rshr, eu, eur, hd, hdr, b, br, x0, x1, e1, e2, wout, gain, xb)


def project_kernel(meta_ref, dq_ref, dk_ref, dv_ref, w_ref, m_ref, e_ref, low_ref, *refs, W, count):
    n_refs, refs = refs[:count], refs[count:]
    mine_ref, o_refs, g_ref, n_ref, t_ref = refs[0], refs[1:count], refs[count], refs[count + 1], refs[count + 2]
    j = pl.program_id(0)
    me = meta_ref[0]
    D = n_ref.shape[1]
    for jj in range(count):

        @pl.when(j == jj)
        def _(jj=jj):
            n_ref[...] = n_refs[jj][0, :, :D]

    @pl.when(j == 0)
    def _():
        g_ref[...] = jnp.zeros_like(g_ref)

    def work(pieces):
        low_t = turned(low_ref[0])
        dl = sum(dot_nt(d[0], m_ref[0, :, i * W : (i + 1) * W]) for i, d in pieces).astype(BF)
        total = dot_nn(dl, e_ref[0])
        for i, d in pieces:
            total = total + dot_nt(d[0], w_ref[:, i * W : (i + 1) * W])
            g_ref[i] += dot_nn(low_t, d[0])
        g_ref[3, :, :D] += dot_nn(turned(dl), n_ref[...])
        return total

    @pl.when(j == 0)
    def _():
        mine_ref[...] = work([(0, dq_ref), (1, dk_ref), (2, dv_ref)])

    @pl.when((j > 0) & ((me ^ j) < me))
    def _():
        t_ref[:, :D] = work([(1, dk_ref), (2, dv_ref)]).astype(BF)

    for jj in range(1, count):

        @pl.when(j == jj)
        def _(jj=jj):
            o_refs[jj - 1][...] = t_ref[...]


def project(meta, dq, dk, dv, w, m, e_t, low, n_parts, r):
    count = len(n_parts)
    _, L, W = dq.shape
    D = w.shape[0]
    T = count * L
    rank = m.shape[1]
    out = pl.pallas_call(
        functools.partial(project_kernel, W=W, count=count),
        grid_spec=pltpu.PrefetchScalarGridSpec(
            num_scalar_prefetch=1,
            grid=(count,),
            in_specs=[
                whole_spec(dq.shape),
                pl.BlockSpec((1, L, W), lambda j, _: (0, j, 0)),
                pl.BlockSpec((1, L, W), lambda j, _: (0, j, 0)),
                whole_spec(w.shape),
                pl.BlockSpec((1, rank, 3 * W), lambda j, _: (r, 0, 0)),
                pl.BlockSpec((1, rank, D), lambda j, _: (r, 0, 0)),
                pl.BlockSpec((1, L, rank), lambda j, _: (r, j, 0)),
            ]
            + [pl.BlockSpec((1, L, W), lambda j, _: (r, 0, 0))] * count,
            out_specs=[whole_spec((L, D))] + [whole_spec((L, W))] * (count - 1) + [whole_spec((4, rank, W))],
            scratch_shapes=[pltpu.VMEM((L, D), BF), pltpu.VMEM((L, W), BF)],
        ),
        out_shape=[jax.ShapeDtypeStruct((L, D), F32)]
        + [jax.ShapeDtypeStruct((L, W), BF)] * (count - 1)
        + [jax.ShapeDtypeStruct((4, rank, W), F32)],
        compiler_params=pltpu.CompilerParams(vmem_limit_bytes=56 << 20),
        cost_estimate=pl.CostEstimate(
            flops=2 * T * D * 2 * W, bytes_accessed=2 * (w.size + 2 * T * W + 2 * T * D), transcendentals=0
        ),
        name="project",
    )(meta, dq, dk, dv, w, m, e_t, low, *n_parts)
    return out[:count], out[count]


def norm_kernel(x_ref, dy_ref, gain_ref, shift_ref, n_ref, xr_ref, dyr_ref):
    x = x_ref[0].astype(F32)
    centred = x - jnp.mean(x, axis=0, keepdims=True)
    inv = lax.rsqrt(jnp.mean(centred * centred, axis=0, keepdims=True) + EPS)
    n = (centred * inv * gain_ref[...] + shift_ref[...]).astype(BF).T
    n_ref[0] = jnp.concatenate([n, jnp.zeros((n.shape[0], n_ref.shape[2] - n.shape[1]), BF)], axis=1)
    xr_ref[0] = x_ref[0].T
    dyr_ref[0] = dy_ref[0].T


def first_norm(x_t, dy_t, gain, shift, W):
    R, D, L = x_t.shape
    col = pl.BlockSpec((1, D, L), lambda r: (r, 0, 0))
    row = pl.BlockSpec((1, L, D), lambda r: (r, 0, 0))
    return pl.pallas_call(
        norm_kernel,
        grid=(R,),
        in_specs=[col, col, whole_spec((D, 1)), whole_spec((D, 1))],
        out_specs=[pl.BlockSpec((1, L, W), lambda r: (r, 0, 0)), row, row],
        out_shape=[jax.ShapeDtypeStruct((R, L, W), BF)] + [jax.ShapeDtypeStruct((R, L, D), BF)] * 2,
        compiler_params=pltpu.CompilerParams(vmem_limit_bytes=48 << 20),
        cost_estimate=pl.CostEstimate(flops=10 * x_t.size, bytes_accessed=10 * x_t.size, transcendentals=0),
        name="first_norm",
    )(x_t, dy_t, gain[:, None], shift[:, None])


def last_kernel(*refs, count, alias):
    if alias:
        refs = refs[1:]
    terms, (dr_ref, x_ref, gain_ref, o_ref) = refs[:count], refs[count:]
    D = x_ref.shape[2]
    dn = terms[0][...]
    for t in terms[1:]:
        dn = dn + t[:, :D].astype(F32)
    z, inv = layer_stats(x_ref[0].astype(F32))
    o_ref[0] = (dr_ref[0] + norm_back(dn * gain_ref[...], z, inv)).astype(BF).T


def last(r, before, terms, dr, x, gain):
    R, L, D = x.shape
    alias = before is not None
    return pl.pallas_call(
        functools.partial(last_kernel, count=len(terms), alias=alias),
        grid=(1,),
        in_specs=[pl.BlockSpec(memory_space=pl.ANY)] * alias
        + [whole_spec(t.shape) for t in terms]
        + [pl.BlockSpec((1, L, D), lambda i: (r, 0, 0))] * 2
        + [whole_spec((1, D))],
        out_specs=pl.BlockSpec((1, D, L), lambda i: (r, 0, 0)),
        out_shape=jax.ShapeDtypeStruct((R, D, L), BF),
        input_output_aliases={0: 0} if alias else {},
        compiler_params=pltpu.CompilerParams(vmem_limit_bytes=48 << 20),
        cost_estimate=pl.CostEstimate(flops=20 * L * D, bytes_accessed=12 * L * D, transcendentals=0),
        name="last",
    )(*([before] if alias else []), *terms, dr, x, gain)


def late_kernel(slot_ref, part_ref, *refs, R, parts, D, W):
    g_refs, mix_ref, entry_ref, total = refs[:R], refs[R], refs[R + 1], refs[R + 2]
    total[...] = jnp.zeros_like(total)
    count = g_refs[0].shape[0]
    for r in range(R):

        def one(i, carry):
            a = slot_ref[r * count + i]
            c = part_ref[i]
            total[a, c] = total[a, c] + g_refs[r][i].astype(F32)
            return carry

        lax.fori_loop(0, count, one, 0)
    per = parts // 4
    wide = [jnp.concatenate([total[:, i * per + p] for p in range(per)], axis=-1) for i in range(4)]
    mix_ref[...] = jnp.concatenate([w[:, :, :D] for w in wide[:3]], axis=-1)
    entry_ref[...] = wide[3][:, :, :D]


def late_slots(slot, part, gs, adapters, parts, D, W):
    R = len(gs)
    _, rank, width = gs[0].shape
    return pl.pallas_call(
        functools.partial(late_kernel, R=R, parts=parts, D=D, W=W),
        grid_spec=pltpu.PrefetchScalarGridSpec(
            num_scalar_prefetch=2,
            grid=(1,),
            in_specs=[whole_spec(g.shape) for g in gs],
            out_specs=[whole_spec((adapters, rank, 3 * D)), whole_spec((adapters, rank, D))],
            scratch_shapes=[pltpu.VMEM((adapters, parts, rank, width), F32)],
        ),
        out_shape=[
            jax.ShapeDtypeStruct((adapters, rank, 3 * D), F32),
            jax.ShapeDtypeStruct((adapters, rank, D), F32),
        ],
        compiler_params=pltpu.CompilerParams(vmem_limit_bytes=48 << 20),
        cost_estimate=pl.CostEstimate(flops=0, bytes_accessed=8 << 20, transcendentals=0),
        name="late_slots",
    )(slot, part, *gs)


def mm(pattern, a, b):
    return jnp.einsum(pattern, a, b, preferred_element_type=F32)


def layer_stats(v):
    middle = jnp.mean(v, axis=-1, keepdims=True)
    centred = v - middle
    inv = lax.rsqrt(jnp.mean(centred * centred, axis=-1, keepdims=True) + EPS)
    return centred * inv, inv


def norm_back(e, z, inv):
    return (e - jnp.mean(e, -1, keepdims=True) - z * jnp.mean(e * z, -1, keepdims=True)) * inv


def swap(x, axis, bit, needed):
    n = lax.axis_size(axis)
    return lax.ppermute(x, axis, [(d ^ bit, d) for d in range(n) if needed(d)])


def blocks_of(x, bits):
    found = {0: x}
    for bit in reversed(bits):
        for j in sorted(found):
            found[j | bit] = swap(found[j], "ctx", bit, lambda d, k=j | bit: (d ^ k) < d)
    return [found[j] for j in sorted(found)]


def blocks_back(parts, bits):
    held = {j: [p] for j, p in enumerate(parts)}
    for bit in bits:
        for j in sorted(held):
            if j & bit:
                sent = held.pop(j)
                sent = sent[0] if len(sent) == 1 else sum(t.astype(F32) for t in sent).astype(BF)
                got = swap(sent, "ctx", bit, lambda d, k=j, b=bit: ((d ^ b) ^ k) < (d ^ b))
                held[j ^ bit].append(got)
    return held[0]


def ctx_sum_rows(g, bits):
    n = lax.axis_size("ctx")
    me = lax.axis_index("ctx")
    for bit in reversed(bits):
        half = g.shape[0] // 2
        mine = (me & bit) != 0
        low, high = g[:half], g[half:]
        got = lax.ppermute(jnp.where(mine, low, high), "ctx", [(d, d ^ bit) for d in range(n)])
        g = jnp.where(mine, high, low) + got
    return g


def gather_all(x, seq_count, ctx_count):
    n = seq_count * ctx_count
    seq_bits = [ctx_count << i for i in range(seq_count.bit_length() - 1)]
    ctx_bits = [1 << i for i in range(ctx_count.bit_length() - 1)]
    held, order = x[None], [0]
    for bit in seq_bits + ctx_bits[::-1]:
        got = lax.ppermute(held, BOTH, [(d, d ^ bit) for d in range(n)])
        held = jnp.concatenate([held, got], 0)
        order = order + [o ^ bit for o in order]
    return held, order


def slots_kernel(index_ref, g_ref, *refs, count, spans):
    outs, total = refs[:-1], refs[-1]
    total[...] = jnp.zeros_like(total)

    def one(i, carry):
        a = index_ref[i]
        total[a] = total[a] + g_ref[i].astype(F32)
        return carry

    lax.fori_loop(0, count, one, 0)
    for out, pieces in zip(outs, spans):
        parts = [total[:, :, first : first + width] for first, width in pieces]
        out[...] = parts[0] if len(parts) == 1 else jnp.concatenate(parts, axis=-1)


def to_slots(index, g, adapters, spans):
    count, rank, wide = g.shape
    rows = 8
    widths = [sum(w for _, w in pieces) for pieces in spans]
    return pl.pallas_call(
        functools.partial(slots_kernel, count=count, spans=spans),
        grid_spec=pltpu.PrefetchScalarGridSpec(
            num_scalar_prefetch=1,
            grid=(rank // rows,),
            in_specs=[pl.BlockSpec((count, rows, wide), lambda i, m: (0, i, 0))],
            out_specs=[pl.BlockSpec((adapters, rows, w), lambda i, m: (0, i, 0)) for w in widths],
            scratch_shapes=[pltpu.VMEM((adapters, rows, wide), F32)],
        ),
        out_shape=[jax.ShapeDtypeStruct((adapters, rank, w), F32) for w in widths],
        compiler_params=pltpu.CompilerParams(vmem_limit_bytes=48 << 20),
        cost_estimate=pl.CostEstimate(
            flops=count * rank * wide, bytes_accessed=count * rank * wide * 2 + adapters * rank * wide * 4, transcendentals=0
        ),
        name="to_slots",
    )(index, g)


def per_device(
    tokens, segments, adapter_index, norm_gains, norm_shifts, head_biases, expand_bias, exit_biases,
    mixing_weight, output_weight, expand_weight, shrink_weight,
    entry_adapters, mixing_adapters, expand_adapters, hidden_adapters, exit_adapters, cotangent,
):
    micro, seqs, L, D = tokens.shape
    R = micro * seqs
    adapters, rank = mixing_adapters.shape[:2]
    FF = expand_bias.shape[0]
    C = lax.axis_size("ctx")
    S = lax.axis_size("seq")
    bits = [1 << i for i in range(C.bit_length() - 1)]
    me = lax.axis_index("ctx")
    T = C * L
    W = -(-D // 128) * 128
    pad = W - D

    rows = mixing_weight.shape[0]
    cm, co, ce = mixing_weight.shape[1], output_weight.shape[1], expand_weight.shape[1]
    first = jnp.concatenate([mixing_weight, output_weight], 1)
    first = jnp.concatenate([first[: rows // 2], first[rows // 2 :]], 1)
    main = ce // 128 * 128
    rem = ce - main
    per = S // C
    shr_t = shrink_weight.T.reshape(co, per, ce).transpose(1, 0, 2)
    rest = jnp.concatenate([expand_weight[:, main:].reshape(-1), shr_t[:, :, main:].reshape(-1)])
    rest_rows = -(-rest.shape[0] // first.shape[1])
    rest = jnp.pad(rest, (0, rest_rows * first.shape[1] - rest.shape[0])).reshape(rest_rows, -1)
    first = jnp.concatenate([first, rest], 0)
    second = jnp.concatenate([expand_weight[:, :main], shr_t[:, :, :main].reshape(per * co, main)], 0)
    g1 = lax.all_gather(first, BOTH)
    g2 = lax.all_gather(second, BOTH).reshape(S, C, -1, main)
    w_mix, w_out = unpack(g1, S, C, rows // 2, cm, co, D, W)
    if rows % 16 == 0 and per * co == rows and co % 8 == 0:
        w_exp = w_shr = g2
    else:
        w_exp = g2[:, :, :rows].reshape(S, D, main)
        w_shr = g2[:, :, rows:].reshape(S, C, per, co, main).transpose(1, 2, 0, 3, 4).reshape(S, D, main)
    flat = g1[:, rows // 2 :].reshape(S, C, -1)
    r_exp = flat[..., : rows * rem].reshape(S, C, rows, rem).transpose(1, 2, 0, 3).reshape(D, S * rem)
    r_shr = flat[..., rows * rem : rows * rem + per * co * rem].reshape(S, C, per, co, rem)
    r_shr = r_shr.transpose(0, 3, 1, 2, 4).reshape(D, S * rem)

    def split_ff(m):
        m = m.reshape(m.shape[:-1] + (S, ce))
        return m[..., :main].reshape(m.shape[:-2] + (S * main,)), m[..., main:].reshape(m.shape[:-2] + (S * rem,))

    index = adapter_index.reshape(R)
    take = lambda table, axis: jnp.stack(
        [lax.dynamic_index_in_dim(table, index[r], axis, keepdims=False) for r in range(R)], axis
    )
    entry = take(entry_adapters, 1)
    mix_up = take(mixing_adapters, 0)
    exp_up = take(expand_adapters, 0)
    hid = take(hidden_adapters, 0)
    exit_up = take(exit_adapters, 1)
    pad_heads = lambda m: jnp.concatenate([padded(m[..., i * D : (i + 1) * D]) for i in range(3)], -1)
    padded = lambda m: jnp.pad(m, [(0, 0)] * (m.ndim - 1) + [(0, pad)])
    mix_up = pad_heads(mix_up)
    flip = lambda m: jnp.swapaxes(m, -1, -2)
    entry_t = flip(entry)
    exp_main, exp_rest = split_ff(exp_up)
    hid_main, hid_rest = split_ff(flip(hid))
    bias_main, bias_rest = split_ff(expand_bias[None])
    head_bias = pad_heads(jnp.concatenate([head_biases[0], jnp.zeros_like(head_biases[0]), head_biases[1]])[None])

    seg = segments.reshape(R, L)
    seg_blocks = blocks_of(seg, bits)
    start = jnp.zeros((R, L), jnp.int32)
    for j, other in enumerate(seg_blocks):
        ok = (me ^ j) <= me
        start = start + jnp.sum(((other[:, None, :] < seg[:, :, None]) & ok).astype(jnp.int32), -1)
    QB = KB = min(512, L)
    meta = jnp.concatenate(
        [me[None].astype(jnp.int32)]
        + [start[r, (qi + e) * QB - e][None] for r in range(R) for qi in range(L // QB) for e in (0, 1)]
    )
    start = start[:, None, :]

    n1, x, dy = first_norm(
        flip(tokens.reshape(R, L, D)), flip(cotangent.reshape(R, L, D)), norm_gains[0], norm_shifts[0], W
    )
    n1_parts = blocks_of(n1, bits)
    q, k, v, l1_all = qkv(meta, n1_parts, w_mix, entry_t[0], mix_up, head_bias)

    o, lse = attn_fwd(meta, start, q, k, v, QB=QB, KB=KB)

    lo = mm("rtd,rdk->rtk", o, entry[1]).astype(BF)
    res = x.astype(F32) + mm("rtd,de->rte", o, w_out) + mm("rtk,rke->rte", lo, exit_up[0]) + exit_biases[0]
    z2, inv2 = layer_stats(res)
    n2 = (z2 * norm_gains[1] + norm_shifts[1]).astype(BF)
    l3 = mm("rtd,rdk->rtk", n2, entry[2]).astype(BF)
    y, dr, do, g1, g2_, gx0, gx1, ge, ger, gh, ghr = ffn(
        n2, dy, res, o, lo, l3, w_exp, w_shr, r_exp, r_shr, exp_main, exp_rest, hid_main, hid_rest, bias_main, bias_rest,
        exit_up[0], exit_up[1], entry_t[1], entry_t[2], w_out, norm_gains[1][None], exit_biases[1][None],
    )
    layer_output = flip(y).reshape(tokens.shape)

    number = jnp.broadcast_to((index.astype(F32) / C)[:, None, None], (R, rank, 128))
    early = jnp.concatenate([g1, g2_, gx0, gx1, ge, ger, gh, ghr, number], -1).reshape(R * rank, -1)
    early = ctx_sum_rows(early, bits).astype(BF)
    early = lax.all_gather(early, BOTH).reshape(S * R, rank, -1)
    all_index = early[:, 0, -1].astype(jnp.int32)
    spans = [[(i * D, D)] for i in range(4)]
    for at in (4 * D, 4 * D + FF):
        spans.append(
            [p for i in range(S) for p in ((at + i * main, main), (at + S * main + i * rem, rem))]
        )
    entry1_g, entry2_g, exit0_g, exit1_g, expand_g, hidden_g = to_slots(all_index, early, adapters, spans)

    input_grad, late, terms = None, [], []
    for r in range(R):
        dq, dk, dv = attn_bwd(meta, start, q, k, v, do, o, lse, QB=QB, KB=KB, r0=r)
        if r:
            dk, terms[r - 1] = lax.optimization_barrier((dk, terms[r - 1]))
        parts, g = project(meta, dq, dk, dv, w_mix, mix_up, entry_t[0], l1_all, n1_parts, r)
        if r + 1 < R:
            do, parts = lax.optimization_barrier((do, parts))
        terms.append(blocks_back(parts, bits))
        g = g.reshape(4, rank, C // 4, -1).transpose(0, 2, 1, 3).reshape(C, rank, -1)
        late.append(gather_all(ctx_sum_rows(g, bits)[0].astype(BF), S, C))
    for r in range(R):
        input_grad = last(r, input_grad, terms[r], dr, x, norm_gains[0][None])
    device = lax.axis_index("seq") * C + me
    order = device ^ jnp.array(late[0][1], jnp.int32)
    by_row = all_index.reshape(S, R)
    slot = jnp.concatenate([jnp.sum(jnp.where((order // C)[:, None] == jnp.arange(S), by_row[:, r], 0), 1) for r in range(R)])
    mixing_g, entry0_g = late_slots(slot, order % C, [g for g, _ in late], adapters, C, D, W)
    input_grad = flip(input_grad).reshape(tokens.shape)

    return (
        layer_output,
        input_grad,
        jnp.stack([flip(entry0_g), flip(entry1_g), flip(entry2_g)]),
        mixing_g,
        expand_g,
        flip(hidden_g),
        jnp.stack([exit0_g, exit1_g]),
    )


def solution(mesh):
    rows = P(None, "seq", "ctx", None)
    weight = P("ctx", "seq")
    in_specs = (
        (rows, P(None, "seq", "ctx"), P(None, "seq")) + (P(),) * 5 + (weight,) * 4 + (P(),) * 5 + (rows,)
    )
    out_specs = (rows, rows) + (P(),) * 5
    return jax.shard_map(per_device, mesh=mesh, in_specs=in_specs, out_specs=out_specs, check_vma=False)
```

```python
import functools

import jax
import jax.numpy as jnp
from jax import lax
from jax.experimental import pallas as pl
from jax.experimental.pallas import tpu as pltpu
from jax.sharding import PartitionSpec as P

HEADS = 17
EPS = 1e-05
NEG = -1e30
BF = jnp.bfloat16
F32 = jnp.float32
BOTH = ("seq", "ctx")


FAR = -1e30


def product(a, b, ca, cb):
    return lax.dot_general(a, b, (((ca,), (cb,)), ((), ())), preferred_element_type=F32)


def thirds(x):
    a = x.astype(BF)
    b = (x - a.astype(F32)).astype(BF)
    c = (x - a.astype(F32) - b.astype(F32)).astype(BF)
    return a, b, c


def lanes_of(h, lane):
    return (lane < 64) if h == 0 else (lane >= 64)


def attn_fwd_kernel(
    meta_ref, q_ref, k_ref, v_ref, qa_ref, ka_ref, o_ref, a_ref, kh_ref, vt_ref, s_ref, acc_ref, st_ref, *, L
):
    r = pl.program_id(0)
    me = meta_ref[0]
    lo = meta_ref[1 + r]
    lane = lax.broadcasted_iota(jnp.int32, (1, 128), 1)
    vt_ref[...] = v_ref[0].T
    q2, qa = q_ref[0], qa_ref[0]
    qh = [jnp.where(lanes_of(h, lane), q2, qa) for h in range(2)]
    for h in range(2):
        kh_ref[h] = jnp.where(lanes_of(h, lane), k_ref[0], ka_ref[0])
        st_ref[h] = jnp.concatenate([jnp.full((1, L), NEG, F32), jnp.zeros((7, L), F32)], axis=0)
    acc_ref[...] = jnp.zeros_like(acc_ref)

    def at(t):
        return pl.multiple_of((t ^ me) * L, L)

    def scores(t, h):
        s_ref[h] = product(kh_ref[h, pl.ds(at(t), L), :], qh[h], 1, 1)

    def gather(t, h, diagonal):
        s = s_ref[h]
        if diagonal:
            ok = lax.broadcasted_iota(jnp.int32, (L, L), 0) <= lax.broadcasted_iota(jnp.int32, (L, L), 1)
            s = jnp.where(ok, s, NEG)
        m = st_ref[h, 0:1]
        new = jnp.maximum(m, jnp.max(s, axis=0, keepdims=True))
        scale = jnp.exp(m - new)
        p = jnp.exp(s - new)
        st_ref[h, 1:2] = st_ref[h, 1:2] * scale + jnp.sum(p, axis=0, keepdims=True)
        st_ref[h, 0:1] = new
        rows = slice(h * 64, (h + 1) * 64)
        acc_ref[rows] = acc_ref[rows] * scale + product(vt_ref[rows, pl.ds(at(t), L)], p.astype(BF), 1, 0)

    scores(lo, 0)

    def body(t, carry):
        scores(t, 1)
        gather(t, 0, False)
        scores(t + 1, 0)
        gather(t, 1, False)
        return carry

    lax.fori_loop(lo, me, body, 0)
    scores(me, 1)
    gather(me, 0, True)
    gather(me, 1, True)
    rows = []
    for h in range(2):
        total = st_ref[h, 1:2]
        sl = slice(h * 64, (h + 1) * 64)
        acc_ref[sl] = acc_ref[sl] / total
        rows.append(thirds(-(st_ref[h, 0:1] + jnp.log(total))))
    o_ref[0] = acc_ref[...].T.astype(o_ref.dtype)
    sub = lax.broadcasted_iota(jnp.int32, (128, 1), 0)
    extra = jnp.zeros((128, L), F32)
    for h in range(2):
        for i in range(3):
            extra = jnp.where(sub == (1 - h) * 64 + 8 + i, rows[h][i].astype(F32), extra)
    a_ref[0, 0] = (qa.astype(F32) + extra.T).astype(BF)


def attn_fwd(meta, q, k, v, qa, ka, D):
    R, L, W = q.shape
    T = k.shape[1]
    NP = W // 128
    col = lambda r, p, m: (r, 0, p)
    one = lambda r, p, m: (r, 0, 0)
    return pl.pallas_call(
        functools.partial(attn_fwd_kernel, L=L),
        grid_spec=pltpu.PrefetchScalarGridSpec(
            num_scalar_prefetch=1,
            grid=(R, NP),
            in_specs=[
                pl.BlockSpec((1, L, 128), col),
                pl.BlockSpec((1, T, 128), col),
                pl.BlockSpec((1, T, 128), col),
                pl.BlockSpec((1, L, 128), one),
                pl.BlockSpec((1, T, 128), one),
            ],
            out_specs=[pl.BlockSpec((1, L, 128), col), pl.BlockSpec((1, 1, L, 128), lambda r, p, m: (r, p, 0, 0))],
            scratch_shapes=[
                pltpu.VMEM((2, T, 128), BF),
                pltpu.VMEM((128, T), BF),
                pltpu.VMEM((2, L, L), F32),
                pltpu.VMEM((128, L), F32),
                pltpu.VMEM((2, 8, L), F32),
            ],
        ),
        out_shape=[jax.ShapeDtypeStruct((R, L, D), BF), jax.ShapeDtypeStruct((R, NP, L, 128), BF)],
        compiler_params=pltpu.CompilerParams(vmem_limit_bytes=48 << 20),
        cost_estimate=pl.CostEstimate(
            flops=R * 40 * L * T * W, bytes_accessed=R * (2 * L + 2 * T) * W * 2, transcendentals=R * L * T * 18
        ),
        name="attn_fwd",
    )(meta, q, k, v, qa, ka)


def attn_bwd_kernel(
    meta_ref, q_ref, k_ref, v_ref, do_ref, o_ref, a_ref, ka_ref, dq_ref, dk_ref, dv_ref,
    kh_ref, vh_ref, kt_ref, s_ref, dp_ref, dqt_ref, dkt_ref, dvt_ref, *, L, r0, D,
):
    me = meta_ref[0]
    lo = meta_ref[1 + r0]
    lane = lax.broadcasted_iota(jnp.int32, (1, 128), 1)
    limit = D - pl.program_id(0) * 128
    kt_ref[...] = k_ref[0].T
    ones = jnp.where((lane % 64 >= 8) & (lane % 64 < 11), 1.0, 0.0).astype(BF)
    do2 = jnp.where(lane < limit, do_ref[0], jnp.zeros((), BF))
    o2 = jnp.where(lane < limit, o_ref[0], jnp.zeros((), BF))
    q2 = q_ref[0]
    prod = do2.astype(F32) * o2.astype(F32)
    qh, dh = [], []
    for h in range(2):
        mine = lanes_of(h, lane)
        parts = thirds(-jnp.sum(jnp.where(mine, prod, 0.0), axis=1, keepdims=True))
        extra = jnp.zeros((1, 128), BF)
        for i in range(3):
            extra = jnp.where(lane == (1 - h) * 64 + 8 + i, parts[i], extra)
        dh.append(jnp.where(mine, do2, extra))
        qh.append(jnp.where(mine, q2, a_ref[0, 0]))
        kh_ref[h] = jnp.where(mine, k_ref[0], ka_ref[0])
        vh_ref[h] = jnp.where(mine, v_ref[0], ones)
    qt, dot_ = q2.T, do2.T
    dqt_ref[...] = jnp.zeros_like(dqt_ref)

    def at(t):
        return pl.multiple_of((t ^ me) * L, L)

    def scores(t, h):
        s_ref[h] = product(kh_ref[h, pl.ds(at(t), L), :], qh[h], 1, 1)
        dp_ref[h] = product(vh_ref[h, pl.ds(at(t), L), :], dh[h], 1, 1)

    def gather(t, h, diagonal):
        p = jnp.exp(s_ref[h])
        if diagonal:
            ok = lax.broadcasted_iota(jnp.int32, (L, L), 0) <= lax.broadcasted_iota(jnp.int32, (L, L), 1)
            p = jnp.where(ok, p, 0.0)
        ds = (p * dp_ref[h]).astype(BF)
        rows = slice(h * 64, (h + 1) * 64)
        here = pl.ds(at(t), L)
        dvt_ref[rows, :] = product(dot_[rows], p.astype(BF), 1, 1)
        dkt_ref[rows, :] = product(qt[rows], ds, 1, 1)
        dqt_ref[rows] += product(kt_ref[rows, here], ds, 1, 0)

    def store(t):
        here = pl.ds(at(t), L)
        dk_ref[0, here, :] = dkt_ref[...].astype(BF).T
        dv_ref[0, here, :] = dvt_ref[...].astype(BF).T

    def none(t, carry):
        dk_ref[0, pl.ds(at(t), L), :] = jnp.zeros((L, 128), BF)
        dv_ref[0, pl.ds(at(t), L), :] = jnp.zeros((L, 128), BF)
        return carry

    lax.fori_loop(0, lo, none, 0)
    scores(lo, 0)

    def body(t, carry):
        scores(t, 1)
        gather(t, 0, False)
        scores(t + 1, 0)
        gather(t, 1, False)
        store(t)
        return carry

    lax.fori_loop(lo, me, body, 0)
    scores(me, 1)
    gather(me, 0, True)
    gather(me, 1, True)
    store(me)
    dq_ref[0] = dqt_ref[...].astype(BF).T * jnp.asarray(0.125, BF)


def attn_bwd(meta, q, k, v, do, o, extra, ka, r0):
    R, L, W = q.shape
    T, D = k.shape[1], do.shape[2]
    NP = W // 128
    col = lambda p, m: (r0, 0, p)
    out = lambda p, m: (0, 0, p)
    return pl.pallas_call(
        functools.partial(attn_bwd_kernel, L=L, r0=r0, D=D),
        grid_spec=pltpu.PrefetchScalarGridSpec(
            num_scalar_prefetch=1,
            grid=(NP,),
            in_specs=[
                pl.BlockSpec((1, L, 128), col),
                pl.BlockSpec((1, T, 128), col),
                pl.BlockSpec((1, T, 128), col),
                pl.BlockSpec((1, L, 128), col),
                pl.BlockSpec((1, L, 128), col),
                pl.BlockSpec((1, 1, L, 128), lambda p, m: (r0, p, 0, 0)),
                pl.BlockSpec((1, T, 128), lambda p, m: (r0, 0, 0)),
            ],
            out_specs=[pl.BlockSpec((1, L, 128), out), pl.BlockSpec((1, T, 128), out), pl.BlockSpec((1, T, 128), out)],
            scratch_shapes=[
                pltpu.VMEM((2, T, 128), BF),
                pltpu.VMEM((2, T, 128), BF),
                pltpu.VMEM((128, T), BF),
                pltpu.VMEM((2, L, L), F32),
                pltpu.VMEM((2, L, L), F32),
                pltpu.VMEM((128, L), F32),
                pltpu.VMEM((128, L), F32),
                pltpu.VMEM((128, L), F32),
            ],
        ),
        out_shape=[
            jax.ShapeDtypeStruct((1, L, W), BF),
            jax.ShapeDtypeStruct((1, T, W), BF),
            jax.ShapeDtypeStruct((1, T, W), BF),
        ],
        compiler_params=pltpu.CompilerParams(vmem_limit_bytes=48 << 20),
        cost_estimate=pl.CostEstimate(
            flops=60 * L * T * W, bytes_accessed=(3 * L + 4 * T) * W * 2, transcendentals=L * T * 18
        ),
        name="attn_bwd",
    )(meta, q, k, v, do, o, extra, ka)


def document_lanes(seg_q, seg_k):
    number = jnp.arange(64, dtype=jnp.int32)
    two = lambda m: jnp.concatenate([m, m], -1).astype(BF)
    qa = jnp.where((number < 8) & (number != seg_q[..., None]), FAR, 0.0)
    ka = jnp.where((number == seg_k[..., None]) | ((number >= 8) & (number < 11)), 1.0, 0.0)
    return two(qa), two(ka)


def dot_nn(a, b):
    return lax.dot_general(a, b, (((1,), (0,)), ((), ())), preferred_element_type=F32)


def dot_nt(a, b):
    return lax.dot_general(a, b, (((1,), (1,)), ((), ())), preferred_element_type=F32)


def turned(x):
    rank = x.shape[1]
    eye = (
        lax.broadcasted_iota(jnp.int32, (rank, rank), 0) == lax.broadcasted_iota(jnp.int32, (rank, rank), 1)
    ).astype(F32).astype(BF)
    return dot_nt(eye, x).astype(BF)


def place(x, first, width):
    rank = x.shape[1]
    to = lax.broadcasted_iota(jnp.int32, (rank, width), 1) == lax.broadcasted_iota(jnp.int32, (rank, width), 0) + first
    return dot_nn(x, to.astype(F32).astype(BF)).astype(BF)


def taken(x, first, rank):
    width = x.shape[1]
    to = lax.broadcasted_iota(jnp.int32, (rank, width), 1) == lax.broadcasted_iota(jnp.int32, (rank, width), 0) + first
    return dot_nt(to.astype(F32).astype(BF), x).astype(BF)


def whole_spec(shape, **kw):
    return pl.BlockSpec(shape, lambda *_: (0,) * len(shape), pipeline_mode=pl.Buffered(1))


def unpack_kernel(g_ref, mix_ref, out_ref, *, cm, co, D, W):
    S = g_ref.shape[0]
    rows = mix_ref.shape[2]
    half_width = cm + co
    for half in range(2):
        at = half * half_width
        mix = jnp.concatenate([g_ref[s, 0, :rows, at : at + cm] for s in range(S)], axis=1)
        out = jnp.concatenate([g_ref[s, 0, :rows, at + cm : at + half_width] for s in range(S)], axis=1)
        zero = jnp.zeros((mix.shape[0], W - D), mix.dtype)
        for i in range(3):
            mix_ref[0, half, :, i * W : (i + 1) * W] = jnp.concatenate([mix[:, i * D : (i + 1) * D], zero], axis=1)
        out_ref[0, half] = out


def unpack(g, S, C, rows2, cm, co, D, W):
    g = g.reshape(S, C, -1, 2 * (cm + co))
    mix, out = pl.pallas_call(
        functools.partial(unpack_kernel, cm=cm, co=co, D=D, W=W),
        grid=(C,),
        in_specs=[pl.BlockSpec((S, 1) + g.shape[2:], lambda c: (0, c, 0, 0))],
        out_specs=[
            pl.BlockSpec((1, 2, rows2, 3 * W), lambda c: (c, 0, 0, 0)),
            pl.BlockSpec((1, 2, rows2, D), lambda c: (c, 0, 0, 0)),
        ],
        out_shape=[
            jax.ShapeDtypeStruct((C, 2, rows2, 3 * W), BF),
            jax.ShapeDtypeStruct((C, 2, rows2, D), BF),
        ],
        compiler_params=pltpu.CompilerParams(vmem_limit_bytes=48 << 20),
        cost_estimate=pl.CostEstimate(flops=0, bytes_accessed=4 * g.size, transcendentals=0),
        name="unpack",
    )(g)
    return mix.reshape(D, 3 * W), out.reshape(D, D)


def qkv_kernel(meta_ref, *refs, count, W, R):
    n_refs = refs[:count]
    w_ref, m_ref, b_ref, q_ref, k_ref, v_ref, n_ref, wa_ref = refs[count:]
    j = pl.program_id(0)
    me = meta_ref[0]
    D = w_ref.shape[0]
    rank = m_ref.shape[1]
    for jj in range(count):

        @pl.when(j == jj)
        def _(jj=jj):
            n_ref[...] = n_refs[jj][...].reshape(n_ref.shape)

    @pl.when(j == 0)
    def _():
        wa_ref[:D] = w_ref[...]
        for r in range(R):
            wa_ref[D + r * rank : D + (r + 1) * rank] = m_ref[r]
        wa_ref[D + R * rank :] = jnp.zeros((W - D - R * rank, 3 * W), BF)

    def part(i):
        s = slice(i * W, (i + 1) * W)
        return (dot_nn(n_ref[...], wa_ref[:, s]) + b_ref[:, s]).reshape(R, -1, W)

    @pl.when(j == 0)
    def _():
        q_ref[...] = (part(0) * 0.125).astype(BF)

    @pl.when((me ^ j) <= me)
    def _():
        k_ref[...] = part(1).astype(BF)
        v_ref[...] = part(2).astype(BF)


def qkv(meta, n_parts, w, m, b):
    count = len(n_parts)
    R, L, W = n_parts[0].shape
    T = count * L
    row = pl.BlockSpec((R, L, W), lambda j, _: (0, j, 0))
    return pl.pallas_call(
        functools.partial(qkv_kernel, W=W, count=count, R=R),
        grid_spec=pltpu.PrefetchScalarGridSpec(
            num_scalar_prefetch=1,
            grid=(count,),
            in_specs=[whole_spec(x.shape) for x in (*n_parts, w, m, b)],
            out_specs=[whole_spec((R, L, W)), row, row],
            scratch_shapes=[pltpu.VMEM((R * L, W), BF), pltpu.VMEM((W, 3 * W), BF)],
        ),
        out_shape=[
            jax.ShapeDtypeStruct((R, L, W), BF),
            jax.ShapeDtypeStruct((R, T, W), BF),
            jax.ShapeDtypeStruct((R, T, W), BF),
        ],
        compiler_params=pltpu.CompilerParams(vmem_limit_bytes=60 << 20),
        cost_estimate=pl.CostEstimate(
            flops=4 * R * T * W * 2 * W, bytes_accessed=2 * (R * T * W + w.size + 2 * R * T * W), transcendentals=0
        ),
        name="qkv",
    )(meta, *n_parts, w, m, b)


def mid_kernel(
    o_ref, x_ref, dy_ref, wout_ref, e1_ref, e2_ref, x0_ref, x1_ref, gain_ref, shift_ref, xb_ref,
    res_ref, na_ref, da_ref, lo_ref,
):
    r = pl.program_id(0)
    D, W = o_ref.shape[2], na_ref.shape[2]
    rank = e1_ref.shape[1]
    o, dy = o_ref[0], dy_ref[0]
    lo = dot_nt(o, e1_ref[0]).astype(BF)
    lo_ref[0] = lo
    res = x_ref[0].astype(F32) + dot_nn(o, wout_ref[...]) + dot_nn(lo, x0_ref[0]) + xb_ref[...]
    res_ref[0] = res
    z, _ = layer_stats(res)
    n2 = (z * gain_ref[...] + shift_ref[...]).astype(BF)
    l3 = dot_nt(n2, e2_ref[0]).astype(BF)
    na_ref[0] = jnp.concatenate([n2, place(l3, r * rank, W - D)], axis=1)
    dl4 = dot_nt(dy, x1_ref[0]).astype(BF)
    da_ref[0] = jnp.concatenate([dy, place(dl4, r * rank, W - D)], axis=1)


def mid(o, x, dy, wout, e1, e2, x0, x1, gain, shift, xb, W):
    R, L, D = o.shape
    rank = e1.shape[1]
    row = pl.BlockSpec((1, L, D), lambda r: (r, 0, 0))
    wide = pl.BlockSpec((1, L, W), lambda r: (r, 0, 0))
    small = pl.BlockSpec((1, rank, D), lambda r: (r, 0, 0))
    return pl.pallas_call(
        mid_kernel,
        grid=(R,),
        in_specs=[row] * 3 + [whole_spec(wout.shape)] + [small] * 4 + [whole_spec((1, D))] * 3,
        out_specs=[row, wide, wide, pl.BlockSpec((1, L, rank), lambda r: (r, 0, 0))],
        out_shape=[
            jax.ShapeDtypeStruct((R, L, D), F32),
            jax.ShapeDtypeStruct((R, L, W), BF),
            jax.ShapeDtypeStruct((R, L, W), BF),
            jax.ShapeDtypeStruct((R, L, rank), BF),
        ],
        compiler_params=pltpu.CompilerParams(vmem_limit_bytes=48 << 20),
        cost_estimate=pl.CostEstimate(flops=2 * R * L * D * D, bytes_accessed=16 * R * L * D, transcendentals=0),
        name="mid",
    )(o, x, dy, wout, e1, e2, x0, x1, gain, shift, xb)


def ffn_kernel(
    na_ref, da_ref, res_ref, o_ref, lo_ref, wexp_ref, wshr_ref, rexp_ref, rshr_ref, eu_ref, eur_ref,
    hd_ref, hdr_ref, b_ref, br_ref, x0_ref, x1_ref, e1_ref, e2_ref, wout_ref, gain_ref, xb_ref,
    y_ref, dr_ref, do_ref, g1_ref, g2_ref, gx0_ref, gx1_ref, ge_ref, ger_ref, gh_ref, ghr_ref,
    out_acc, dn_acc, we_ref, ws_ref, l3_ref, dl4_ref, *, R, per, co,
):
    f = pl.program_id(0)
    last = pl.num_programs(0) - 1
    N, W = na_ref.shape
    L, D, rank = N // R, res_ref.shape[2], x0_ref.shape[1]

    @pl.when(f == 0)
    def _():
        out_acc[...] = jnp.zeros_like(out_acc)
        dn_acc[...] = jnp.zeros_like(dn_acc)
        we_ref[D:] = jnp.zeros((W - D, we_ref.shape[1]), BF)
        ws_ref[D:] = jnp.zeros((W - D, ws_ref.shape[1]), BF)
        for r in range(R):
            l3_ref[r] = taken(na_ref[r * L : (r + 1) * L, D // 128 * 128 :], D % 128 + r * rank, rank)
            dl4_ref[r] = taken(da_ref[r * L : (r + 1) * L, D // 128 * 128 :], D % 128 + r * rank, rank)

    def narrow(eu, hd, width):
        for r in range(R):
            we_ref[D + r * rank : D + (r + 1) * rank, :width] = eu[r]
            ws_ref[D + r * rank : D + (r + 1) * rank, :width] = hd[r]

    def block(width, b, ge, gh):
        we, ws = we_ref[:, :width], ws_ref[:, :width]
        h = dot_nn(na_ref[...], we) + b
        dg = dot_nn(da_ref[...], ws)
        c0, c1 = 0.7978845608028654, 0.7978845608028654 * 0.044715
        hh = h * h
        th = jnp.tanh(h * (c0 + c1 * hh))
        half = 0.5 + 0.5 * th
        g = (h * half).astype(BF)
        slope = half + (h * (0.5 - 0.5 * (th * th))) * (c0 + (3 * c1) * hh)
        dh = (dg * slope).astype(BF)
        out_acc[...] += dot_nt(g, ws)
        dn_acc[...] += dot_nt(dh, we)
        for r in range(R):
            gh[r] = dot_nn(dl4_ref[r], g[r * L : (r + 1) * L])
            ge[r] = dot_nn(l3_ref[r], dh[r * L : (r + 1) * L])

    we_ref[:D] = wexp_ref[...].reshape(D, -1)
    if per:
        for part in range(per):

            @pl.when(lax.rem(f, per) == part)
            def _(part=part):
                for s in range(wshr_ref.shape[0]):
                    ws_ref[s * co : (s + 1) * co] = wshr_ref[s, 0, part * co : (part + 1) * co]

    else:
        ws_ref[:D] = wshr_ref[0]
    narrow(eu_ref, hd_ref, we_ref.shape[1])
    block(we_ref.shape[1], b_ref[...], ge_ref, gh_ref)

    @pl.when(f == last)
    def _():
        width = rexp_ref.shape[1]
        we_ref[:D, :width] = rexp_ref[...]
        ws_ref[:D, :width] = rshr_ref[...]
        narrow(eur_ref, hdr_ref, width)
        block(width, br_ref[...], ger_ref, ghr_ref)

        def rows(r, carry):
            here = pl.ds(pl.multiple_of(r * L, L), L)
            edge = D // 128 * 128
            dy = da_ref[here, :D]
            l4_t = taken(out_acc[here, edge:].astype(BF), D % 128 + r * rank, rank)
            dl3_t = taken(dn_acc[here, edge:].astype(BF), D % 128 + r * rank, rank)
            gx1_ref[r] = dot_nn(l4_t, dy)
            g2_ref[r] = dot_nn(dl3_t, na_ref[here, :D])
            res = res_ref[r]
            low = lambda t, w: lax.dot_general(t, w, (((0,), (0,)), ((), ())), preferred_element_type=F32)
            y_ref[r] = (res + out_acc[here, :D] + low(l4_t, x1_ref[r]) + xb_ref[...]).astype(BF).T
            e = (dn_acc[here, :D] + low(dl3_t, e2_ref[r])) * gain_ref[...]
            z, inv = layer_stats(res)
            dr = dy.astype(F32) + norm_back(e, z, inv)
            dr_ref[r] = dr
            drb = dr.astype(BF)
            dl2 = dot_nt(drb, x0_ref[r]).astype(BF)
            do_ref[r] = (dot_nt(drb, wout_ref[...]) + dot_nn(dl2, e1_ref[r])).astype(BF)
            g1_ref[r] = dot_nn(turned(dl2), o_ref[r])
            gx0_ref[r] = dot_nn(turned(lo_ref[r]), drb)
            return carry

        lax.fori_loop(0, R, rows, 0)


def ffn(na, da, res, o, lo, wexp, wshr, rexp, rshr, eu, eur, hd, hdr, b, br, x0, x1, e1, e2, wout, gain, xb):
    R, L, D = res.shape
    N, W = na.shape
    rank = x0.shape[1]
    width, rem = wexp.shape[-1], rexp.shape[1]
    blocks = eu.shape[2] // width
    cols = lambda *lead: pl.BlockSpec(lead + (width,), lambda f: (0,) * len(lead) + (f,))
    if wexp.ndim == 4:
        S, C = wexp.shape[:2]
        per, co = S // C, D // S
        wexp_spec = pl.BlockSpec((1, C, D // C, width), lambda f: (f, 0, 0, 0))
        wshr_spec = pl.BlockSpec((S, 1, D // C, width), lambda f: (0, f // per, 1, 0))
    else:
        per = co = 0
        wexp_spec = wshr_spec = pl.BlockSpec((1, D, width), lambda f: (f, 0, 0))
    shapes = [
        ((R, D, L), BF), ((R, L, D), F32), ((R, L, D), BF),
        ((R, rank, D), F32), ((R, rank, D), F32), ((R, rank, D), F32), ((R, rank, D), F32),
        ((R, rank, blocks * width), F32), ((R, rank, rem), F32), ((R, rank, blocks * width), F32), ((R, rank, rem), F32),
    ]
    out_specs = [whole_spec(s) for s, _ in shapes]
    out_specs[7] = out_specs[9] = cols(R, rank)
    ff = blocks * width + rem
    return pl.pallas_call(
        functools.partial(ffn_kernel, R=R, per=per, co=co),
        grid=(blocks,),
        in_specs=[whole_spec(a.shape) for a in (na, da, res, o, lo)]
        + [wexp_spec, wshr_spec, whole_spec(rexp.shape), whole_spec(rshr.shape)]
        + [cols(R, rank), whole_spec(eur.shape), cols(R, rank), whole_spec(hdr.shape), cols(1), whole_spec(br.shape)]
        + [whole_spec(a.shape) for a in (x0, x1, e1, e2, wout, gain, xb)],
        out_specs=out_specs,
        out_shape=[jax.ShapeDtypeStruct(s, d) for s, d in shapes],
        scratch_shapes=[
            pltpu.VMEM((N, W), F32), pltpu.VMEM((N, W), F32), pltpu.VMEM((W, width), BF), pltpu.VMEM((W, width), BF),
            pltpu.VMEM((R, rank, L), BF), pltpu.VMEM((R, rank, L), BF),
        ],
        compiler_params=pltpu.CompilerParams(vmem_limit_bytes=60 << 20),
        cost_estimate=pl.CostEstimate(
            flops=16 * N * D * ff, bytes_accessed=4 * D * ff + 24 * N * D, transcendentals=N * ff
        ),
        name="ffn",
    )(na, da, res, o, lo, wexp, wshr, rexp, rshr, eu, eur, hd, hdr, b, br, x0, x1, e1, e2, wout, gain, xb)


def project_kernel(meta_ref, dq_ref, dk_ref, dv_ref, w_ref, m_ref, *refs, W, count, r):
    n_refs, refs = refs[:count], refs[count:]
    mine_ref, o_refs, g_ref, n_ref, t_ref, wa_ref = refs[0], refs[1:count], refs[count], *refs[count + 1 :]
    j = pl.program_id(0)
    me = meta_ref[0]
    D = w_ref.shape[0]
    rank = m_ref.shape[1]
    edge = D // 128 * 128
    for jj in range(count):

        @pl.when(j == jj)
        def _(jj=jj):
            n_ref[...] = n_refs[jj][0]

    @pl.when(j == 0)
    def _():
        g_ref[...] = jnp.zeros_like(g_ref)
        wa_ref[:D] = w_ref[...]
        wa_ref[D : D + rank] = m_ref[0]
        wa_ref[D + rank :] = jnp.zeros((W - D - rank, 3 * W), BF)

    def work(pieces):
        low_t = taken(n_ref[:, edge:], D % 128 + r * rank, rank)
        total = sum(dot_nt(d[0], wa_ref[:, i * W : (i + 1) * W]) for i, d in pieces)
        for i, d in pieces:
            g_ref[i] += dot_nn(low_t, d[0])
        g_ref[3] += dot_nn(taken(total[:, edge:].astype(BF), D % 128, rank), n_ref[...])
        return total

    @pl.when(j == 0)
    def _():
        mine_ref[...] = work([(0, dq_ref), (1, dk_ref), (2, dv_ref)])

    @pl.when((j > 0) & ((me ^ j) < me))
    def _():
        t_ref[...] = work([(1, dk_ref), (2, dv_ref)]).astype(BF)

    for jj in range(1, count):

        @pl.when(j == jj)
        def _(jj=jj):
            o_refs[jj - 1][...] = t_ref[...]


def project(meta, dq, dk, dv, w, m, n_parts, r):
    count = len(n_parts)
    _, L, W = dq.shape
    T = count * L
    rank = m.shape[1]
    out = pl.pallas_call(
        functools.partial(project_kernel, W=W, count=count, r=r),
        grid_spec=pltpu.PrefetchScalarGridSpec(
            num_scalar_prefetch=1,
            grid=(count,),
            in_specs=[
                whole_spec(dq.shape),
                pl.BlockSpec((1, L, W), lambda j, _: (0, j, 0)),
                pl.BlockSpec((1, L, W), lambda j, _: (0, j, 0)),
                whole_spec(w.shape),
                pl.BlockSpec((1, rank, 3 * W), lambda j, _: (r, 0, 0)),
            ]
            + [pl.BlockSpec((1, L, W), lambda j, _: (r, 0, 0))] * count,
            out_specs=[whole_spec((L, W))] * count + [whole_spec((4, rank, W))],
            scratch_shapes=[pltpu.VMEM((L, W), BF), pltpu.VMEM((L, W), BF), pltpu.VMEM((W, 3 * W), BF)],
        ),
        out_shape=[jax.ShapeDtypeStruct((L, W), F32)]
        + [jax.ShapeDtypeStruct((L, W), BF)] * (count - 1)
        + [jax.ShapeDtypeStruct((4, rank, W), F32)],
        compiler_params=pltpu.CompilerParams(vmem_limit_bytes=60 << 20),
        cost_estimate=pl.CostEstimate(
            flops=6 * T * W * 2 * W, bytes_accessed=2 * (w.size + 2 * T * W + 2 * T * W), transcendentals=0
        ),
        name="project",
    )(meta, dq, dk, dv, w, m, *n_parts)
    return out[:count], out[count]


def norm_kernel(x_ref, dy_ref, gain_ref, shift_ref, e_ref, n_ref, xr_ref, dyr_ref):
    x = x_ref[0].astype(F32)
    centred = x - jnp.mean(x, axis=0, keepdims=True)
    inv = lax.rsqrt(jnp.mean(centred * centred, axis=0, keepdims=True) + EPS)
    n = (centred * inv * gain_ref[...] + shift_ref[...]).astype(BF).T
    low = dot_nt(n, e_ref[0]).astype(BF)
    narrow = place(low, pl.program_id(0) * low.shape[1], n_ref.shape[2] - n.shape[1])
    n_ref[0] = jnp.concatenate([n, narrow], axis=1)
    xr_ref[0] = x_ref[0].T
    dyr_ref[0] = dy_ref[0].T


def first_norm(x_t, dy_t, gain, shift, e_t, W):
    R, D, L = x_t.shape
    col = pl.BlockSpec((1, D, L), lambda r: (r, 0, 0))
    row = pl.BlockSpec((1, L, D), lambda r: (r, 0, 0))
    return pl.pallas_call(
        norm_kernel,
        grid=(R,),
        in_specs=[col, col, whole_spec((D, 1)), whole_spec((D, 1)), pl.BlockSpec((1,) + e_t.shape[1:], lambda r: (r, 0, 0))],
        out_specs=[pl.BlockSpec((1, L, W), lambda r: (r, 0, 0)), row, row],
        out_shape=[jax.ShapeDtypeStruct((R, L, W), BF)] + [jax.ShapeDtypeStruct((R, L, D), BF)] * 2,
        compiler_params=pltpu.CompilerParams(vmem_limit_bytes=48 << 20),
        cost_estimate=pl.CostEstimate(flops=10 * x_t.size, bytes_accessed=10 * x_t.size, transcendentals=0),
        name="first_norm",
    )(x_t, dy_t, gain[:, None], shift[:, None], e_t)


def last_kernel(*refs, count, alias):
    if alias:
        refs = refs[1:]
    terms, (dr_ref, x_ref, gain_ref, e_ref, o_ref) = refs[:count], refs[count:]
    D = x_ref.shape[2]
    dn = terms[0][...]
    for t in terms[1:]:
        dn = dn + t[...].astype(F32)
    edge = D // 128 * 128
    rank = e_ref.shape[1]
    low_t = taken(dn[:, edge:].astype(BF), D % 128, rank)
    dn = dn[:, :D] + lax.dot_general(low_t, e_ref[0], (((0,), (0,)), ((), ())), preferred_element_type=F32)
    z, inv = layer_stats(x_ref[0].astype(F32))
    o_ref[0] = (dr_ref[0] + norm_back(dn * gain_ref[...], z, inv)).astype(BF).T


def last(r, before, terms, dr, x, gain, e_t):
    R, L, D = x.shape
    alias = before is not None
    return pl.pallas_call(
        functools.partial(last_kernel, count=len(terms), alias=alias),
        grid=(1,),
        in_specs=[pl.BlockSpec(memory_space=pl.ANY)] * alias
        + [whole_spec(t.shape) for t in terms]
        + [pl.BlockSpec((1, L, D), lambda i: (r, 0, 0))] * 2
        + [whole_spec((1, D)), pl.BlockSpec((1,) + e_t.shape[1:], lambda i: (r, 0, 0))],
        out_specs=pl.BlockSpec((1, D, L), lambda i: (r, 0, 0)),
        out_shape=jax.ShapeDtypeStruct((R, D, L), BF),
        input_output_aliases={0: 0} if alias else {},
        compiler_params=pltpu.CompilerParams(vmem_limit_bytes=48 << 20),
        cost_estimate=pl.CostEstimate(flops=20 * L * D, bytes_accessed=12 * L * D, transcendentals=0),
        name="last",
    )(*([before] if alias else []), *terms, dr, x, gain, e_t)


def late_kernel(slot_ref, part_ref, *refs, R, parts, D, W):
    g_refs, mix_ref, entry_ref, total = refs[:R], refs[R], refs[R + 1], refs[R + 2]
    total[...] = jnp.zeros_like(total)
    count = g_refs[0].shape[0]
    for r in range(R):

        def one(i, carry):
            a = slot_ref[r * count + i]
            c = part_ref[i]
            total[a, c] = total[a, c] + g_refs[r][i].astype(F32)
            return carry

        lax.fori_loop(0, count, one, 0)
    per = parts // 4
    wide = [jnp.concatenate([total[:, i * per + p] for p in range(per)], axis=-1) for i in range(4)]
    mix_ref[...] = jnp.concatenate([w[:, :, :D] for w in wide[:3]], axis=-1)
    entry_ref[...] = wide[3][:, :, :D]


def late_slots(slot, part, gs, adapters, parts, D, W):
    R = len(gs)
    _, rank, width = gs[0].shape
    return pl.pallas_call(
        functools.partial(late_kernel, R=R, parts=parts, D=D, W=W),
        grid_spec=pltpu.PrefetchScalarGridSpec(
            num_scalar_prefetch=2,
            grid=(1,),
            in_specs=[whole_spec(g.shape) for g in gs],
            out_specs=[whole_spec((adapters, rank, 3 * D)), whole_spec((adapters, rank, D))],
            scratch_shapes=[pltpu.VMEM((adapters, parts, rank, width), F32)],
        ),
        out_shape=[
            jax.ShapeDtypeStruct((adapters, rank, 3 * D), F32),
            jax.ShapeDtypeStruct((adapters, rank, D), F32),
        ],
        compiler_params=pltpu.CompilerParams(vmem_limit_bytes=48 << 20),
        cost_estimate=pl.CostEstimate(flops=0, bytes_accessed=8 << 20, transcendentals=0),
        name="late_slots",
    )(slot, part, *gs)


def mm(pattern, a, b):
    return jnp.einsum(pattern, a, b, preferred_element_type=F32)


def layer_stats(v):
    middle = jnp.mean(v, axis=-1, keepdims=True)
    centred = v - middle
    inv = lax.rsqrt(jnp.mean(centred * centred, axis=-1, keepdims=True) + EPS)
    return centred * inv, inv


def norm_back(e, z, inv):
    return (e - jnp.mean(e, -1, keepdims=True) - z * jnp.mean(e * z, -1, keepdims=True)) * inv


def swap(x, axis, bit, needed):
    n = lax.axis_size(axis)
    return lax.ppermute(x, axis, [(d ^ bit, d) for d in range(n) if needed(d)])


def blocks_of(x, bits):
    found = {0: x}
    for bit in reversed(bits):
        for j in sorted(found):
            found[j | bit] = swap(found[j], "ctx", bit, lambda d, k=j | bit: (d ^ k) < d)
    return [found[j] for j in sorted(found)]


def blocks_back(parts, bits):
    held = {j: [p] for j, p in enumerate(parts)}
    for bit in bits:
        for j in sorted(held):
            if j & bit:
                sent = held.pop(j)
                sent = sent[0] if len(sent) == 1 else sum(t.astype(F32) for t in sent).astype(BF)
                got = swap(sent, "ctx", bit, lambda d, k=j, b=bit: ((d ^ b) ^ k) < (d ^ b))
                held[j ^ bit].append(got)
    return held[0]


def ctx_sum_rows(g, bits):
    n = lax.axis_size("ctx")
    me = lax.axis_index("ctx")
    for bit in reversed(bits):
        half = g.shape[0] // 2
        mine = (me & bit) != 0
        low, high = g[:half], g[half:]
        got = lax.ppermute(jnp.where(mine, low, high), "ctx", [(d, d ^ bit) for d in range(n)])
        g = jnp.where(mine, high, low) + got
    return g


def gather_all(x, seq_count, ctx_count):
    n = seq_count * ctx_count
    seq_bits = [ctx_count << i for i in range(seq_count.bit_length() - 1)]
    ctx_bits = [1 << i for i in range(ctx_count.bit_length() - 1)]
    held, order = x[None], [0]
    for bit in seq_bits + ctx_bits[::-1]:
        got = lax.ppermute(held, BOTH, [(d, d ^ bit) for d in range(n)])
        held = jnp.concatenate([held, got], 0)
        order = order + [o ^ bit for o in order]
    return held, order


def slots_kernel(index_ref, g_ref, *refs, count, spans):
    outs, total = refs[:-1], refs[-1]
    total[...] = jnp.zeros_like(total)

    def one(i, carry):
        a = index_ref[i]
        total[a] = total[a] + g_ref[i].astype(F32)
        return carry

    lax.fori_loop(0, count, one, 0)
    for out, pieces in zip(outs, spans):
        parts = [total[:, :, first : first + width] for first, width in pieces]
        out[...] = parts[0] if len(parts) == 1 else jnp.concatenate(parts, axis=-1)


def to_slots(index, g, adapters, spans):
    count, rank, wide = g.shape
    rows = 8
    widths = [sum(w for _, w in pieces) for pieces in spans]
    return pl.pallas_call(
        functools.partial(slots_kernel, count=count, spans=spans),
        grid_spec=pltpu.PrefetchScalarGridSpec(
            num_scalar_prefetch=1,
            grid=(rank // rows,),
            in_specs=[pl.BlockSpec((count, rows, wide), lambda i, m: (0, i, 0))],
            out_specs=[pl.BlockSpec((adapters, rows, w), lambda i, m: (0, i, 0)) for w in widths],
            scratch_shapes=[pltpu.VMEM((adapters, rows, wide), F32)],
        ),
        out_shape=[jax.ShapeDtypeStruct((adapters, rank, w), F32) for w in widths],
        compiler_params=pltpu.CompilerParams(vmem_limit_bytes=48 << 20),
        cost_estimate=pl.CostEstimate(
            flops=count * rank * wide, bytes_accessed=count * rank * wide * 2 + adapters * rank * wide * 4, transcendentals=0
        ),
        name="to_slots",
    )(index, g)


def per_device(
    tokens, segments, adapter_index, norm_gains, norm_shifts, head_biases, expand_bias, exit_biases,
    mixing_weight, output_weight, expand_weight, shrink_weight,
    entry_adapters, mixing_adapters, expand_adapters, hidden_adapters, exit_adapters, cotangent,
):
    micro, seqs, L, D = tokens.shape
    R = micro * seqs
    adapters, rank = mixing_adapters.shape[:2]
    FF = expand_bias.shape[0]
    C = lax.axis_size("ctx")
    S = lax.axis_size("seq")
    bits = [1 << i for i in range(C.bit_length() - 1)]
    me = lax.axis_index("ctx")
    T = C * L
    W = -(-D // 128) * 128
    pad = W - D

    rows = mixing_weight.shape[0]
    cm, co, ce = mixing_weight.shape[1], output_weight.shape[1], expand_weight.shape[1]
    first = jnp.concatenate([mixing_weight, output_weight], 1)
    first = jnp.concatenate([first[: rows // 2], first[rows // 2 :]], 1)
    main = ce // 128 * 128
    rem = ce - main
    per = S // C
    shr_t = shrink_weight.T.reshape(co, per, ce).transpose(1, 0, 2)
    rest = jnp.concatenate([expand_weight[:, main:].reshape(-1), shr_t[:, :, main:].reshape(-1)])
    rest_rows = -(-rest.shape[0] // first.shape[1])
    rest = jnp.pad(rest, (0, rest_rows * first.shape[1] - rest.shape[0])).reshape(rest_rows, -1)
    first = jnp.concatenate([first, rest], 0)
    second = jnp.concatenate([expand_weight[:, :main], shr_t[:, :, :main].reshape(per * co, main)], 0)
    g1 = lax.all_gather(first, BOTH)
    g2 = lax.all_gather(second, BOTH).reshape(S, C, -1, main)
    w_mix, w_out = unpack(g1, S, C, rows // 2, cm, co, D, W)
    if rows % 16 == 0 and per * co == rows and co % 8 == 0:
        w_exp = w_shr = g2
    else:
        w_exp = g2[:, :, :rows].reshape(S, D, main)
        w_shr = g2[:, :, rows:].reshape(S, C, per, co, main).transpose(1, 2, 0, 3, 4).reshape(S, D, main)
    flat = g1[:, rows // 2 :].reshape(S, C, -1)
    r_exp = flat[..., : rows * rem].reshape(S, C, rows, rem).transpose(1, 2, 0, 3).reshape(D, S * rem)
    r_shr = flat[..., rows * rem : rows * rem + per * co * rem].reshape(S, C, per, co, rem)
    r_shr = r_shr.transpose(0, 3, 1, 2, 4).reshape(D, S * rem)

    def split_ff(m):
        m = m.reshape(m.shape[:-1] + (S, ce))
        return m[..., :main].reshape(m.shape[:-2] + (S * main,)), m[..., main:].reshape(m.shape[:-2] + (S * rem,))

    index = adapter_index.reshape(R)
    take = lambda table, axis: jnp.stack(
        [lax.dynamic_index_in_dim(table, index[r], axis, keepdims=False) for r in range(R)], axis
    )
    entry = take(entry_adapters, 1)
    mix_up = take(mixing_adapters, 0)
    exp_up = take(expand_adapters, 0)
    hid = take(hidden_adapters, 0)
    exit_up = take(exit_adapters, 1)
    pad_heads = lambda m: jnp.concatenate([padded(m[..., i * D : (i + 1) * D]) for i in range(3)], -1)
    padded = lambda m: jnp.pad(m, [(0, 0)] * (m.ndim - 1) + [(0, pad)])
    mix_up = pad_heads(mix_up)
    flip = lambda m: jnp.swapaxes(m, -1, -2)
    entry_t = flip(entry)
    exp_main, exp_rest = split_ff(exp_up)
    hid_main, hid_rest = split_ff(flip(hid))
    bias_main, bias_rest = split_ff(expand_bias[None])
    head_bias = pad_heads(jnp.concatenate([head_biases[0], jnp.zeros_like(head_biases[0]), head_biases[1]])[None])

    seg = segments.reshape(R, L)
    seg_blocks = blocks_of(seg, bits)
    first_block = me * jnp.ones((R,), jnp.int32)
    for j, other in enumerate(seg_blocks):
        reached = ((me ^ j) <= me) & jnp.any(other == seg[:, :1], axis=1)
        first_block = jnp.where(reached, jnp.minimum(first_block, me ^ j), first_block)
    meta = jnp.concatenate([me[None], first_block]).astype(jnp.int32)
    qa, ka = document_lanes(seg, jnp.concatenate(seg_blocks, 1))

    n1, x, dy = first_norm(
        flip(tokens.reshape(R, L, D)), flip(cotangent.reshape(R, L, D)), norm_gains[0], norm_shifts[0],
        entry_t[0], W,
    )
    n1_parts = blocks_of(n1, bits)
    q, k, v = qkv(meta, n1_parts, w_mix, mix_up, head_bias)
    o, extra = attn_fwd(meta, q, k, v, qa, ka, D)

    res, na, da, lo = mid(
        o, x, dy, w_out, entry_t[1], entry_t[2], exit_up[0], exit_up[1], norm_gains[1][None], norm_shifts[1][None],
        exit_biases[0][None], W,
    )
    y, dr, do, g1, g2_, gx0, gx1, ge, ger, gh, ghr = ffn(
        na.reshape(R * L, W), da.reshape(R * L, W), res, o, lo, w_exp, w_shr, r_exp, r_shr,
        exp_main, exp_rest, hid_main, hid_rest, bias_main, bias_rest,
        exit_up[0], exit_up[1], entry_t[1], entry_t[2], w_out, norm_gains[1][None], exit_biases[1][None],
    )
    layer_output = flip(y).reshape(tokens.shape)

    number = jnp.broadcast_to((index.astype(F32) / C)[:, None, None], (R, rank, 128))
    early = jnp.concatenate([g1, g2_, gx0, gx1, ge, ger, gh, ghr, number], -1).reshape(R * rank, -1)
    early = ctx_sum_rows(early, bits).astype(BF)
    early = lax.all_gather(early, BOTH).reshape(S * R, rank, -1)
    all_index = early[:, 0, -1].astype(jnp.int32)
    spans = [[(i * D, D)] for i in range(4)]
    for at in (4 * D, 4 * D + FF):
        spans.append(
            [p for i in range(S) for p in ((at + i * main, main), (at + S * main + i * rem, rem))]
        )
    entry1_g, entry2_g, exit0_g, exit1_g, expand_g, hidden_g = to_slots(all_index, early, adapters, spans)

    input_grad, late, terms = None, [], []
    for r in range(R):
        dq, dk, dv = attn_bwd(meta, q, k, v, do, o, extra, ka, r)
        if r:
            dk, terms[r - 1] = lax.optimization_barrier((dk, terms[r - 1]))
        parts, g = project(meta, dq, dk, dv, w_mix, mix_up, n1_parts, r)
        if r + 1 < R:
            do, parts = lax.optimization_barrier((do, parts))
        terms.append(blocks_back(parts, bits))
        g = g.reshape(4, rank, C // 4, -1).transpose(0, 2, 1, 3).reshape(C, rank, -1)
        late.append(gather_all(ctx_sum_rows(g, bits)[0].astype(BF), S, C))
    for r in range(R):
        input_grad = last(r, input_grad, terms[r], dr, x, norm_gains[0][None], entry_t[0])
    device = lax.axis_index("seq") * C + me
    order = device ^ jnp.array(late[0][1], jnp.int32)
    by_row = all_index.reshape(S, R)
    slot = jnp.concatenate([jnp.sum(jnp.where((order // C)[:, None] == jnp.arange(S), by_row[:, r], 0), 1) for r in range(R)])
    mixing_g, entry0_g = late_slots(slot, order % C, [g for g, _ in late], adapters, C, D, W)
    input_grad = flip(input_grad).reshape(tokens.shape)

    return (
        layer_output,
        input_grad,
        jnp.stack([flip(entry0_g), flip(entry1_g), flip(entry2_g)]),
        mixing_g,
        expand_g,
        flip(hidden_g),
        jnp.stack([exit0_g, exit1_g]),
    )


def solution(mesh):
    rows = P(None, "seq", "ctx", None)
    weight = P("ctx", "seq")
    in_specs = (
        (rows, P(None, "seq", "ctx"), P(None, "seq")) + (P(),) * 5 + (weight,) * 4 + (P(),) * 5 + (rows,)
    )
    out_specs = (rows, rows) + (P(),) * 5
    return jax.shard_map(per_device, mesh=mesh, in_specs=in_specs, out_specs=out_specs, check_vma=False)
```

```python
import functools

import jax
import jax.numpy as jnp
from jax import lax
from jax.experimental import pallas as pl
from jax.experimental.pallas import tpu as pltpu
from jax.sharding import PartitionSpec as P

HEADS = 17
EPS = 1e-05
NEG = -1e30
BF = jnp.bfloat16
F32 = jnp.float32
BOTH = ("seq", "ctx")


FAR = -1e30


def product(a, b, ca, cb):
    return lax.dot_general(a, b, (((ca,), (cb,)), ((), ())), preferred_element_type=F32)


def thirds(x):
    a = x.astype(BF)
    b = (x - a.astype(F32)).astype(BF)
    c = (x - a.astype(F32) - b.astype(F32)).astype(BF)
    return a, b, c


def lanes_of(h, lane):
    return (lane < 64) if h == 0 else (lane >= 64)


def attn_fwd_kernel(
    meta_ref, q_ref, k_ref, v_ref, qa_ref, ka_ref, o_ref, a_ref, kh_ref, vt_ref, s_ref, acc_ref, st_ref, *, L
):
    r = pl.program_id(0)
    me = meta_ref[0]
    lo = meta_ref[1 + r]
    lane = lax.broadcasted_iota(jnp.int32, (1, 128), 1)
    vt_ref[...] = v_ref[0].T
    q2, qa = q_ref[0], qa_ref[0]
    qh = [jnp.where(lanes_of(h, lane), q2, qa).T for h in range(2)]
    for h in range(2):
        kh_ref[h] = jnp.where(lanes_of(h, lane), k_ref[0], ka_ref[0])
        st_ref[h] = jnp.concatenate([jnp.full((1, L), NEG, F32), jnp.zeros((7, L), F32)], axis=0)
    acc_ref[...] = jnp.zeros_like(acc_ref)

    def at(t):
        return pl.multiple_of((t ^ me) * L, L)

    def scores(t, h):
        s_ref[h] = product(kh_ref[h, pl.ds(at(t), L), :], qh[h], 1, 0)

    def gather(t, h, diagonal):
        s = s_ref[h]
        if diagonal:
            ok = lax.broadcasted_iota(jnp.int32, (L, L), 0) <= lax.broadcasted_iota(jnp.int32, (L, L), 1)
            s = jnp.where(ok, s, NEG)
        m = st_ref[h, 0:1]
        new = jnp.maximum(m, jnp.max(s, axis=0, keepdims=True))
        scale = jnp.exp(m - new)
        p = jnp.exp(s - new)
        st_ref[h, 1:2] = st_ref[h, 1:2] * scale + jnp.sum(p, axis=0, keepdims=True)
        st_ref[h, 0:1] = new
        rows = slice(h * 64, (h + 1) * 64)
        acc_ref[rows] = acc_ref[rows] * scale + product(vt_ref[rows, pl.ds(at(t), L)], p.astype(BF), 1, 0)

    scores(lo, 0)

    def body(t, carry):
        scores(t, 1)
        gather(t, 0, False)
        scores(t + 1, 0)
        gather(t, 1, False)
        return carry

    lax.fori_loop(lo, me, body, 0)
    scores(me, 1)
    gather(me, 0, True)
    gather(me, 1, True)
    rows = []
    for h in range(2):
        total = st_ref[h, 1:2]
        sl = slice(h * 64, (h + 1) * 64)
        acc_ref[sl] = acc_ref[sl] / total
        rows.append(thirds(-(st_ref[h, 0:1] + jnp.log(total))))
    o_ref[0] = acc_ref[...].T.astype(o_ref.dtype)
    sub = lax.broadcasted_iota(jnp.int32, (128, 1), 0)
    extra = jnp.zeros((128, L), F32)
    for h in range(2):
        for i in range(3):
            extra = jnp.where(sub == (1 - h) * 64 + 8 + i, rows[h][i].astype(F32), extra)
    a_ref[0, 0] = (qa.astype(F32) + extra.T).astype(BF)


def attn_fwd(meta, q, k, v, qa, ka, D):
    R, L, W = q.shape
    T = k.shape[1]
    NP = W // 128
    col = lambda r, p, m: (r, 0, p)
    one = lambda r, p, m: (r, 0, 0)
    return pl.pallas_call(
        functools.partial(attn_fwd_kernel, L=L),
        grid_spec=pltpu.PrefetchScalarGridSpec(
            num_scalar_prefetch=1,
            grid=(R, NP),
            in_specs=[
                pl.BlockSpec((1, L, 128), col),
                pl.BlockSpec((1, T, 128), col),
                pl.BlockSpec((1, T, 128), col),
                pl.BlockSpec((1, L, 128), one),
                pl.BlockSpec((1, T, 128), one),
            ],
            out_specs=[pl.BlockSpec((1, L, 128), col), pl.BlockSpec((1, 1, L, 128), lambda r, p, m: (r, p, 0, 0))],
            scratch_shapes=[
                pltpu.VMEM((2, T, 128), BF),
                pltpu.VMEM((128, T), BF),
                pltpu.VMEM((2, L, L), F32),
                pltpu.VMEM((128, L), F32),
                pltpu.VMEM((2, 8, L), F32),
            ],
        ),
        out_shape=[jax.ShapeDtypeStruct((R, L, D), BF), jax.ShapeDtypeStruct((R, NP, L, 128), BF)],
        compiler_params=pltpu.CompilerParams(vmem_limit_bytes=48 << 20),
        cost_estimate=pl.CostEstimate(
            flops=R * 40 * L * T * W, bytes_accessed=R * (2 * L + 2 * T) * W * 2, transcendentals=R * L * T * 18
        ),
        name="attn_fwd",
    )(meta, q, k, v, qa, ka)


def attn_bwd_kernel(
    meta_ref, q_ref, k_ref, v_ref, do_ref, o_ref, a_ref, ka_ref, *refs, L, r0, D, first,
):
    dq_ref, dk_ref, dv_ref, kh_ref, vh_ref, kt_ref, s_ref, dp_ref, dqt_ref, dkt_ref, dvt_ref = refs[-11:]
    me = meta_ref[0]
    lo = meta_ref[1 + r0]
    lane = lax.broadcasted_iota(jnp.int32, (1, 128), 1)
    row = lax.broadcasted_iota(jnp.int32, (128, 1), 0)
    limit = D - (pl.program_id(0) + first) * 128
    ones = jnp.where((row % 64 >= 8) & (row % 64 < 11), 1.0, 0.0).astype(BF)
    do2 = jnp.where(lane < limit, do_ref[0], jnp.zeros((), BF))
    o2 = jnp.where(lane < limit, o_ref[0], jnp.zeros((), BF))
    q2 = q_ref[0]
    prod = do2.astype(F32) * o2.astype(F32)
    qh, dh = [], []
    for h in range(2):
        mine = lanes_of(h, lane)
        parts = thirds(-jnp.sum(jnp.where(mine, prod, 0.0), axis=1, keepdims=True))
        extra = jnp.zeros((1, 128), BF)
        for i in range(3):
            extra = jnp.where(lane == (1 - h) * 64 + 8 + i, parts[i], extra)
        dh.append(jnp.where(mine, do2, extra))
        qh.append(jnp.where(mine, q2, a_ref[0, 0]))
    qt, dot_ = q2.T, do2.T
    dqt_ref[...] = jnp.zeros_like(dqt_ref)

    def at(t):
        return pl.multiple_of((t ^ me) * L, L)

    def turn(t):
        here = pl.ds(at(t), L)
        kt = k_ref[0, here, :].T
        vt = v_ref[0, here, :].T
        kt_ref[:, here] = kt
        for h in range(2):
            kh_ref[h, :, here] = jnp.where(lanes_of(h, row), kt, ka_ref[0, :, here])
            vh_ref[h, :, here] = jnp.where(lanes_of(h, row), vt, ones)

    def scores(t, h):
        here = pl.ds(at(t), L)
        s_ref[h] = product(qh[h], kh_ref[h, :, here], 1, 0)
        dp_ref[h] = product(dh[h], vh_ref[h, :, here], 1, 0)

    def gather(t, h, diagonal):
        p = jnp.exp(s_ref[h])
        if diagonal:
            ok = lax.broadcasted_iota(jnp.int32, (L, L), 1) <= lax.broadcasted_iota(jnp.int32, (L, L), 0)
            p = jnp.where(ok, p, 0.0)
        ds = (p * dp_ref[h]).astype(BF)
        rows = slice(h * 64, (h + 1) * 64)
        dvt_ref[rows] = product(dot_[rows], p.astype(BF), 1, 0)
        dkt_ref[rows] = product(qt[rows], ds, 1, 0)
        dqt_ref[rows] += product(kt_ref[rows, pl.ds(at(t), L)], ds, 1, 1)

    def store(t):
        here = pl.ds(at(t), L)
        dk_ref[0, here, :] = dkt_ref[...].astype(BF).T
        dv_ref[0, here, :] = dvt_ref[...].astype(BF).T

    def none(t, carry):
        dk_ref[0, pl.ds(at(t), L), :] = jnp.zeros((L, 128), BF)
        dv_ref[0, pl.ds(at(t), L), :] = jnp.zeros((L, 128), BF)
        return carry

    lax.fori_loop(0, lo, none, 0)
    turn(lo)
    scores(lo, 0)

    def body(t, carry):
        scores(t, 1)
        turn(t + 1)
        gather(t, 0, False)
        scores(t + 1, 0)
        gather(t, 1, False)
        store(t)
        return carry

    lax.fori_loop(lo, me, body, 0)
    scores(me, 1)
    gather(me, 0, True)
    gather(me, 1, True)
    store(me)
    dq_ref[0] = dqt_ref[...].astype(BF).T * jnp.asarray(0.125, BF)


def attn_bwd(meta, q, k, v, do, o, extra, ka_t, r0, first, count, before=()):
    R, L, W = q.shape
    T, D = k.shape[1], do.shape[2]
    col = lambda p, m: (r0, 0, p + first)
    out = lambda p, m: (0, 0, p + first)
    return pl.pallas_call(
        functools.partial(attn_bwd_kernel, L=L, r0=r0, D=D, first=first),
        grid_spec=pltpu.PrefetchScalarGridSpec(
            num_scalar_prefetch=1,
            grid=(count,),
            in_specs=[
                pl.BlockSpec((1, L, 128), col),
                pl.BlockSpec((1, T, 128), col),
                pl.BlockSpec((1, T, 128), col),
                pl.BlockSpec((1, L, 128), col),
                pl.BlockSpec((1, L, 128), col),
                pl.BlockSpec((1, 1, L, 128), lambda p, m: (r0, p + first, 0, 0)),
                pl.BlockSpec((1, 128, T), lambda p, m: (r0, 0, 0)),
            ]
            + [pl.BlockSpec(memory_space=pl.ANY) for _ in before],
            out_specs=[pl.BlockSpec((1, L, 128), out), pl.BlockSpec((1, T, 128), out), pl.BlockSpec((1, T, 128), out)],
            scratch_shapes=[
                pltpu.VMEM((2, 128, T), BF),
                pltpu.VMEM((2, 128, T), BF),
                pltpu.VMEM((128, T), BF),
                pltpu.VMEM((2, L, L), F32),
                pltpu.VMEM((2, L, L), F32),
                pltpu.VMEM((128, L), F32),
                pltpu.VMEM((128, L), F32),
                pltpu.VMEM((128, L), F32),
            ],
        ),
        out_shape=[
            jax.ShapeDtypeStruct((1, L, W), BF),
            jax.ShapeDtypeStruct((1, T, W), BF),
            jax.ShapeDtypeStruct((1, T, W), BF),
        ],
        compiler_params=pltpu.CompilerParams(vmem_limit_bytes=48 << 20),
        input_output_aliases={8 + i: i for i in range(len(before))},
        cost_estimate=pl.CostEstimate(
            flops=60 * L * T * 128 * count, bytes_accessed=(3 * L + 4 * T) * 256 * count, transcendentals=L * T * 2 * count
        ),
        name="attn_bwd",
    )(meta, q, k, v, do, o, extra, ka_t, *before)


def document_lanes(seg_q, seg_k):
    number = jnp.arange(64, dtype=jnp.int32)
    two = lambda m: jnp.concatenate([m, m], -1).astype(BF)
    qa = jnp.where((number < 8) & (number != seg_q[..., None]), FAR, 0.0)
    ka = jnp.where((number == seg_k[..., None]) | ((number >= 8) & (number < 11)), 1.0, 0.0)
    return two(qa), two(ka)


def dot_nn(a, b):
    return lax.dot_general(a, b, (((1,), (0,)), ((), ())), preferred_element_type=F32)


def dot_nt(a, b):
    return lax.dot_general(a, b, (((1,), (1,)), ((), ())), preferred_element_type=F32)


def turned(x):
    rank = x.shape[1]
    eye = (
        lax.broadcasted_iota(jnp.int32, (rank, rank), 0) == lax.broadcasted_iota(jnp.int32, (rank, rank), 1)
    ).astype(F32).astype(BF)
    return dot_nt(eye, x).astype(BF)


def place(x, first, width):
    rank = x.shape[1]
    to = lax.broadcasted_iota(jnp.int32, (rank, width), 1) == lax.broadcasted_iota(jnp.int32, (rank, width), 0) + first
    return dot_nn(x, to.astype(F32).astype(BF)).astype(BF)


def taken(x, first, rank):
    width = x.shape[1]
    to = lax.broadcasted_iota(jnp.int32, (rank, width), 1) == lax.broadcasted_iota(jnp.int32, (rank, width), 0) + first
    return dot_nt(to.astype(F32).astype(BF), x).astype(BF)


def whole_spec(shape, **kw):
    return pl.BlockSpec(shape, lambda *_: (0,) * len(shape), pipeline_mode=pl.Buffered(1))


def unpack_kernel(g_ref, mix_ref, out_ref, rexp_ref, rshr_ref, *, cm, co, D, W, rem, per):
    S = g_ref.shape[0]
    rows = mix_ref.shape[2]
    half_width = cm + co
    for half in range(2):
        at = half * half_width
        mix = jnp.concatenate([g_ref[s, 0, :rows, at : at + cm] for s in range(S)], axis=1)
        out = jnp.concatenate([g_ref[s, 0, :rows, at + cm : at + half_width] for s in range(S)], axis=1)
        zero = jnp.zeros((mix.shape[0], W - D), mix.dtype)
        for i in range(3):
            mix_ref[0, half, :, i * W : (i + 1) * W] = jnp.concatenate([mix[:, i * D : (i + 1) * D], zero], axis=1)
        out_ref[0, half] = out
    for s in range(S):
        for i in range(rem // 8):
            rexp_ref[0, s * rem + i * 8 : s * rem + i * 8 + 8] = g_ref[
                s, 0, rows : rows + 8, i * 2 * rows : (i + 1) * 2 * rows
            ]
    for i in range(per * rem // 8):
        rshr_ref[0, i * 8 : i * 8 + 8] = jnp.concatenate(
            [g_ref[s, 0, rows + 8 : rows + 16, i * co : (i + 1) * co] for s in range(S)], axis=1
        )


def unpack(g, S, C, rows2, cm, co, D, W, rem, per):
    g = g.reshape(S, C, -1, 2 * (cm + co))
    shapes = [(C, 2, rows2, 3 * W), (C, 2, rows2, D), (C, S * rem, 2 * rows2), (C, per * rem, D)]
    mix, out, rexp, rshr = pl.pallas_call(
        functools.partial(unpack_kernel, cm=cm, co=co, D=D, W=W, rem=rem, per=per),
        grid=(C,),
        in_specs=[pl.BlockSpec((S, 1) + g.shape[2:], lambda c: (0, c, 0, 0))],
        out_specs=[pl.BlockSpec((1,) + s[1:], lambda c, n=len(s): (c,) + (0,) * (n - 1)) for s in shapes],
        out_shape=[jax.ShapeDtypeStruct(s, BF) for s in shapes],
        compiler_params=pltpu.CompilerParams(vmem_limit_bytes=48 << 20),
        cost_estimate=pl.CostEstimate(flops=0, bytes_accessed=4 * g.size, transcendentals=0),
        name="unpack",
    )(g)
    return mix.reshape(D, 3 * W), out.reshape(D, D), rexp, rshr.reshape(C * per * rem, D)


def qkv_kernel(meta_ref, *refs, count, W, R):
    n_refs = refs[:count]
    w_ref, m_ref, b_ref, q_ref, k_ref, v_ref, n_ref, wa_ref = refs[count:]
    j = pl.program_id(0)
    me = meta_ref[0]
    D = w_ref.shape[0]
    rank = m_ref.shape[1]
    for jj in range(count):

        @pl.when(j == jj)
        def _(jj=jj):
            n_ref[...] = n_refs[jj][...].reshape(n_ref.shape)

    @pl.when(j == 0)
    def _():
        wa_ref[:D] = w_ref[...]
        for r in range(R):
            wa_ref[D + r * rank : D + (r + 1) * rank] = m_ref[r]
        wa_ref[D + R * rank :] = jnp.zeros((W - D - R * rank, 3 * W), BF)

    def part(i):
        s = slice(i * W, (i + 1) * W)
        return (dot_nn(n_ref[...], wa_ref[:, s]) + b_ref[:, s]).reshape(R, -1, W)

    @pl.when(j == 0)
    def _():
        q_ref[...] = (part(0) * 0.125).astype(BF)

    @pl.when((me ^ j) <= me)
    def _():
        k_ref[...] = part(1).astype(BF)
        v_ref[...] = part(2).astype(BF)


def qkv(meta, n_parts, w, m, b):
    count = len(n_parts)
    R, L, W = n_parts[0].shape
    T = count * L
    row = pl.BlockSpec((R, L, W), lambda j, _: (0, j, 0))
    return pl.pallas_call(
        functools.partial(qkv_kernel, W=W, count=count, R=R),
        grid_spec=pltpu.PrefetchScalarGridSpec(
            num_scalar_prefetch=1,
            grid=(count,),
            in_specs=[whole_spec(x.shape) for x in (*n_parts, w, m, b)],
            out_specs=[whole_spec((R, L, W)), row, row],
            scratch_shapes=[pltpu.VMEM((R * L, W), BF), pltpu.VMEM((W, 3 * W), BF)],
        ),
        out_shape=[
            jax.ShapeDtypeStruct((R, L, W), BF),
            jax.ShapeDtypeStruct((R, T, W), BF),
            jax.ShapeDtypeStruct((R, T, W), BF),
        ],
        compiler_params=pltpu.CompilerParams(vmem_limit_bytes=60 << 20),
        cost_estimate=pl.CostEstimate(
            flops=4 * R * T * W * 2 * W, bytes_accessed=2 * (R * T * W + w.size + 2 * R * T * W), transcendentals=0
        ),
        name="qkv",
    )(meta, *n_parts, w, m, b)


def mid_kernel(
    o_ref, x_ref, dy_ref, wout_ref, e1_ref, e2_ref, x0_ref, x1_ref, gain_ref, shift_ref, xb_ref,
    res_ref, na_ref, da_ref, lo_ref,
):
    r = pl.program_id(0)
    D, W = o_ref.shape[2], na_ref.shape[2]
    rank = e1_ref.shape[1]
    o, dy = o_ref[0], dy_ref[0]
    lo = dot_nt(o, e1_ref[0]).astype(BF)
    lo_ref[0] = lo
    res = x_ref[0].astype(F32) + dot_nn(o, wout_ref[...]) + dot_nn(lo, x0_ref[0]) + xb_ref[...]
    res_ref[0] = res
    z, _ = layer_stats(res)
    n2 = (z * gain_ref[...] + shift_ref[...]).astype(BF)
    l3 = dot_nt(n2, e2_ref[0]).astype(BF)
    na_ref[0] = jnp.concatenate([n2, place(l3, r * rank, W - D)], axis=1)
    dl4 = dot_nt(dy, x1_ref[0]).astype(BF)
    da_ref[0] = jnp.concatenate([dy, place(dl4, r * rank, W - D)], axis=1)


def mid(o, x, dy, wout, e1, e2, x0, x1, gain, shift, xb, W):
    R, L, D = o.shape
    rank = e1.shape[1]
    row = pl.BlockSpec((1, L, D), lambda r: (r, 0, 0))
    wide = pl.BlockSpec((1, L, W), lambda r: (r, 0, 0))
    small = pl.BlockSpec((1, rank, D), lambda r: (r, 0, 0))
    return pl.pallas_call(
        mid_kernel,
        grid=(R,),
        in_specs=[row] * 3 + [whole_spec(wout.shape)] + [small] * 4 + [whole_spec((1, D))] * 3,
        out_specs=[row, wide, wide, pl.BlockSpec((1, L, rank), lambda r: (r, 0, 0))],
        out_shape=[
            jax.ShapeDtypeStruct((R, L, D), F32),
            jax.ShapeDtypeStruct((R, L, W), BF),
            jax.ShapeDtypeStruct((R, L, W), BF),
            jax.ShapeDtypeStruct((R, L, rank), BF),
        ],
        compiler_params=pltpu.CompilerParams(vmem_limit_bytes=48 << 20),
        cost_estimate=pl.CostEstimate(flops=2 * R * L * D * D, bytes_accessed=16 * R * L * D, transcendentals=0),
        name="mid",
    )(o, x, dy, wout, e1, e2, x0, x1, gain, shift, xb)


def ffn_kernel(
    na_ref, da_ref, res_ref, o_ref, lo_ref, wexp_ref, wshr_ref, rexp_ref, rshr_ref, eu_ref, eur_ref,
    hd_ref, hdr_ref, b_ref, br_ref, x0_ref, x1_ref, e1_ref, e2_ref, wout_ref, gain_ref, xb_ref,
    y_ref, dr_ref, do_ref, g1_ref, g2_ref, gx0_ref, gx1_ref, ge_ref, ger_ref, gh_ref, ghr_ref,
    out_acc, dn_acc, we_ref, ws_ref, l3_ref, dl4_ref, *, R, per, co,
):
    f = pl.program_id(0)
    last = pl.num_programs(0) - 1
    N, W = na_ref.shape
    L, D, rank = N // R, res_ref.shape[2], x0_ref.shape[1]

    @pl.when(f == 0)
    def _():
        out_acc[...] = jnp.zeros_like(out_acc)
        dn_acc[...] = jnp.zeros_like(dn_acc)
        we_ref[D:] = jnp.zeros((W - D, we_ref.shape[1]), BF)
        ws_ref[D:] = jnp.zeros((W - D, ws_ref.shape[1]), BF)
        for r in range(R):
            l3_ref[r] = taken(na_ref[r * L : (r + 1) * L, D // 128 * 128 :], D % 128 + r * rank, rank)
            dl4_ref[r] = taken(da_ref[r * L : (r + 1) * L, D // 128 * 128 :], D % 128 + r * rank, rank)

    def narrow(eu, hd, width):
        for r in range(R):
            we_ref[D + r * rank : D + (r + 1) * rank, :width] = eu[r]
            ws_ref[D + r * rank : D + (r + 1) * rank, :width] = hd[r]

    def block(width, b, ge, gh):
        we, ws = we_ref[:, :width], ws_ref[:, :width]
        h = dot_nn(na_ref[...], we) + b
        dg = dot_nn(da_ref[...], ws)
        c0, c1 = 0.7978845608028654, 0.7978845608028654 * 0.044715
        hh = h * h
        th = jnp.tanh(h * (c0 + c1 * hh))
        half = 0.5 + 0.5 * th
        g = (h * half).astype(BF)
        slope = half + (h * (0.5 - 0.5 * (th * th))) * (c0 + (3 * c1) * hh)
        dh = (dg * slope).astype(BF)
        out_acc[...] += dot_nt(g, ws)
        dn_acc[...] += dot_nt(dh, we)
        for r in range(R):
            gh[r] = dot_nn(dl4_ref[r], g[r * L : (r + 1) * L])
            ge[r] = dot_nn(l3_ref[r], dh[r * L : (r + 1) * L])

    we_ref[:D] = wexp_ref[...].reshape(D, -1)
    if per:
        for part in range(per):

            @pl.when(lax.rem(f, per) == part)
            def _(part=part):
                for s in range(wshr_ref.shape[0]):
                    ws_ref[s * co : (s + 1) * co] = wshr_ref[s, 0, part * co : (part + 1) * co]

    else:
        ws_ref[:D] = wshr_ref[0]
    narrow(eu_ref, hd_ref, we_ref.shape[1])
    block(we_ref.shape[1], b_ref[...], ge_ref, gh_ref)

    @pl.when(f == last)
    def _():
        width = rshr_ref.shape[0]
        we_ref[:D, :width] = jnp.concatenate([rexp_ref[c] for c in range(rexp_ref.shape[0])], axis=1).T
        ws_ref[:D, :width] = rshr_ref[...].T
        narrow(eur_ref, hdr_ref, width)
        block(width, br_ref[...], ger_ref, ghr_ref)

        def rows(r, carry):
            here = pl.ds(pl.multiple_of(r * L, L), L)
            edge = D // 128 * 128
            dy = da_ref[here, :D]
            l4_t = taken(out_acc[here, edge:].astype(BF), D % 128 + r * rank, rank)
            dl3_t = taken(dn_acc[here, edge:].astype(BF), D % 128 + r * rank, rank)
            gx1_ref[r] = dot_nn(l4_t, dy)
            g2_ref[r] = dot_nn(dl3_t, na_ref[here, :D])
            res = res_ref[r]
            low = lambda t, w: lax.dot_general(t, w, (((0,), (0,)), ((), ())), preferred_element_type=F32)
            y_ref[r] = (res + out_acc[here, :D] + low(l4_t, x1_ref[r]) + xb_ref[...]).astype(BF).T
            e = (dn_acc[here, :D] + low(dl3_t, e2_ref[r])) * gain_ref[...]
            z, inv = layer_stats(res)
            dr = dy.astype(F32) + norm_back(e, z, inv)
            dr_ref[r] = dr
            drb = dr.astype(BF)
            dl2 = dot_nt(drb, x0_ref[r]).astype(BF)
            do_ref[r] = (dot_nt(drb, wout_ref[...]) + dot_nn(dl2, e1_ref[r])).astype(BF)
            g1_ref[r] = dot_nn(turned(dl2), o_ref[r])
            gx0_ref[r] = dot_nn(turned(lo_ref[r]), drb)
            return carry

        lax.fori_loop(0, R, rows, 0)


def ffn(na, da, res, o, lo, wexp, wshr, rexp, rshr, eu, eur, hd, hdr, b, br, x0, x1, e1, e2, wout, gain, xb):
    R, L, D = res.shape
    N, W = na.shape
    rank = x0.shape[1]
    width, rem = wexp.shape[-1], rshr.shape[0]
    blocks = eu.shape[2] // width
    cols = lambda *lead: pl.BlockSpec(lead + (width,), lambda f: (0,) * len(lead) + (f,))
    if wexp.ndim == 4:
        S, C = wexp.shape[:2]
        per, co = S // C, D // S
        wexp_spec = pl.BlockSpec((1, C, D // C, width), lambda f: (f, 0, 0, 0))
        wshr_spec = pl.BlockSpec((S, 1, D // C, width), lambda f: (0, f // per, 1, 0))
    else:
        per = co = 0
        wexp_spec = wshr_spec = pl.BlockSpec((1, D, width), lambda f: (f, 0, 0))
    shapes = [
        ((R, D, L), BF), ((R, L, D), F32), ((R, L, D), BF),
        ((R, rank, D), F32), ((R, rank, D), F32), ((R, rank, D), F32), ((R, rank, D), F32),
        ((R, rank, blocks * width), F32), ((R, rank, rem), F32), ((R, rank, blocks * width), F32), ((R, rank, rem), F32),
    ]
    out_specs = [whole_spec(s) for s, _ in shapes]
    out_specs[7] = out_specs[9] = cols(R, rank)
    ff = blocks * width + rem
    return pl.pallas_call(
        functools.partial(ffn_kernel, R=R, per=per, co=co),
        grid=(blocks,),
        in_specs=[whole_spec(a.shape) for a in (na, da, res, o, lo)]
        + [wexp_spec, wshr_spec, whole_spec(rexp.shape), whole_spec(rshr.shape)]
        + [cols(R, rank), whole_spec(eur.shape), cols(R, rank), whole_spec(hdr.shape), cols(1), whole_spec(br.shape)]
        + [whole_spec(a.shape) for a in (x0, x1, e1, e2, wout, gain, xb)],
        out_specs=out_specs,
        out_shape=[jax.ShapeDtypeStruct(s, d) for s, d in shapes],
        scratch_shapes=[
            pltpu.VMEM((N, W), F32), pltpu.VMEM((N, W), F32), pltpu.VMEM((W, width), BF), pltpu.VMEM((W, width), BF),
            pltpu.VMEM((R, rank, L), BF), pltpu.VMEM((R, rank, L), BF),
        ],
        compiler_params=pltpu.CompilerParams(vmem_limit_bytes=60 << 20),
        cost_estimate=pl.CostEstimate(
            flops=16 * N * D * ff, bytes_accessed=4 * D * ff + 24 * N * D, transcendentals=N * ff
        ),
        name="ffn",
    )(na, da, res, o, lo, wexp, wshr, rexp, rshr, eu, eur, hd, hdr, b, br, x0, x1, e1, e2, wout, gain, xb)


def project_kernel(meta_ref, dq_ref, dk_ref, dv_ref, w_ref, m_ref, *refs, W, js, r):
    count = len(js)
    n_refs, o_refs = refs[:count], refs[count : 2 * count]
    g_ref, n_ref, t_ref, wa_ref = refs[2 * count :]
    step = pl.program_id(0)
    j = step + js[0]
    me = meta_ref[0]
    D = w_ref.shape[0]
    rank = m_ref.shape[1]
    edge = D // 128 * 128
    for i in range(count):

        @pl.when(step == i)
        def _(i=i):
            n_ref[...] = n_refs[i][0]

    @pl.when(step == 0)
    def _():
        g_ref[...] = jnp.zeros_like(g_ref)
        wa_ref[:D] = w_ref[...]
        wa_ref[D : D + rank] = m_ref[0]
        wa_ref[D + rank :] = jnp.zeros((W - D - rank, 3 * W), BF)

    def work(pieces):
        low_t = taken(n_ref[:, edge:], D % 128 + r * rank, rank)
        total = sum(dot_nt(d[0], wa_ref[:, i * W : (i + 1) * W]) for i, d in pieces)
        for i, d in pieces:
            g_ref[i] += dot_nn(low_t, d[0])
        g_ref[3] += dot_nn(taken(total[:, edge:].astype(BF), D % 128, rank), n_ref[...])
        return total

    if js[0] == 0:

        @pl.when(j == 0)
        def _():
            o_refs[0][...] = work([(0, dq_ref), (1, dk_ref), (2, dv_ref)])

    if js[-1] > 0:

        @pl.when((j > 0) & ((me ^ j) < me))
        def _():
            t_ref[...] = work([(1, dk_ref), (2, dv_ref)]).astype(BF)

    for i in range(count):
        if js[i] > 0:

            @pl.when(step == i)
            def _(i=i):
                o_refs[i][...] = t_ref[...]


def project(meta, dq, dk, dv, w, m, n_parts, r, js):
    _, L, W = dq.shape
    rank = m.shape[1]
    count = len(js)
    out = pl.pallas_call(
        functools.partial(project_kernel, W=W, js=tuple(js), r=r),
        grid_spec=pltpu.PrefetchScalarGridSpec(
            num_scalar_prefetch=1,
            grid=(count,),
            in_specs=[
                whole_spec(dq.shape),
                pl.BlockSpec((1, L, W), lambda j, _: (0, j + js[0], 0)),
                pl.BlockSpec((1, L, W), lambda j, _: (0, j + js[0], 0)),
                whole_spec(w.shape),
                pl.BlockSpec((1, rank, 3 * W), lambda j, _: (r, 0, 0)),
            ]
            + [pl.BlockSpec((1, L, W), lambda j, _: (r, 0, 0))] * count,
            out_specs=[whole_spec((L, W))] * count + [whole_spec((4, rank, W))],
            scratch_shapes=[pltpu.VMEM((L, W), BF), pltpu.VMEM((L, W), BF), pltpu.VMEM((W, 3 * W), BF)],
        ),
        out_shape=[jax.ShapeDtypeStruct((L, W), BF if j else F32) for j in js]
        + [jax.ShapeDtypeStruct((4, rank, W), F32)],
        compiler_params=pltpu.CompilerParams(vmem_limit_bytes=60 << 20),
        cost_estimate=pl.CostEstimate(
            flops=8 * count * L * W * 2 * W, bytes_accessed=2 * (w.size + 4 * count * L * W), transcendentals=0
        ),
        name="project",
    )(meta, dq, dk, dv, w, m, *[n_parts[j] for j in js])
    return list(out[:count]), out[count]


def norm_kernel(x_ref, dy_ref, gain_ref, shift_ref, e_ref, n_ref, xr_ref, dyr_ref):
    x = x_ref[0].astype(F32)
    centred = x - jnp.mean(x, axis=0, keepdims=True)
    inv = lax.rsqrt(jnp.mean(centred * centred, axis=0, keepdims=True) + EPS)
    n = (centred * inv * gain_ref[...] + shift_ref[...]).astype(BF).T
    low = dot_nt(n, e_ref[0]).astype(BF)
    narrow = place(low, pl.program_id(0) * low.shape[1], n_ref.shape[2] - n.shape[1])
    n_ref[0] = jnp.concatenate([n, narrow], axis=1)
    xr_ref[0] = x_ref[0].T
    dyr_ref[0] = dy_ref[0].T


def first_norm(x_t, dy_t, gain, shift, e_t, W):
    R, D, L = x_t.shape
    col = pl.BlockSpec((1, D, L), lambda r: (r, 0, 0))
    row = pl.BlockSpec((1, L, D), lambda r: (r, 0, 0))
    return pl.pallas_call(
        norm_kernel,
        grid=(R,),
        in_specs=[col, col, whole_spec((D, 1)), whole_spec((D, 1)), pl.BlockSpec((1,) + e_t.shape[1:], lambda r: (r, 0, 0))],
        out_specs=[pl.BlockSpec((1, L, W), lambda r: (r, 0, 0)), row, row],
        out_shape=[jax.ShapeDtypeStruct((R, L, W), BF)] + [jax.ShapeDtypeStruct((R, L, D), BF)] * 2,
        compiler_params=pltpu.CompilerParams(vmem_limit_bytes=48 << 20),
        cost_estimate=pl.CostEstimate(flops=10 * x_t.size, bytes_accessed=10 * x_t.size, transcendentals=0),
        name="first_norm",
    )(x_t, dy_t, gain[:, None], shift[:, None], e_t)


def last_kernel(*refs, count, alias):
    if alias:
        refs = refs[1:]
    terms, (dr_ref, x_ref, gain_ref, e_ref, o_ref) = refs[:count], refs[count:]
    D = x_ref.shape[2]
    dn = terms[0][...]
    for t in terms[1:]:
        dn = dn + t[...].astype(F32)
    edge = D // 128 * 128
    rank = e_ref.shape[1]
    low_t = taken(dn[:, edge:].astype(BF), D % 128, rank)
    dn = dn[:, :D] + lax.dot_general(low_t, e_ref[0], (((0,), (0,)), ((), ())), preferred_element_type=F32)
    z, inv = layer_stats(x_ref[0].astype(F32))
    o_ref[0] = (dr_ref[0] + norm_back(dn * gain_ref[...], z, inv)).astype(BF).T


def last(r, before, terms, dr, x, gain, e_t):
    R, L, D = x.shape
    alias = before is not None
    return pl.pallas_call(
        functools.partial(last_kernel, count=len(terms), alias=alias),
        grid=(1,),
        in_specs=[pl.BlockSpec(memory_space=pl.ANY)] * alias
        + [whole_spec(t.shape) for t in terms]
        + [pl.BlockSpec((1, L, D), lambda i: (r, 0, 0))] * 2
        + [whole_spec((1, D)), pl.BlockSpec((1,) + e_t.shape[1:], lambda i: (r, 0, 0))],
        out_specs=pl.BlockSpec((1, D, L), lambda i: (r, 0, 0)),
        out_shape=jax.ShapeDtypeStruct((R, D, L), BF),
        input_output_aliases={0: 0} if alias else {},
        compiler_params=pltpu.CompilerParams(vmem_limit_bytes=48 << 20),
        cost_estimate=pl.CostEstimate(flops=20 * L * D, bytes_accessed=12 * L * D, transcendentals=0),
        name="last",
    )(*([before] if alias else []), *terms, dr, x, gain, e_t)


def late_kernel(slot_ref, part_ref, *refs, R, parts, D, W):
    g_refs, mix_ref, entry_ref, total = refs[:R], refs[R + 1], refs[R + 2], refs[R + 3]
    total[...] = jnp.zeros_like(total)
    count = g_refs[0].shape[0]
    for r in range(R):

        def one(i, carry):
            a = slot_ref[r * count + i]
            if r + 1 < R:
                total[a] = total[a] + g_refs[r][i].astype(F32)
            else:
                c = part_ref[i]
                total[a, c] = total[a, c] + g_refs[r][i].astype(F32)
            return carry

        lax.fori_loop(0, count, one, 0)
    per = parts // 4
    wide = [jnp.concatenate([total[:, i * per + p] for p in range(per)], axis=-1) for i in range(4)]
    mix_ref[...] = jnp.concatenate([w[:, :, :D] for w in wide[:3]], axis=-1)
    entry_ref[0] = wide[3][:, :, :D]


def late_slots(slot, part, gs, entry, D, W):
    R = len(gs)
    adapters = entry.shape[1]
    _, rank, width = gs[-1].shape
    parts = 4 * W // width
    return pl.pallas_call(
        functools.partial(late_kernel, R=R, parts=parts, D=D, W=W),
        grid_spec=pltpu.PrefetchScalarGridSpec(
            num_scalar_prefetch=2,
            grid=(1,),
            in_specs=[whole_spec(g.shape) for g in gs] + [pl.BlockSpec(memory_space=pl.ANY)],
            out_specs=[
                whole_spec((adapters, rank, 3 * D)),
                pl.BlockSpec((1, adapters, rank, D), lambda i, *_: (0, 0, 0, 0)),
            ],
            scratch_shapes=[pltpu.VMEM((adapters, parts, rank, width), F32)],
        ),
        out_shape=[
            jax.ShapeDtypeStruct((adapters, rank, 3 * D), F32),
            jax.ShapeDtypeStruct(entry.shape, F32),
        ],
        input_output_aliases={2 + R: 1},
        compiler_params=pltpu.CompilerParams(vmem_limit_bytes=60 << 20),
        cost_estimate=pl.CostEstimate(flops=0, bytes_accessed=12 << 20, transcendentals=0),
        name="late_slots",
    )(slot, part, *gs, entry)


def mm(pattern, a, b):
    return jnp.einsum(pattern, a, b, preferred_element_type=F32)


def layer_stats(v):
    middle = jnp.mean(v, axis=-1, keepdims=True)
    centred = v - middle
    inv = lax.rsqrt(jnp.mean(centred * centred, axis=-1, keepdims=True) + EPS)
    return centred * inv, inv


def norm_back(e, z, inv):
    return (e - jnp.mean(e, -1, keepdims=True) - z * jnp.mean(e * z, -1, keepdims=True)) * inv


def swap(x, axis, bit, needed):
    n = lax.axis_size(axis)
    return lax.ppermute(x, axis, [(d ^ bit, d) for d in range(n) if needed(d)])


def blocks_of(x, bits):
    found = {0: x}
    for bit in reversed(bits):
        for j in sorted(found):
            found[j | bit] = swap(found[j], "ctx", bit, lambda d, k=j | bit: (d ^ k) < d)
    return [found[j] for j in sorted(found)]


def block_sum(terms):
    return terms[0] if len(terms) == 1 else sum(t.astype(F32) for t in terms).astype(BF)


def blocks_back(held, bit):
    held = dict(held)
    for j in sorted(held):
        if j & bit:
            sent = block_sum(held.pop(j))
            got = swap(sent, "ctx", bit, lambda d, k=j, b=bit: ((d ^ b) ^ k) < (d ^ b))
            held[j ^ bit] = held[j ^ bit] + [got]
    return held


def turned_order(bits):
    count = 2 * bits[-1]
    return sorted(range(count), key=lambda c: [c & b for b in bits])


def ctx_sum_stage(g, bit):
    n = lax.axis_size("ctx")
    half = g.shape[0] // 2
    mine = (lax.axis_index("ctx") & bit) != 0
    low, high = g[:half], g[half:]
    got = lax.ppermute(jnp.where(mine, low, high), "ctx", [(d, d ^ bit) for d in range(n)])
    return jnp.where(mine, high, low) + got


def gather_all(x, seq_count, ctx_count, at, beside):
    n = seq_count * ctx_count
    seq_bits = [ctx_count << i for i in range(seq_count.bit_length() - 1)]
    ctx_bits = [1 << i for i in range(ctx_count.bit_length() - 1)]
    steps = seq_bits[::-1] + ctx_bits[::-1]
    held, order, beside = x[None], [0], list(beside)
    for i, bit in enumerate(steps):
        k = i - at
        if 0 <= k < len(beside):
            if callable(beside[k]):
                beside[k] = beside[k](beside[k - 1])
            held, beside[k] = lax.optimization_barrier((held, beside[k]))
        got = lax.ppermute(held, BOTH, [(d, d ^ bit) for d in range(n)])
        held = jnp.concatenate([held, got], 0)
        order = order + [o ^ bit for o in order]
    return held, order, beside


def slots_kernel(index_ref, g_ref, *refs, count, spans):
    outs, total = refs[:-1], refs[-1]
    total[...] = jnp.zeros_like(total)

    def one(i, carry):
        a = index_ref[i]
        total[a] = total[a] + g_ref[i].astype(F32)
        return carry

    lax.fori_loop(0, count, one, 0)
    for out, layers in zip(outs, spans):
        for i, pieces in enumerate(layers):
            parts = [total[:, :, first : first + width] for first, width in pieces]
            if parts:
                out[i] = parts[0] if len(parts) == 1 else jnp.concatenate(parts, axis=-1)


def to_slots(index, g, adapters, spans):
    count, rank, wide = g.shape
    rows = 8
    shapes = [(len(layers), adapters, rank, sum(w for _, w in layers[-1])) for layers in spans]
    return pl.pallas_call(
        functools.partial(slots_kernel, count=count, spans=spans),
        grid_spec=pltpu.PrefetchScalarGridSpec(
            num_scalar_prefetch=1,
            grid=(rank // rows,),
            in_specs=[pl.BlockSpec((count, rows, wide), lambda i, m: (0, i, 0))],
            out_specs=[pl.BlockSpec(s[:2] + (rows, s[3]), lambda i, m: (0, 0, i, 0)) for s in shapes],
            scratch_shapes=[pltpu.VMEM((adapters, rows, wide), F32)],
        ),
        out_shape=[jax.ShapeDtypeStruct(s, F32) for s in shapes],
        compiler_params=pltpu.CompilerParams(vmem_limit_bytes=48 << 20),
        cost_estimate=pl.CostEstimate(
            flops=count * rank * wide, bytes_accessed=count * rank * wide * 2 + adapters * rank * wide * 4, transcendentals=0
        ),
        name="to_slots",
    )(index, g)


def per_device(
    tokens, segments, adapter_index, norm_gains, norm_shifts, head_biases, expand_bias, exit_biases,
    mixing_weight, output_weight, expand_weight, shrink_weight,
    entry_adapters, mixing_adapters, expand_adapters, hidden_adapters, exit_adapters, cotangent,
):
    micro, seqs, L, D = tokens.shape
    R = micro * seqs
    adapters, rank = mixing_adapters.shape[:2]
    FF = expand_bias.shape[0]
    C = lax.axis_size("ctx")
    S = lax.axis_size("seq")
    bits = [1 << i for i in range(C.bit_length() - 1)]
    me = lax.axis_index("ctx")
    T = C * L
    W = -(-D // 128) * 128
    pad = W - D

    flip = lambda m: jnp.swapaxes(m, -1, -2)
    rows = mixing_weight.shape[0]
    cm, co, ce = mixing_weight.shape[1], output_weight.shape[1], expand_weight.shape[1]
    first = jnp.concatenate([mixing_weight, output_weight], 1)
    first = jnp.concatenate([first[: rows // 2], first[rows // 2 :]], 1)
    main = ce // 128 * 128
    rem = ce - main
    per = S // C
    shr_t = shrink_weight.T.reshape(co, per, ce).transpose(1, 0, 2)
    wide = first.shape[1]
    folded = lambda m: jnp.pad(
        m.reshape(-1, 8, m.shape[1]).transpose(1, 0, 2).reshape(8, -1), ((0, 0), (0, wide - m.size // 8))
    )
    rest = [folded(expand_weight[:, main:].T), folded(flip(shr_t[:, :, main:]).reshape(per * rem, co))]
    rest = jnp.concatenate(rest, 0)
    first = jnp.concatenate([first, rest], 0)
    second = jnp.concatenate([expand_weight[:, :main], shr_t[:, :, :main].reshape(per * co, main)], 0)
    g1 = lax.all_gather(first, BOTH)
    g2 = lax.all_gather(second, BOTH).reshape(S, C, -1, main)
    w_mix, w_out, r_exp, r_shr = unpack(g1, S, C, rows // 2, cm, co, D, W, rem, per)
    if rows % 16 == 0 and per * co == rows and co % 8 == 0:
        w_exp = w_shr = g2
    else:
        w_exp = g2[:, :, :rows].reshape(S, D, main)
        w_shr = g2[:, :, rows:].reshape(S, C, per, co, main).transpose(1, 2, 0, 3, 4).reshape(S, D, main)

    def split_ff(m):
        m = m.reshape(m.shape[:-1] + (S, ce))
        return m[..., :main].reshape(m.shape[:-2] + (S * main,)), m[..., main:].reshape(m.shape[:-2] + (S * rem,))

    index = adapter_index.reshape(R)
    take = lambda table, axis: jnp.stack(
        [lax.dynamic_index_in_dim(table, index[r], axis, keepdims=False) for r in range(R)], axis
    )
    entry = take(entry_adapters, 1)
    mix_up = take(mixing_adapters, 0)
    exp_up = take(expand_adapters, 0)
    hid = take(hidden_adapters, 0)
    exit_up = take(exit_adapters, 1)
    pad_heads = lambda m: jnp.concatenate([padded(m[..., i * D : (i + 1) * D]) for i in range(3)], -1)
    padded = lambda m: jnp.pad(m, [(0, 0)] * (m.ndim - 1) + [(0, pad)])
    mix_up = pad_heads(mix_up)
    entry_t = flip(entry)
    exp_main, exp_rest = split_ff(exp_up)
    hid_main, hid_rest = split_ff(flip(hid))
    bias_main, bias_rest = split_ff(expand_bias[None])
    head_bias = pad_heads(jnp.concatenate([head_biases[0], jnp.zeros_like(head_biases[0]), head_biases[1]])[None])

    seg = segments.reshape(R, L)
    seg_blocks = blocks_of(seg, bits)
    first_block = me * jnp.ones((R,), jnp.int32)
    for j, other in enumerate(seg_blocks):
        reached = ((me ^ j) <= me) & jnp.any(other == seg[:, :1], axis=1)
        first_block = jnp.where(reached, jnp.minimum(first_block, me ^ j), first_block)
    meta = jnp.concatenate([me[None], first_block]).astype(jnp.int32)
    qa, ka = document_lanes(seg, jnp.concatenate(seg_blocks, 1))

    n1, x, dy = first_norm(
        flip(tokens.reshape(R, L, D)), flip(cotangent.reshape(R, L, D)), norm_gains[0], norm_shifts[0],
        entry_t[0], W,
    )
    n1_parts = blocks_of(n1, bits)
    q, k, v = qkv(meta, n1_parts, w_mix, mix_up, head_bias)
    o, extra = attn_fwd(meta, q, k, v, qa, ka, D)

    res, na, da, lo = mid(
        o, x, dy, w_out, entry_t[1], entry_t[2], exit_up[0], exit_up[1], norm_gains[1][None], norm_shifts[1][None],
        exit_biases[0][None], W,
    )
    y, dr, do, g1, g2_, gx0, gx1, ge, ger, gh, ghr = ffn(
        na.reshape(R * L, W), da.reshape(R * L, W), res, o, lo, w_exp, w_shr, r_exp, r_shr,
        exp_main, exp_rest, hid_main, hid_rest, bias_main, bias_rest,
        exit_up[0], exit_up[1], entry_t[1], entry_t[2], w_out, norm_gains[1][None], exit_biases[1][None],
    )
    layer_output = flip(y).reshape(tokens.shape)

    number = jnp.broadcast_to((index.astype(F32) / C)[:, None, None], (R, rank, 128))
    early = jnp.concatenate([g1, g2_, gx0, gx1, ge, ger, gh, ghr, number], -1).reshape(R * rank, -1)
    swapped = turned_order(bits)
    share = R * rank // C
    early = jnp.concatenate([early[c * share : (c + 1) * share] for c in swapped], 0)

    pairs = W // 128
    ka_t = flip(ka)
    late, terms, held = [], [], None
    everything = list(range(C))
    for r in range(R):
        grads = ()
        cuts = [i * pairs // (len(bits) if held is None else 2) for i in range(len(bits) + 1 if held is None else 3)]
        for i, (p0, p1) in enumerate(zip(cuts, cuts[1:])):
            grads = attn_bwd(meta, q, k, v, do, o, extra, ka_t, r, p0, p1 - p0, grads)
            if held is None:
                early = ctx_sum_stage(early, bits[i])
                if i + 1 < len(bits):
                    do, early = lax.optimization_barrier((do, early))
            if held is not None and i == 0:
                held = blocks_back(held, bits[0])
                held = {j: [block_sum(t)] if j else t for j, t in held.items()}
                do, held = lax.optimization_barrier((do, held))
                for bit in bits[1:]:
                    held = blocks_back(held, bit)
        dq, dk, dv = grads
        if held is None:
            dk, early = lax.optimization_barrier((dk, early))
            early = lax.all_gather(early.astype(BF), BOTH).reshape(S * R, rank, -1)
        if held is not None:
            dk, held = lax.optimization_barrier((dk, held))
            terms.append(held[0])
        if r + 1 < R:
            parts, g = project(meta, dq, dk, dv, w_mix, mix_up, n1_parts, r, everything)
            held = {j: [p] for j, p in enumerate(parts)}
            do, held = lax.optimization_barrier((do, held))
        else:
            parts, g = project(meta, dq, dk, dv, w_mix, mix_up, n1_parts, r, everything[1:])
            dq, parts = lax.optimization_barrier((dq, parts))
            own, g_own = project(meta, dq, dk, dv, w_mix, mix_up, n1_parts, r, [0])
            g = g + g_own
            held = {j: [p] for j, p in enumerate(own + parts)}
            held = blocks_back(held, bits[0])
            held = {j: [block_sum(t)] if j else t for j, t in held.items()}
        g = g.reshape(4, rank, C // 4, -1).transpose(0, 2, 1, 3).reshape(C, rank, -1)
        if r + 1 < R:
            late.append(lax.all_gather(g.astype(BF), BOTH))
        else:
            g = jnp.concatenate([g[c : c + 1] for c in swapped], 0)
            for bit in bits:
                g = ctx_sum_stage(g, bit)
            g, held = lax.optimization_barrier((g, held))
            for bit in bits[1:]:
                held = blocks_back(held, bit)
            terms.append(held[0])
            grad_of = lambda i, before: last(i, before, terms[i], dr, x, norm_gains[0][None], entry_t[0])
            input_grad = None
            for i in range(R - 1):
                input_grad = grad_of(i, input_grad)
            all_index = early[:, 0, -1].astype(jnp.int32)
            both = []
            for at in (4 * D, 4 * D + FF):
                both.append([p for i in range(S) for p in ((at + i * main, main), (at + S * main + i * rem, rem))])
            entry_g, exit_g, expand_g, hidden_g = to_slots(
                all_index, early, adapters,
                [[[], [(0, D)], [(D, D)]], [[(2 * D, D)], [(3 * D, D)]], [both[0]], [both[1]]],
            )
            early_g = (entry_g, exit_g, expand_g, hidden_g)
            before = early_g if input_grad is None else (*early_g, input_grad)
            last_late, order, beside = gather_all(
                g[0].astype(BF), S, C, S.bit_length() - 1,
                [before, lambda done: grad_of(r, done[4] if len(done) > 4 else None)],
            )
            entry_g, exit_g, expand_g, hidden_g = beside[0][:4]
            input_grad = beside[1]
            late.append(last_late)
    device = lax.axis_index("seq") * C + me
    order = device ^ jnp.array(order, jnp.int32)
    by_row = all_index.reshape(S, R)
    slot = [jnp.repeat(by_row[:, r], C) for r in range(R - 1)]
    slot.append(jnp.sum(jnp.where((order // C)[:, None] == jnp.arange(S), by_row[:, R - 1], 0), 1))
    mixing_g, entry_g = late_slots(jnp.concatenate(slot), order % C, late, entry_g, D, W)
    input_grad = flip(input_grad).reshape(tokens.shape)

    return (
        layer_output,
        input_grad,
        flip(entry_g),
        mixing_g,
        expand_g[0],
        flip(hidden_g[0]),
        exit_g,
    )


def solution(mesh):
    rows = P(None, "seq", "ctx", None)
    weight = P("ctx", "seq")
    in_specs = (
        (rows, P(None, "seq", "ctx"), P(None, "seq")) + (P(),) * 5 + (weight,) * 4 + (P(),) * 5 + (rows,)
    )
    out_specs = (rows, rows) + (P(),) * 5
    return jax.shard_map(per_device, mesh=mesh, in_specs=in_specs, out_specs=out_specs, check_vma=False)
```

```python
import functools

import jax
import jax.numpy as jnp
from jax import lax
from jax.experimental import pallas as pl
from jax.experimental.pallas import tpu as pltpu
from jax.sharding import PartitionSpec as P

HEADS = 17
EPS = 1e-05
NEG = -1e30
BF = jnp.bfloat16
F32 = jnp.float32
BOTH = ("seq", "ctx")


FAR = -1e30


def product(a, b, ca, cb):
    return lax.dot_general(a, b, (((ca,), (cb,)), ((), ())), preferred_element_type=F32)


def thirds(x):
    a = x.astype(BF)
    b = (x - a.astype(F32)).astype(BF)
    c = (x - a.astype(F32) - b.astype(F32)).astype(BF)
    return a, b, c


def lanes_of(h, lane):
    return (lane < 64) if h == 0 else (lane >= 64)


def attn_fwd_kernel(
    meta_ref, q_ref, k_ref, v_ref, qa_ref, ka_ref, o_ref, a_ref, kh_ref, vt_ref, s_ref, acc_ref, st_ref, *, L
):
    r = pl.program_id(0)
    me = meta_ref[0]
    lo = meta_ref[1 + r]
    lane = lax.broadcasted_iota(jnp.int32, (1, 128), 1)
    vt_ref[...] = v_ref[0].T
    q2, qa = q_ref[0], qa_ref[0]
    qh = [jnp.where(lanes_of(h, lane), q2, qa).T for h in range(2)]
    for h in range(2):
        kh_ref[h] = jnp.where(lanes_of(h, lane), k_ref[0], ka_ref[0])
        st_ref[h] = jnp.concatenate([jnp.full((1, L), NEG, F32), jnp.zeros((7, L), F32)], axis=0)
    acc_ref[...] = jnp.zeros_like(acc_ref)

    def at(t):
        return pl.multiple_of((t ^ me) * L, L)

    def scores(t, h):
        s_ref[h] = product(kh_ref[h, pl.ds(at(t), L), :], qh[h], 1, 0)

    def gather(t, h, diagonal):
        s = s_ref[h]
        if diagonal:
            ok = lax.broadcasted_iota(jnp.int32, (L, L), 0) <= lax.broadcasted_iota(jnp.int32, (L, L), 1)
            s = jnp.where(ok, s, NEG)
        m = st_ref[h, 0:1]
        new = jnp.maximum(m, jnp.max(s, axis=0, keepdims=True))
        scale = jnp.exp(m - new)
        p = jnp.exp(s - new)
        st_ref[h, 1:2] = st_ref[h, 1:2] * scale + jnp.sum(p, axis=0, keepdims=True)
        st_ref[h, 0:1] = new
        rows = slice(h * 64, (h + 1) * 64)
        acc_ref[rows] = acc_ref[rows] * scale + product(vt_ref[rows, pl.ds(at(t), L)], p.astype(BF), 1, 0)

    def triangle(h):
        H = L // 2
        ok = lax.broadcasted_iota(jnp.int32, (H, H), 0) <= lax.broadcasted_iota(jnp.int32, (H, H), 1)
        s00 = jnp.where(ok, s_ref[h, :H, :H], NEG)
        s01 = s_ref[h, :H, H:]
        s11 = jnp.where(ok, s_ref[h, H:, H:], NEG)
        top = lambda s: jnp.max(s, axis=0, keepdims=True)
        add = lambda p: jnp.sum(p, axis=0, keepdims=True)
        m = st_ref[h, 0:1]
        new = jnp.maximum(m, jnp.concatenate([top(s00), jnp.maximum(top(s01), top(s11))], axis=1))
        scale = jnp.exp(m - new)
        p00 = jnp.exp(s00 - new[:, :H])
        p01 = jnp.exp(s01 - new[:, H:])
        p11 = jnp.exp(s11 - new[:, H:])
        st_ref[h, 1:2] = st_ref[h, 1:2] * scale + jnp.concatenate([add(p00), add(p01) + add(p11)], axis=1)
        st_ref[h, 0:1] = new
        rows = slice(h * 64, (h + 1) * 64)
        first, second = vt_ref[rows, :H], vt_ref[rows, H:L]
        left = product(first, p00.astype(BF), 1, 0)
        right = product(first, p01.astype(BF), 1, 0) + product(second, p11.astype(BF), 1, 0)
        acc_ref[rows, :H] = acc_ref[rows, :H] * scale[:, :H] + left
        acc_ref[rows, H:] = acc_ref[rows, H:] * scale[:, H:] + right

    scores(lo, 0)

    def body(t, carry):
        scores(t, 1)
        gather(t, 0, False)
        scores(t + 1, 0)
        gather(t, 1, False)
        return carry

    lax.fori_loop(lo, me, body, 0)
    scores(me, 1)
    for h in range(2):
        if L % 256 == 0:
            triangle(h)
        else:
            gather(me, h, True)
    rows = []
    for h in range(2):
        total = st_ref[h, 1:2]
        sl = slice(h * 64, (h + 1) * 64)
        acc_ref[sl] = acc_ref[sl] / total
        rows.append(thirds(-(st_ref[h, 0:1] + jnp.log(total))))
    o_ref[0] = acc_ref[...].astype(BF).T
    sub = lax.broadcasted_iota(jnp.int32, (128, 1), 0)
    extra = jnp.zeros((128, L), F32)
    for h in range(2):
        for i in range(3):
            extra = jnp.where(sub == (1 - h) * 64 + 8 + i, rows[h][i].astype(F32), extra)
    a_ref[0, 0] = qa + extra.astype(BF).T


def attn_fwd(meta, q, k, v, qa, ka, D):
    R, L, W = q.shape
    T = k.shape[1]
    NP = W // 128
    col = lambda r, p, m: (r, 0, p)
    one = lambda r, p, m: (r, 0, 0)
    return pl.pallas_call(
        functools.partial(attn_fwd_kernel, L=L),
        grid_spec=pltpu.PrefetchScalarGridSpec(
            num_scalar_prefetch=1,
            grid=(R, NP),
            in_specs=[
                pl.BlockSpec((1, L, 128), col),
                pl.BlockSpec((1, T, 128), col),
                pl.BlockSpec((1, T, 128), col),
                pl.BlockSpec((1, L, 128), one),
                pl.BlockSpec((1, T, 128), one),
            ],
            out_specs=[pl.BlockSpec((1, L, 128), col), pl.BlockSpec((1, 1, L, 128), lambda r, p, m: (r, p, 0, 0))],
            scratch_shapes=[
                pltpu.VMEM((2, T, 128), BF),
                pltpu.VMEM((128, T), BF),
                pltpu.VMEM((2, L, L), F32),
                pltpu.VMEM((128, L), F32),
                pltpu.VMEM((2, 8, L), F32),
            ],
        ),
        out_shape=[jax.ShapeDtypeStruct((R, L, D), BF), jax.ShapeDtypeStruct((R, NP, L, 128), BF)],
        compiler_params=pltpu.CompilerParams(vmem_limit_bytes=48 << 20),
        cost_estimate=pl.CostEstimate(
            flops=R * 40 * L * T * W, bytes_accessed=R * (2 * L + 2 * T) * W * 2, transcendentals=R * L * T * 18
        ),
        name="attn_fwd",
    )(meta, q, k, v, qa, ka)


def attn_bwd_kernel(
    meta_ref, q_ref, k_ref, v_ref, do_ref, o_ref, a_ref, ka_ref, *refs, L, r0, D, first,
):
    dq_ref, dk_ref, dv_ref, kh_ref, vh_ref, kt_ref, s_ref, dp_ref, dqt_ref, dkt_ref, dvt_ref = refs[-11:]
    me = meta_ref[0]
    lo = meta_ref[1 + r0]
    lane = lax.broadcasted_iota(jnp.int32, (1, 128), 1)
    row = lax.broadcasted_iota(jnp.int32, (128, 1), 0)
    limit = D - (pl.program_id(0) + first) * 128
    ones = jnp.where((row % 64 >= 8) & (row % 64 < 11), 1.0, 0.0).astype(BF)
    do2 = jnp.where(lane < limit, do_ref[0], jnp.zeros((), BF))
    o2 = jnp.where(lane < limit, o_ref[0], jnp.zeros((), BF))
    q2 = q_ref[0]
    prod = do2.astype(F32) * o2.astype(F32)
    qh, dh = [], []
    for h in range(2):
        mine = lanes_of(h, lane)
        parts = thirds(-jnp.sum(jnp.where(mine, prod, 0.0), axis=1, keepdims=True))
        extra = jnp.zeros((1, 128), BF)
        for i in range(3):
            extra = jnp.where(lane == (1 - h) * 64 + 8 + i, parts[i], extra)
        dh.append(jnp.where(mine, do2, extra))
        qh.append(jnp.where(mine, q2, a_ref[0, 0]))
    qt, dot_ = q2.T, do2.T
    dqt_ref[...] = jnp.zeros_like(dqt_ref)

    def at(t):
        return pl.multiple_of((t ^ me) * L, L)

    def turn(t):
        here = pl.ds(at(t), L)
        kt = k_ref[0, here, :].T
        vt = v_ref[0, here, :].T
        kt_ref[:, here] = kt
        for h in range(2):
            kh_ref[h, :, here] = jnp.where(lanes_of(h, row), kt, ka_ref[0, :, here])
            vh_ref[h, :, here] = jnp.where(lanes_of(h, row), vt, ones)

    def scores(t, h):
        here = pl.ds(at(t), L)
        s_ref[h] = product(qh[h], kh_ref[h, :, here], 1, 0)
        dp_ref[h] = product(dh[h], vh_ref[h, :, here], 1, 0)

    def gather(t, h, diagonal):
        p = jnp.exp(s_ref[h])
        if diagonal:
            ok = lax.broadcasted_iota(jnp.int32, (L, L), 1) <= lax.broadcasted_iota(jnp.int32, (L, L), 0)
            p = jnp.where(ok, p, 0.0)
        ds = (p * dp_ref[h]).astype(BF)
        rows = slice(h * 64, (h + 1) * 64)
        dvt_ref[rows] = product(dot_[rows], p.astype(BF), 1, 0)
        dkt_ref[rows] = product(qt[rows], ds, 1, 0)
        dqt_ref[rows] += product(kt_ref[rows, pl.ds(at(t), L)], ds, 1, 1)

    def triangle(h):
        H = L // 2
        ok = lax.broadcasted_iota(jnp.int32, (H, H), 1) <= lax.broadcasted_iota(jnp.int32, (H, H), 0)
        p00 = jnp.where(ok, jnp.exp(s_ref[h, :H, :H]), 0.0)
        p10 = jnp.exp(s_ref[h, H:, :H])
        p11 = jnp.where(ok, jnp.exp(s_ref[h, H:, H:]), 0.0)
        ds00 = (p00 * dp_ref[h, :H, :H]).astype(BF)
        ds10 = (p10 * dp_ref[h, H:, :H]).astype(BF)
        ds11 = (p11 * dp_ref[h, H:, H:]).astype(BF)
        rows = slice(h * 64, (h + 1) * 64)
        do_h, q_h, k_h = dot_[rows], qt[rows], kt_ref[rows, :L]
        dvt_ref[rows, :H] = product(do_h[:, :H], p00.astype(BF), 1, 0) + product(do_h[:, H:], p10.astype(BF), 1, 0)
        dvt_ref[rows, H:] = product(do_h[:, H:], p11.astype(BF), 1, 0)
        dkt_ref[rows, :H] = product(q_h[:, :H], ds00, 1, 0) + product(q_h[:, H:], ds10, 1, 0)
        dkt_ref[rows, H:] = product(q_h[:, H:], ds11, 1, 0)
        dqt_ref[rows, :H] += product(k_h[:, :H], ds00, 1, 1)
        dqt_ref[rows, H:] += product(k_h[:, :H], ds10, 1, 1) + product(k_h[:, H:], ds11, 1, 1)

    def store(t):
        here = pl.ds(at(t), L)
        dk_ref[0, here, :] = dkt_ref[...].astype(BF).T
        dv_ref[0, here, :] = dvt_ref[...].astype(BF).T

    def none(t, carry):
        dk_ref[0, pl.ds(at(t), L), :] = jnp.zeros((L, 128), BF)
        dv_ref[0, pl.ds(at(t), L), :] = jnp.zeros((L, 128), BF)
        return carry

    lax.fori_loop(0, lo, none, 0)
    turn(lo)
    scores(lo, 0)

    def body(t, carry):
        scores(t, 1)
        turn(t + 1)
        gather(t, 0, False)
        scores(t + 1, 0)
        gather(t, 1, False)
        store(t)
        return carry

    lax.fori_loop(lo, me, body, 0)
    scores(me, 1)
    for h in range(2):
        if L % 256 == 0:
            triangle(h)
        else:
            gather(me, h, True)
    store(me)
    dq_ref[0] = dqt_ref[...].astype(BF).T * jnp.asarray(0.125, BF)


def attn_bwd(meta, q, k, v, do, o, extra, ka_t, r0, first, count, before=()):
    R, L, W = q.shape
    T, D = k.shape[1], do.shape[2]
    col = lambda p, m: (r0, 0, p + first)
    out = lambda p, m: (0, 0, p + first)
    return pl.pallas_call(
        functools.partial(attn_bwd_kernel, L=L, r0=r0, D=D, first=first),
        grid_spec=pltpu.PrefetchScalarGridSpec(
            num_scalar_prefetch=1,
            grid=(count,),
            in_specs=[
                pl.BlockSpec((1, L, 128), col),
                pl.BlockSpec((1, T, 128), col),
                pl.BlockSpec((1, T, 128), col),
                pl.BlockSpec((1, L, 128), col),
                pl.BlockSpec((1, L, 128), col),
                pl.BlockSpec((1, 1, L, 128), lambda p, m: (r0, p + first, 0, 0)),
                pl.BlockSpec((1, 128, T), lambda p, m: (r0, 0, 0)),
            ]
            + [pl.BlockSpec(memory_space=pl.ANY) for _ in before],
            out_specs=[pl.BlockSpec((1, L, 128), out), pl.BlockSpec((1, T, 128), out), pl.BlockSpec((1, T, 128), out)],
            scratch_shapes=[
                pltpu.VMEM((2, 128, T), BF),
                pltpu.VMEM((2, 128, T), BF),
                pltpu.VMEM((128, T), BF),
                pltpu.VMEM((2, L, L), F32),
                pltpu.VMEM((2, L, L), F32),
                pltpu.VMEM((128, L), F32),
                pltpu.VMEM((128, L), F32),
                pltpu.VMEM((128, L), F32),
            ],
        ),
        out_shape=[
            jax.ShapeDtypeStruct((1, L, W), BF),
            jax.ShapeDtypeStruct((1, T, W), BF),
            jax.ShapeDtypeStruct((1, T, W), BF),
        ],
        compiler_params=pltpu.CompilerParams(vmem_limit_bytes=48 << 20),
        input_output_aliases={8 + i: i for i in range(len(before))},
        cost_estimate=pl.CostEstimate(
            flops=60 * L * T * 128 * count, bytes_accessed=(3 * L + 4 * T) * 256 * count, transcendentals=L * T * 2 * count
        ),
        name="attn_bwd",
    )(meta, q, k, v, do, o, extra, ka_t, *before)


def document_lanes(seg_q, seg_k):
    number = jnp.arange(64, dtype=jnp.int32)
    two = lambda m: jnp.concatenate([m, m], -1).astype(BF)
    qa = jnp.where((number < 8) & (number != seg_q[..., None]), FAR, 0.0)
    ka = jnp.where((number == seg_k[..., None]) | ((number >= 8) & (number < 11)), 1.0, 0.0)
    return two(qa), two(ka)


def dot_nn(a, b):
    return lax.dot_general(a, b, (((1,), (0,)), ((), ())), preferred_element_type=F32)


def dot_nt(a, b):
    return lax.dot_general(a, b, (((1,), (1,)), ((), ())), preferred_element_type=F32)


def turned(x):
    rank = x.shape[1]
    eye = (
        lax.broadcasted_iota(jnp.int32, (rank, rank), 0) == lax.broadcasted_iota(jnp.int32, (rank, rank), 1)
    ).astype(F32).astype(BF)
    return dot_nt(eye, x).astype(BF)


def place(x, first, width):
    rank = x.shape[1]
    to = lax.broadcasted_iota(jnp.int32, (rank, width), 1) == lax.broadcasted_iota(jnp.int32, (rank, width), 0) + first
    return dot_nn(x, to.astype(F32).astype(BF)).astype(BF)


def taken(x, first, rank):
    width = x.shape[1]
    to = lax.broadcasted_iota(jnp.int32, (rank, width), 1) == lax.broadcasted_iota(jnp.int32, (rank, width), 0) + first
    return dot_nt(to.astype(F32).astype(BF), x).astype(BF)


def whole_spec(shape, **kw):
    return pl.BlockSpec(shape, lambda *_: (0,) * len(shape), pipeline_mode=pl.Buffered(1))


def unpack_kernel(g_ref, mix_ref, out_ref, rexp_ref, rshr_ref, *, cm, co, D, W, rem, per):
    S = g_ref.shape[0]
    rows = mix_ref.shape[2]
    half_width = cm + co
    for half in range(2):
        at = half * half_width
        mix = jnp.concatenate([g_ref[s, 0, :rows, at : at + cm] for s in range(S)], axis=1)
        out = jnp.concatenate([g_ref[s, 0, :rows, at + cm : at + half_width] for s in range(S)], axis=1)
        zero = jnp.zeros((mix.shape[0], W - D), mix.dtype)
        for i in range(3):
            mix_ref[0, half, :, i * W : (i + 1) * W] = jnp.concatenate([mix[:, i * D : (i + 1) * D], zero], axis=1)
        out_ref[0, half] = out
    for s in range(S):
        for i in range(rem // 8):
            rexp_ref[0, s * rem + i * 8 : s * rem + i * 8 + 8] = g_ref[
                s, 0, rows : rows + 8, i * 2 * rows : (i + 1) * 2 * rows
            ]
    for i in range(per * rem // 8):
        rshr_ref[0, i * 8 : i * 8 + 8] = jnp.concatenate(
            [g_ref[s, 0, rows + 8 : rows + 16, i * co : (i + 1) * co] for s in range(S)], axis=1
        )


def unpack(g, S, C, rows2, cm, co, D, W, rem, per):
    g = g.reshape(S, C, -1, 2 * (cm + co))
    shapes = [(C, 2, rows2, 3 * W), (C, 2, rows2, D), (C, S * rem, 2 * rows2), (C, per * rem, D)]
    mix, out, rexp, rshr = pl.pallas_call(
        functools.partial(unpack_kernel, cm=cm, co=co, D=D, W=W, rem=rem, per=per),
        grid=(C,),
        in_specs=[pl.BlockSpec((S, 1) + g.shape[2:], lambda c: (0, c, 0, 0))],
        out_specs=[pl.BlockSpec((1,) + s[1:], lambda c, n=len(s): (c,) + (0,) * (n - 1)) for s in shapes],
        out_shape=[jax.ShapeDtypeStruct(s, BF) for s in shapes],
        compiler_params=pltpu.CompilerParams(vmem_limit_bytes=48 << 20),
        cost_estimate=pl.CostEstimate(flops=0, bytes_accessed=4 * g.size, transcendentals=0),
        name="unpack",
    )(g)
    return mix.reshape(D, 3 * W), out.reshape(D, D), rexp, rshr.reshape(C * per * rem, D)


def qkv_kernel(meta_ref, *refs, count, W, R):
    n_refs = refs[:count]
    w_ref, m_ref, b_ref, q_ref, k_ref, v_ref, n_ref, wa_ref = refs[count:]
    j = pl.program_id(0)
    me = meta_ref[0]
    D = w_ref.shape[0]
    rank = m_ref.shape[1]
    for jj in range(count):

        @pl.when(j == jj)
        def _(jj=jj):
            n_ref[...] = n_refs[jj][...].reshape(n_ref.shape)

    @pl.when(j == 0)
    def _():
        wa_ref[:D] = w_ref[...]
        for r in range(R):
            wa_ref[D + r * rank : D + (r + 1) * rank] = m_ref[r]
        wa_ref[D + R * rank :] = jnp.zeros((W - D - R * rank, 3 * W), BF)

    def part(i):
        s = slice(i * W, (i + 1) * W)
        return (dot_nn(n_ref[...], wa_ref[:, s]) + b_ref[:, s]).reshape(R, -1, W)

    @pl.when(j == 0)
    def _():
        q_ref[...] = (part(0) * 0.125).astype(BF)

    @pl.when((me ^ j) <= me)
    def _():
        k_ref[...] = part(1).astype(BF)
        v_ref[...] = part(2).astype(BF)


def qkv(meta, n_parts, w, m, b):
    count = len(n_parts)
    R, L, W = n_parts[0].shape
    T = count * L
    row = pl.BlockSpec((R, L, W), lambda j, _: (0, j, 0))
    return pl.pallas_call(
        functools.partial(qkv_kernel, W=W, count=count, R=R),
        grid_spec=pltpu.PrefetchScalarGridSpec(
            num_scalar_prefetch=1,
            grid=(count,),
            in_specs=[whole_spec(x.shape) for x in (*n_parts, w, m, b)],
            out_specs=[whole_spec((R, L, W)), row, row],
            scratch_shapes=[pltpu.VMEM((R * L, W), BF), pltpu.VMEM((W, 3 * W), BF)],
        ),
        out_shape=[
            jax.ShapeDtypeStruct((R, L, W), BF),
            jax.ShapeDtypeStruct((R, T, W), BF),
            jax.ShapeDtypeStruct((R, T, W), BF),
        ],
        compiler_params=pltpu.CompilerParams(vmem_limit_bytes=60 << 20),
        cost_estimate=pl.CostEstimate(
            flops=4 * R * T * W * 2 * W, bytes_accessed=2 * (R * T * W + w.size + 2 * R * T * W), transcendentals=0
        ),
        name="qkv",
    )(meta, *n_parts, w, m, b)


def mid_kernel(
    o_ref, x_ref, dy_ref, wout_ref, e1_ref, e2_ref, x0_ref, x1_ref, gain_ref, shift_ref, xb_ref,
    res_ref, na_ref, da_ref, lo_ref,
):
    r = pl.program_id(0)
    D, W = o_ref.shape[2], na_ref.shape[2]
    rank = e1_ref.shape[1]
    o, dy = o_ref[0], dy_ref[0]
    lo = dot_nt(o, e1_ref[0]).astype(BF)
    lo_ref[0] = lo
    res = x_ref[0].astype(F32) + dot_nn(o, wout_ref[...]) + dot_nn(lo, x0_ref[0]) + xb_ref[...]
    res_ref[0] = res
    z, _ = layer_stats(res)
    n2 = (z * gain_ref[...] + shift_ref[...]).astype(BF)
    l3 = dot_nt(n2, e2_ref[0]).astype(BF)
    na_ref[0] = jnp.concatenate([n2, place(l3, r * rank, W - D)], axis=1)
    dl4 = dot_nt(dy, x1_ref[0]).astype(BF)
    da_ref[0] = jnp.concatenate([dy, place(dl4, r * rank, W - D)], axis=1)


def mid(o, x, dy, wout, e1, e2, x0, x1, gain, shift, xb, W):
    R, L, D = o.shape
    rank = e1.shape[1]
    row = pl.BlockSpec((1, L, D), lambda r: (r, 0, 0))
    wide = pl.BlockSpec((1, L, W), lambda r: (r, 0, 0))
    small = pl.BlockSpec((1, rank, D), lambda r: (r, 0, 0))
    return pl.pallas_call(
        mid_kernel,
        grid=(R,),
        in_specs=[row] * 3 + [whole_spec(wout.shape)] + [small] * 4 + [whole_spec((1, D))] * 3,
        out_specs=[row, wide, wide, pl.BlockSpec((1, L, rank), lambda r: (r, 0, 0))],
        out_shape=[
            jax.ShapeDtypeStruct((R, L, D), F32),
            jax.ShapeDtypeStruct((R, L, W), BF),
            jax.ShapeDtypeStruct((R, L, W), BF),
            jax.ShapeDtypeStruct((R, L, rank), BF),
        ],
        compiler_params=pltpu.CompilerParams(vmem_limit_bytes=48 << 20),
        cost_estimate=pl.CostEstimate(flops=2 * R * L * D * D, bytes_accessed=16 * R * L * D, transcendentals=0),
        name="mid",
    )(o, x, dy, wout, e1, e2, x0, x1, gain, shift, xb)


def ffn_kernel(
    na_ref, da_ref, res_ref, o_ref, lo_ref, wexp_ref, wshr_ref, rexp_ref, rshr_ref, eu_ref, eur_ref,
    hd_ref, hdr_ref, b_ref, br_ref, x0_ref, x1_ref, e1_ref, e2_ref, wout_ref, gain_ref, xb_ref,
    y_ref, dr_ref, do_ref, g1_ref, g2_ref, gx0_ref, gx1_ref, ge_ref, ger_ref, gh_ref, ghr_ref,
    out_acc, dn_acc, we_ref, ws_ref, l3_ref, dl4_ref, *, R, per, co,
):
    f = pl.program_id(0)
    last = pl.num_programs(0) - 1
    N, W = na_ref.shape
    L, D, rank = N // R, res_ref.shape[2], x0_ref.shape[1]

    @pl.when(f == 0)
    def _():
        out_acc[...] = jnp.zeros_like(out_acc)
        dn_acc[...] = jnp.zeros_like(dn_acc)
        we_ref[D:] = jnp.zeros((W - D, we_ref.shape[1]), BF)
        ws_ref[D:] = jnp.zeros((W - D, ws_ref.shape[1]), BF)
        for r in range(R):
            l3_ref[r] = taken(na_ref[r * L : (r + 1) * L, D // 128 * 128 :], D % 128 + r * rank, rank)
            dl4_ref[r] = taken(da_ref[r * L : (r + 1) * L, D // 128 * 128 :], D % 128 + r * rank, rank)

    def narrow(eu, hd, width):
        for r in range(R):
            we_ref[D + r * rank : D + (r + 1) * rank, :width] = eu[r]
            ws_ref[D + r * rank : D + (r + 1) * rank, :width] = hd[r]

    def block(width, b, ge, gh):
        we, ws = we_ref[:, :width], ws_ref[:, :width]
        h = dot_nn(na_ref[...], we) + b
        dg = dot_nn(da_ref[...], ws)
        c0, c1 = 0.7978845608028654, 0.7978845608028654 * 0.044715
        hh = h * h
        th = jnp.tanh(h * (c0 + c1 * hh))
        half = 0.5 + 0.5 * th
        g = (h * half).astype(BF)
        slope = half + (h * (0.5 - 0.5 * (th * th))) * (c0 + (3 * c1) * hh)
        dh = (dg * slope).astype(BF)
        out_acc[...] += dot_nt(g, ws)
        dn_acc[...] += dot_nt(dh, we)
        for r in range(R):
            gh[r] = dot_nn(dl4_ref[r], g[r * L : (r + 1) * L])
            ge[r] = dot_nn(l3_ref[r], dh[r * L : (r + 1) * L])

    we_ref[:D] = wexp_ref[...].reshape(D, -1)
    if per:
        for part in range(per):

            @pl.when(lax.rem(f, per) == part)
            def _(part=part):
                for s in range(wshr_ref.shape[0]):
                    ws_ref[s * co : (s + 1) * co] = wshr_ref[s, 0, part * co : (part + 1) * co]

    else:
        ws_ref[:D] = wshr_ref[0]
    narrow(eu_ref, hd_ref, we_ref.shape[1])
    block(we_ref.shape[1], b_ref[...], ge_ref, gh_ref)

    @pl.when(f == last)
    def _():
        width = rshr_ref.shape[0]
        we_ref[:D, :width] = jnp.concatenate([rexp_ref[c] for c in range(rexp_ref.shape[0])], axis=1).T
        ws_ref[:D, :width] = rshr_ref[...].T
        narrow(eur_ref, hdr_ref, width)
        block(width, br_ref[...], ger_ref, ghr_ref)

        def rows(r, carry):
            here = pl.ds(pl.multiple_of(r * L, L), L)
            edge = D // 128 * 128
            dy = da_ref[here, :D]
            l4_t = taken(out_acc[here, edge:].astype(BF), D % 128 + r * rank, rank)
            dl3_t = taken(dn_acc[here, edge:].astype(BF), D % 128 + r * rank, rank)
            gx1_ref[r] = dot_nn(l4_t, dy)
            g2_ref[r] = dot_nn(dl3_t, na_ref[here, :D])
            res = res_ref[r]
            low = lambda t, w: lax.dot_general(t, w, (((0,), (0,)), ((), ())), preferred_element_type=F32)
            y_ref[r] = (res + out_acc[here, :D] + low(l4_t, x1_ref[r]) + xb_ref[...]).astype(BF).T
            e = (dn_acc[here, :D] + low(dl3_t, e2_ref[r])) * gain_ref[...]
            z, inv = layer_stats(res)
            dr = dy.astype(F32) + norm_back(e, z, inv)
            dr_ref[r] = dr
            drb = dr.astype(BF)
            dl2 = dot_nt(drb, x0_ref[r]).astype(BF)
            do_ref[r] = (dot_nt(drb, wout_ref[...]) + dot_nn(dl2, e1_ref[r])).astype(BF)
            g1_ref[r] = dot_nn(turned(dl2), o_ref[r])
            gx0_ref[r] = dot_nn(turned(lo_ref[r]), drb)
            return carry

        lax.fori_loop(0, R, rows, 0)


def ffn(na, da, res, o, lo, wexp, wshr, rexp, rshr, eu, eur, hd, hdr, b, br, x0, x1, e1, e2, wout, gain, xb):
    R, L, D = res.shape
    N, W = na.shape
    rank = x0.shape[1]
    width, rem = wexp.shape[-1], rshr.shape[0]
    blocks = eu.shape[2] // width
    cols = lambda *lead: pl.BlockSpec(lead + (width,), lambda f: (0,) * len(lead) + (f,))
    if wexp.ndim == 4:
        S, C = wexp.shape[:2]
        per, co = S // C, D // S
        wexp_spec = pl.BlockSpec((1, C, D // C, width), lambda f: (f, 0, 0, 0))
        wshr_spec = pl.BlockSpec((S, 1, D // C, width), lambda f: (0, f // per, 1, 0))
    else:
        per = co = 0
        wexp_spec = wshr_spec = pl.BlockSpec((1, D, width), lambda f: (f, 0, 0))
    shapes = [
        ((R, D, L), BF), ((R, L, D), F32), ((R, L, D), BF),
        ((R, rank, D), F32), ((R, rank, D), F32), ((R, rank, D), F32), ((R, rank, D), F32),
        ((R, rank, blocks * width), F32), ((R, rank, rem), F32), ((R, rank, blocks * width), F32), ((R, rank, rem), F32),
    ]
    out_specs = [whole_spec(s) for s, _ in shapes]
    out_specs[7] = out_specs[9] = cols(R, rank)
    ff = blocks * width + rem
    return pl.pallas_call(
        functools.partial(ffn_kernel, R=R, per=per, co=co),
        grid=(blocks,),
        in_specs=[whole_spec(a.shape) for a in (na, da, res, o, lo)]
        + [wexp_spec, wshr_spec, whole_spec(rexp.shape), whole_spec(rshr.shape)]
        + [cols(R, rank), whole_spec(eur.shape), cols(R, rank), whole_spec(hdr.shape), cols(1), whole_spec(br.shape)]
        + [whole_spec(a.shape) for a in (x0, x1, e1, e2, wout, gain, xb)],
        out_specs=out_specs,
        out_shape=[jax.ShapeDtypeStruct(s, d) for s, d in shapes],
        scratch_shapes=[
            pltpu.VMEM((N, W), F32), pltpu.VMEM((N, W), F32), pltpu.VMEM((W, width), BF), pltpu.VMEM((W, width), BF),
            pltpu.VMEM((R, rank, L), BF), pltpu.VMEM((R, rank, L), BF),
        ],
        compiler_params=pltpu.CompilerParams(vmem_limit_bytes=60 << 20),
        cost_estimate=pl.CostEstimate(
            flops=16 * N * D * ff, bytes_accessed=4 * D * ff + 24 * N * D, transcendentals=N * ff
        ),
        name="ffn",
    )(na, da, res, o, lo, wexp, wshr, rexp, rshr, eu, eur, hd, hdr, b, br, x0, x1, e1, e2, wout, gain, xb)


def project_kernel(meta_ref, dq_ref, dk_ref, dv_ref, w_ref, m_ref, *refs, W, js, r):
    count = len(js)
    n_refs, o_refs = refs[:count], refs[count : 2 * count]
    g_ref, n_ref, t_ref, wa_ref = refs[2 * count :]
    step = pl.program_id(0)
    j = step + js[0]
    me = meta_ref[0]
    D = w_ref.shape[0]
    rank = m_ref.shape[1]
    edge = D // 128 * 128
    for i in range(count):

        @pl.when(step == i)
        def _(i=i):
            n_ref[...] = n_refs[i][0]

    @pl.when(step == 0)
    def _():
        g_ref[...] = jnp.zeros_like(g_ref)
        wa_ref[:D] = w_ref[...]
        wa_ref[D : D + rank] = m_ref[0]
        wa_ref[D + rank :] = jnp.zeros((W - D - rank, 3 * W), BF)

    def work(pieces):
        low_t = taken(n_ref[:, edge:], D % 128 + r * rank, rank)
        total = sum(dot_nt(d[0], wa_ref[:, i * W : (i + 1) * W]) for i, d in pieces)
        for i, d in pieces:
            g_ref[i] += dot_nn(low_t, d[0])
        g_ref[3] += dot_nn(taken(total[:, edge:].astype(BF), D % 128, rank), n_ref[...])
        return total

    if js[0] == 0:

        @pl.when(j == 0)
        def _():
            o_refs[0][...] = work([(0, dq_ref), (1, dk_ref), (2, dv_ref)])

    if js[-1] > 0:

        @pl.when((j > 0) & ((me ^ j) < me))
        def _():
            t_ref[...] = work([(1, dk_ref), (2, dv_ref)]).astype(BF)

    for i in range(count):
        if js[i] > 0:

            @pl.when(step == i)
            def _(i=i):
                o_refs[i][...] = t_ref[...]


def project(meta, dq, dk, dv, w, m, n_parts, r, js):
    _, L, W = dq.shape
    rank = m.shape[1]
    count = len(js)
    out = pl.pallas_call(
        functools.partial(project_kernel, W=W, js=tuple(js), r=r),
        grid_spec=pltpu.PrefetchScalarGridSpec(
            num_scalar_prefetch=1,
            grid=(count,),
            in_specs=[
                whole_spec(dq.shape),
                pl.BlockSpec((1, L, W), lambda j, _: (0, j + js[0], 0)),
                pl.BlockSpec((1, L, W), lambda j, _: (0, j + js[0], 0)),
                whole_spec(w.shape),
                pl.BlockSpec((1, rank, 3 * W), lambda j, _: (r, 0, 0)),
            ]
            + [pl.BlockSpec((1, L, W), lambda j, _: (r, 0, 0))] * count,
            out_specs=[whole_spec((L, W))] * count + [whole_spec((4, rank, W))],
            scratch_shapes=[pltpu.VMEM((L, W), BF), pltpu.VMEM((L, W), BF), pltpu.VMEM((W, 3 * W), BF)],
        ),
        out_shape=[jax.ShapeDtypeStruct((L, W), BF if j else F32) for j in js]
        + [jax.ShapeDtypeStruct((4, rank, W), F32)],
        compiler_params=pltpu.CompilerParams(vmem_limit_bytes=60 << 20),
        cost_estimate=pl.CostEstimate(
            flops=8 * count * L * W * 2 * W, bytes_accessed=2 * (w.size + 4 * count * L * W), transcendentals=0
        ),
        name="project",
    )(meta, dq, dk, dv, w, m, *[n_parts[j] for j in js])
    return list(out[:count]), out[count]


def norm_kernel(x_ref, dy_ref, gain_ref, shift_ref, e_ref, n_ref, xr_ref, dyr_ref):
    x = x_ref[0].astype(F32)
    centred = x - jnp.mean(x, axis=0, keepdims=True)
    inv = lax.rsqrt(jnp.mean(centred * centred, axis=0, keepdims=True) + EPS)
    n = (centred * inv * gain_ref[...] + shift_ref[...]).astype(BF).T
    low = dot_nt(n, e_ref[0]).astype(BF)
    narrow = place(low, pl.program_id(0) * low.shape[1], n_ref.shape[2] - n.shape[1])
    n_ref[0] = jnp.concatenate([n, narrow], axis=1)
    xr_ref[0] = x_ref[0].T
    dyr_ref[0] = dy_ref[0].T


def first_norm(x_t, dy_t, gain, shift, e_t, W):
    R, D, L = x_t.shape
    col = pl.BlockSpec((1, D, L), lambda r: (r, 0, 0))
    row = pl.BlockSpec((1, L, D), lambda r: (r, 0, 0))
    return pl.pallas_call(
        norm_kernel,
        grid=(R,),
        in_specs=[col, col, whole_spec((D, 1)), whole_spec((D, 1)), pl.BlockSpec((1,) + e_t.shape[1:], lambda r: (r, 0, 0))],
        out_specs=[pl.BlockSpec((1, L, W), lambda r: (r, 0, 0)), row, row],
        out_shape=[jax.ShapeDtypeStruct((R, L, W), BF)] + [jax.ShapeDtypeStruct((R, L, D), BF)] * 2,
        compiler_params=pltpu.CompilerParams(vmem_limit_bytes=48 << 20),
        cost_estimate=pl.CostEstimate(flops=10 * x_t.size, bytes_accessed=10 * x_t.size, transcendentals=0),
        name="first_norm",
    )(x_t, dy_t, gain[:, None], shift[:, None], e_t)


def last_kernel(*refs, count, alias):
    if alias:
        refs = refs[1:]
    terms, (dr_ref, x_ref, gain_ref, e_ref, o_ref) = refs[:count], refs[count:]
    D = x_ref.shape[2]
    dn = terms[0][...]
    for t in terms[1:]:
        dn = dn + t[...].astype(F32)
    edge = D // 128 * 128
    rank = e_ref.shape[1]
    low_t = taken(dn[:, edge:].astype(BF), D % 128, rank)
    dn = dn[:, :D] + lax.dot_general(low_t, e_ref[0], (((0,), (0,)), ((), ())), preferred_element_type=F32)
    z, inv = layer_stats(x_ref[0].astype(F32))
    o_ref[0] = (dr_ref[0] + norm_back(dn * gain_ref[...], z, inv)).astype(BF).T


def last(r, before, terms, dr, x, gain, e_t):
    R, L, D = x.shape
    alias = before is not None
    return pl.pallas_call(
        functools.partial(last_kernel, count=len(terms), alias=alias),
        grid=(1,),
        in_specs=[pl.BlockSpec(memory_space=pl.ANY)] * alias
        + [whole_spec(t.shape) for t in terms]
        + [pl.BlockSpec((1, L, D), lambda i: (r, 0, 0))] * 2
        + [whole_spec((1, D)), pl.BlockSpec((1,) + e_t.shape[1:], lambda i: (r, 0, 0))],
        out_specs=pl.BlockSpec((1, D, L), lambda i: (r, 0, 0)),
        out_shape=jax.ShapeDtypeStruct((R, D, L), BF),
        input_output_aliases={0: 0} if alias else {},
        compiler_params=pltpu.CompilerParams(vmem_limit_bytes=48 << 20),
        cost_estimate=pl.CostEstimate(flops=20 * L * D, bytes_accessed=12 * L * D, transcendentals=0),
        name="last",
    )(*([before] if alias else []), *terms, dr, x, gain, e_t)


def late_kernel(slot_ref, part_ref, *refs, R, parts, D, W):
    g_refs, mix_ref, entry_ref, total = refs[:R], refs[R + 1], refs[R + 2], refs[R + 3]
    total[...] = jnp.zeros_like(total)
    count = g_refs[0].shape[0]
    for r in range(R):

        def one(i, carry):
            a = slot_ref[r * count + i]
            if r + 1 < R:
                total[a] = total[a] + g_refs[r][i].astype(F32)
            else:
                c = part_ref[i]
                total[a, c] = total[a, c] + g_refs[r][i].astype(F32)
            return carry

        lax.fori_loop(0, count, one, 0)
    per = parts // 4
    wide = [jnp.concatenate([total[:, i * per + p] for p in range(per)], axis=-1) for i in range(4)]
    mix_ref[...] = jnp.concatenate([w[:, :, :D] for w in wide[:3]], axis=-1)
    entry_ref[0] = wide[3][:, :, :D]


def late_slots(slot, part, gs, entry, D, W):
    R = len(gs)
    adapters = entry.shape[1]
    _, rank, width = gs[-1].shape
    parts = 4 * W // width
    return pl.pallas_call(
        functools.partial(late_kernel, R=R, parts=parts, D=D, W=W),
        grid_spec=pltpu.PrefetchScalarGridSpec(
            num_scalar_prefetch=2,
            grid=(1,),
            in_specs=[whole_spec(g.shape) for g in gs] + [pl.BlockSpec(memory_space=pl.ANY)],
            out_specs=[
                whole_spec((adapters, rank, 3 * D)),
                pl.BlockSpec((1, adapters, rank, D), lambda i, *_: (0, 0, 0, 0)),
            ],
            scratch_shapes=[pltpu.VMEM((adapters, parts, rank, width), F32)],
        ),
        out_shape=[
            jax.ShapeDtypeStruct((adapters, rank, 3 * D), F32),
            jax.ShapeDtypeStruct(entry.shape, F32),
        ],
        input_output_aliases={2 + R: 1},
        compiler_params=pltpu.CompilerParams(vmem_limit_bytes=60 << 20),
        cost_estimate=pl.CostEstimate(flops=0, bytes_accessed=12 << 20, transcendentals=0),
        name="late_slots",
    )(slot, part, *gs, entry)


def mm(pattern, a, b):
    return jnp.einsum(pattern, a, b, preferred_element_type=F32)


def layer_stats(v):
    middle = jnp.mean(v, axis=-1, keepdims=True)
    centred = v - middle
    inv = lax.rsqrt(jnp.mean(centred * centred, axis=-1, keepdims=True) + EPS)
    return centred * inv, inv


def norm_back(e, z, inv):
    return (e - jnp.mean(e, -1, keepdims=True) - z * jnp.mean(e * z, -1, keepdims=True)) * inv


def swap(x, axis, bit, needed):
    n = lax.axis_size(axis)
    return lax.ppermute(x, axis, [(d ^ bit, d) for d in range(n) if needed(d)])


def blocks_of(x, bits):
    found = {0: x}
    for bit in reversed(bits):
        for j in sorted(found):
            found[j | bit] = swap(found[j], "ctx", bit, lambda d, k=j | bit: (d ^ k) < d)
    return [found[j] for j in sorted(found)]


def block_sum(terms):
    return terms[0] if len(terms) == 1 else sum(t.astype(F32) for t in terms).astype(BF)


def blocks_back(held, bit):
    held = dict(held)
    for j in sorted(held):
        if j & bit:
            sent = block_sum(held.pop(j))
            got = swap(sent, "ctx", bit, lambda d, k=j, b=bit: ((d ^ b) ^ k) < (d ^ b))
            held[j ^ bit] = held[j ^ bit] + [got]
    return held


def turned_order(bits):
    count = 2 * bits[-1]
    return sorted(range(count), key=lambda c: [c & b for b in bits])


def ctx_sum_stage(g, bit):
    n = lax.axis_size("ctx")
    half = g.shape[0] // 2
    mine = (lax.axis_index("ctx") & bit) != 0
    low, high = g[:half], g[half:]
    got = lax.ppermute(jnp.where(mine, low, high), "ctx", [(d, d ^ bit) for d in range(n)])
    return jnp.where(mine, high, low) + got


def gather_all(x, seq_count, ctx_count, at, beside):
    n = seq_count * ctx_count
    seq_bits = [ctx_count << i for i in range(seq_count.bit_length() - 1)]
    ctx_bits = [1 << i for i in range(ctx_count.bit_length() - 1)]
    steps = seq_bits[::-1] + ctx_bits[::-1]
    held, order, beside = x[None], [0], list(beside)
    for i, bit in enumerate(steps):
        k = i - at
        if 0 <= k < len(beside):
            if callable(beside[k]):
                beside[k] = beside[k](beside[k - 1])
            held, beside[k] = lax.optimization_barrier((held, beside[k]))
        got = lax.ppermute(held, BOTH, [(d, d ^ bit) for d in range(n)])
        held = jnp.concatenate([held, got], 0)
        order = order + [o ^ bit for o in order]
    return held, order, beside


def slots_kernel(index_ref, g_ref, *refs, count, spans):
    outs, total = refs[:-1], refs[-1]
    total[...] = jnp.zeros_like(total)

    def one(i, carry):
        a = index_ref[i]
        total[a] = total[a] + g_ref[i].astype(F32)
        return carry

    lax.fori_loop(0, count, one, 0)
    for out, layers in zip(outs, spans):
        for i, pieces in enumerate(layers):
            parts = [total[:, :, first : first + width] for first, width in pieces]
            if parts:
                out[i] = parts[0] if len(parts) == 1 else jnp.concatenate(parts, axis=-1)


def to_slots(index, g, adapters, spans):
    count, rank, wide = g.shape
    rows = 8
    shapes = [(len(layers), adapters, rank, sum(w for _, w in layers[-1])) for layers in spans]
    return pl.pallas_call(
        functools.partial(slots_kernel, count=count, spans=spans),
        grid_spec=pltpu.PrefetchScalarGridSpec(
            num_scalar_prefetch=1,
            grid=(rank // rows,),
            in_specs=[pl.BlockSpec((count, rows, wide), lambda i, m: (0, i, 0))],
            out_specs=[pl.BlockSpec(s[:2] + (rows, s[3]), lambda i, m: (0, 0, i, 0)) for s in shapes],
            scratch_shapes=[pltpu.VMEM((adapters, rows, wide), F32)],
        ),
        out_shape=[jax.ShapeDtypeStruct(s, F32) for s in shapes],
        compiler_params=pltpu.CompilerParams(vmem_limit_bytes=48 << 20),
        cost_estimate=pl.CostEstimate(
            flops=count * rank * wide, bytes_accessed=count * rank * wide * 2 + adapters * rank * wide * 4, transcendentals=0
        ),
        name="to_slots",
    )(index, g)


def per_device(
    tokens, segments, adapter_index, norm_gains, norm_shifts, head_biases, expand_bias, exit_biases,
    mixing_weight, output_weight, expand_weight, shrink_weight,
    entry_adapters, mixing_adapters, expand_adapters, hidden_adapters, exit_adapters, cotangent,
):
    micro, seqs, L, D = tokens.shape
    R = micro * seqs
    adapters, rank = mixing_adapters.shape[:2]
    FF = expand_bias.shape[0]
    C = lax.axis_size("ctx")
    S = lax.axis_size("seq")
    bits = [1 << i for i in range(C.bit_length() - 1)]
    me = lax.axis_index("ctx")
    T = C * L
    W = -(-D // 128) * 128
    pad = W - D

    flip = lambda m: jnp.swapaxes(m, -1, -2)
    rows = mixing_weight.shape[0]
    cm, co, ce = mixing_weight.shape[1], output_weight.shape[1], expand_weight.shape[1]
    first = jnp.concatenate([mixing_weight, output_weight], 1)
    first = jnp.concatenate([first[: rows // 2], first[rows // 2 :]], 1)
    main = ce // 128 * 128
    rem = ce - main
    per = S // C
    shr_t = shrink_weight.T.reshape(co, per, ce).transpose(1, 0, 2)
    wide = first.shape[1]
    folded = lambda m: jnp.pad(
        m.reshape(-1, 8, m.shape[1]).transpose(1, 0, 2).reshape(8, -1), ((0, 0), (0, wide - m.size // 8))
    )
    rest = [folded(expand_weight[:, main:].T), folded(flip(shr_t[:, :, main:]).reshape(per * rem, co))]
    rest = jnp.concatenate(rest, 0)
    first = jnp.concatenate([first, rest], 0)
    second = jnp.concatenate([expand_weight[:, :main], shr_t[:, :, :main].reshape(per * co, main)], 0)
    g1 = lax.all_gather(first, BOTH)
    g2 = lax.all_gather(second, BOTH).reshape(S, C, -1, main)
    w_mix, w_out, r_exp, r_shr = unpack(g1, S, C, rows // 2, cm, co, D, W, rem, per)
    if rows % 16 == 0 and per * co == rows and co % 8 == 0:
        w_exp = w_shr = g2
    else:
        w_exp = g2[:, :, :rows].reshape(S, D, main)
        w_shr = g2[:, :, rows:].reshape(S, C, per, co, main).transpose(1, 2, 0, 3, 4).reshape(S, D, main)

    def split_ff(m):
        m = m.reshape(m.shape[:-1] + (S, ce))
        return m[..., :main].reshape(m.shape[:-2] + (S * main,)), m[..., main:].reshape(m.shape[:-2] + (S * rem,))

    index = adapter_index.reshape(R)
    take = lambda table, axis: jnp.stack(
        [lax.dynamic_index_in_dim(table, index[r], axis, keepdims=False) for r in range(R)], axis
    )
    entry = take(entry_adapters, 1)
    mix_up = take(mixing_adapters, 0)
    exp_up = take(expand_adapters, 0)
    hid = take(hidden_adapters, 0)
    exit_up = take(exit_adapters, 1)
    pad_heads = lambda m: jnp.concatenate([padded(m[..., i * D : (i + 1) * D]) for i in range(3)], -1)
    padded = lambda m: jnp.pad(m, [(0, 0)] * (m.ndim - 1) + [(0, pad)])
    mix_up = pad_heads(mix_up)
    entry_t = flip(entry)
    exp_main, exp_rest = split_ff(exp_up)
    hid_main, hid_rest = split_ff(flip(hid))
    bias_main, bias_rest = split_ff(expand_bias[None])
    head_bias = pad_heads(jnp.concatenate([head_biases[0], jnp.zeros_like(head_biases[0]), head_biases[1]])[None])

    seg = segments.reshape(R, L)
    seg_blocks = blocks_of(seg, bits)
    first_block = me * jnp.ones((R,), jnp.int32)
    for j, other in enumerate(seg_blocks):
        reached = ((me ^ j) <= me) & jnp.any(other == seg[:, :1], axis=1)
        first_block = jnp.where(reached, jnp.minimum(first_block, me ^ j), first_block)
    meta = jnp.concatenate([me[None], first_block]).astype(jnp.int32)
    qa, ka = document_lanes(seg, jnp.concatenate(seg_blocks, 1))

    n1, x, dy = first_norm(
        flip(tokens.reshape(R, L, D)), flip(cotangent.reshape(R, L, D)), norm_gains[0], norm_shifts[0],
        entry_t[0], W,
    )
    n1_parts = blocks_of(n1, bits)
    q, k, v = qkv(meta, n1_parts, w_mix, mix_up, head_bias)
    o, extra = attn_fwd(meta, q, k, v, qa, ka, D)

    res, na, da, lo = mid(
        o, x, dy, w_out, entry_t[1], entry_t[2], exit_up[0], exit_up[1], norm_gains[1][None], norm_shifts[1][None],
        exit_biases[0][None], W,
    )
    y, dr, do, g1, g2_, gx0, gx1, ge, ger, gh, ghr = ffn(
        na.reshape(R * L, W), da.reshape(R * L, W), res, o, lo, w_exp, w_shr, r_exp, r_shr,
        exp_main, exp_rest, hid_main, hid_rest, bias_main, bias_rest,
        exit_up[0], exit_up[1], entry_t[1], entry_t[2], w_out, norm_gains[1][None], exit_biases[1][None],
    )
    layer_output = flip(y).reshape(tokens.shape)

    number = jnp.broadcast_to((index.astype(F32) / C)[:, None, None], (R, rank, 128))
    early = jnp.concatenate([g1, g2_, gx0, gx1, ge, ger, gh, ghr, number], -1).reshape(R * rank, -1)
    swapped = turned_order(bits)
    share = R * rank // C
    early = jnp.concatenate([early[c * share : (c + 1) * share] for c in swapped], 0)

    pairs = W // 128
    ka_t = flip(ka)
    late, terms, held = [], [], None
    everything = list(range(C))
    for r in range(R):
        grads = ()
        cuts = [i * pairs // (len(bits) if held is None else 2) for i in range(len(bits) + 1 if held is None else 3)]
        for i, (p0, p1) in enumerate(zip(cuts, cuts[1:])):
            grads = attn_bwd(meta, q, k, v, do, o, extra, ka_t, r, p0, p1 - p0, grads)
            if held is None:
                early = ctx_sum_stage(early, bits[i])
                if i + 1 < len(bits):
                    do, early = lax.optimization_barrier((do, early))
            if held is not None and i == 0:
                held = blocks_back(held, bits[0])
                held = {j: [block_sum(t)] if j else t for j, t in held.items()}
                do, held = lax.optimization_barrier((do, held))
                for bit in bits[1:]:
                    held = blocks_back(held, bit)
        dq, dk, dv = grads
        if held is None:
            dk, early = lax.optimization_barrier((dk, early))
            early = lax.all_gather(early.astype(BF), BOTH).reshape(S * R, rank, -1)
        if held is not None:
            dk, held = lax.optimization_barrier((dk, held))
            terms.append(held[0])
        if r + 1 < R:
            parts, g = project(meta, dq, dk, dv, w_mix, mix_up, n1_parts, r, everything)
            held = {j: [p] for j, p in enumerate(parts)}
            do, held = lax.optimization_barrier((do, held))
        else:
            parts, g = project(meta, dq, dk, dv, w_mix, mix_up, n1_parts, r, everything)
            held = {j: [p] for j, p in enumerate(parts)}
            held = blocks_back(held, bits[0])
            held = {j: [block_sum(t)] if j else t for j, t in held.items()}
        g = g.reshape(4, rank, C // 4, -1).transpose(0, 2, 1, 3).reshape(C, rank, -1)
        if r + 1 < R:
            late.append(lax.all_gather(g.astype(BF), BOTH))
        else:
            g = jnp.concatenate([g[c : c + 1] for c in swapped], 0)
            for bit in bits:
                g = ctx_sum_stage(g, bit)
            g, held = lax.optimization_barrier((g, held))
            for bit in bits[1:]:
                held = blocks_back(held, bit)
            terms.append(held[0])
            grad_of = lambda i, before: last(i, before, terms[i], dr, x, norm_gains[0][None], entry_t[0])
            input_grad = None
            for i in range(R - 1):
                input_grad = grad_of(i, input_grad)
            all_index = early[:, 0, -1].astype(jnp.int32)
            both = []
            for at in (4 * D, 4 * D + FF):
                both.append([p for i in range(S) for p in ((at + i * main, main), (at + S * main + i * rem, rem))])
            entry_g, exit_g, expand_g, hidden_g = to_slots(
                all_index, early, adapters,
                [[[], [(0, D)], [(D, D)]], [[(2 * D, D)], [(3 * D, D)]], [both[0]], [both[1]]],
            )
            early_g = (entry_g, exit_g, expand_g, hidden_g)
            before = early_g if input_grad is None else (*early_g, input_grad)
            last_late, order, beside = gather_all(
                g[0].astype(BF), S, C, S.bit_length() - 1,
                [before, lambda done: grad_of(r, done[4] if len(done) > 4 else None)],
            )
            entry_g, exit_g, expand_g, hidden_g = beside[0][:4]
            input_grad = beside[1]
            late.append(last_late)
    device = lax.axis_index("seq") * C + me
    order = device ^ jnp.array(order, jnp.int32)
    by_row = all_index.reshape(S, R)
    slot = [jnp.repeat(by_row[:, r], C) for r in range(R - 1)]
    slot.append(jnp.sum(jnp.where((order // C)[:, None] == jnp.arange(S), by_row[:, R - 1], 0), 1))
    mixing_g, entry_g = late_slots(jnp.concatenate(slot), order % C, late, entry_g, D, W)
    input_grad = flip(input_grad).reshape(tokens.shape)

    return (
        layer_output,
        input_grad,
        flip(entry_g),
        mixing_g,
        expand_g[0],
        flip(hidden_g[0]),
        exit_g,
    )


def solution(mesh):
    rows = P(None, "seq", "ctx", None)
    weight = P("ctx", "seq")
    in_specs = (
        (rows, P(None, "seq", "ctx"), P(None, "seq")) + (P(),) * 5 + (weight,) * 4 + (P(),) * 5 + (rows,)
    )
    out_specs = (rows, rows) + (P(),) * 5
    return jax.shard_map(per_device, mesh=mesh, in_specs=in_specs, out_specs=out_specs, check_vma=False)
```

```python
import functools

import jax
import jax.numpy as jnp
from jax import lax
from jax.experimental import pallas as pl
from jax.experimental.pallas import tpu as pltpu
from jax.sharding import PartitionSpec as P

HEADS = 17
EPS = 1e-05
NEG = -1e30
BF = jnp.bfloat16
F32 = jnp.float32
BOTH = ("seq", "ctx")


FAR = -1e30


def product(a, b, ca, cb):
    return lax.dot_general(a, b, (((ca,), (cb,)), ((), ())), preferred_element_type=F32)


def thirds(x):
    a = x.astype(BF)
    b = (x - a.astype(F32)).astype(BF)
    c = (x - a.astype(F32) - b.astype(F32)).astype(BF)
    return a, b, c


def lanes_of(h, lane):
    return (lane < 64) if h == 0 else (lane >= 64)


def attn_fwd_kernel(
    meta_ref, q_ref, k_ref, v_ref, qa_ref, ka_ref, o_ref, a_ref, kh_ref, vt_ref, s_ref, acc_ref, st_ref, *, L
):
    r = pl.program_id(0)
    me = meta_ref[0]
    lo = meta_ref[1 + r]
    lane = lax.broadcasted_iota(jnp.int32, (1, 128), 1)
    vt_ref[...] = v_ref[0].T
    q2, qa = q_ref[0], qa_ref[0]
    qh = [jnp.where(lanes_of(h, lane), q2, qa).T for h in range(2)]
    for h in range(2):
        kh_ref[h] = jnp.where(lanes_of(h, lane), k_ref[0], ka_ref[0])
        st_ref[h] = jnp.concatenate([jnp.full((1, L), NEG, F32), jnp.zeros((7, L), F32)], axis=0)
    acc_ref[...] = jnp.zeros_like(acc_ref)

    def at(t):
        return pl.multiple_of((t ^ me) * L, L)

    def scores(t, h):
        s_ref[h] = product(kh_ref[h, pl.ds(at(t), L), :], qh[h], 1, 0)

    def gather(t, h, diagonal):
        s = s_ref[h]
        if diagonal:
            ok = lax.broadcasted_iota(jnp.int32, (L, L), 0) <= lax.broadcasted_iota(jnp.int32, (L, L), 1)
            s = jnp.where(ok, s, NEG)
        m = st_ref[h, 0:1]
        new = jnp.maximum(m, jnp.max(s, axis=0, keepdims=True))
        scale = jnp.exp(m - new)
        p = jnp.exp(s - new)
        st_ref[h, 1:2] = st_ref[h, 1:2] * scale + jnp.sum(p, axis=0, keepdims=True)
        st_ref[h, 0:1] = new
        rows = slice(h * 64, (h + 1) * 64)
        acc_ref[rows] = acc_ref[rows] * scale + product(vt_ref[rows, pl.ds(at(t), L)], p.astype(BF), 1, 0)

    def triangle(h):
        H = L // 2
        ok = lax.broadcasted_iota(jnp.int32, (H, H), 0) <= lax.broadcasted_iota(jnp.int32, (H, H), 1)
        s00 = jnp.where(ok, s_ref[h, :H, :H], NEG)
        s01 = s_ref[h, :H, H:]
        s11 = jnp.where(ok, s_ref[h, H:, H:], NEG)
        top = lambda s: jnp.max(s, axis=0, keepdims=True)
        add = lambda p: jnp.sum(p, axis=0, keepdims=True)
        m = st_ref[h, 0:1]
        new = jnp.maximum(m, jnp.concatenate([top(s00), jnp.maximum(top(s01), top(s11))], axis=1))
        scale = jnp.exp(m - new)
        p00 = jnp.exp(s00 - new[:, :H])
        p01 = jnp.exp(s01 - new[:, H:])
        p11 = jnp.exp(s11 - new[:, H:])
        st_ref[h, 1:2] = st_ref[h, 1:2] * scale + jnp.concatenate([add(p00), add(p01) + add(p11)], axis=1)
        st_ref[h, 0:1] = new
        rows = slice(h * 64, (h + 1) * 64)
        first, second = vt_ref[rows, :H], vt_ref[rows, H:L]
        left = product(first, p00.astype(BF), 1, 0)
        right = product(first, p01.astype(BF), 1, 0) + product(second, p11.astype(BF), 1, 0)
        acc_ref[rows, :H] = acc_ref[rows, :H] * scale[:, :H] + left
        acc_ref[rows, H:] = acc_ref[rows, H:] * scale[:, H:] + right

    scores(lo, 0)

    def body(t, carry):
        scores(t, 1)
        gather(t, 0, False)
        scores(t + 1, 0)
        gather(t, 1, False)
        return carry

    lax.fori_loop(lo, me, body, 0)
    scores(me, 1)
    for h in range(2):
        if L % 256 == 0:
            triangle(h)
        else:
            gather(me, h, True)
    rows = []
    for h in range(2):
        total = st_ref[h, 1:2]
        sl = slice(h * 64, (h + 1) * 64)
        acc_ref[sl] = acc_ref[sl] / total
        rows.append(thirds(-(st_ref[h, 0:1] + jnp.log(total))))
    o_ref[0] = acc_ref[...].astype(BF).T
    sub = lax.broadcasted_iota(jnp.int32, (128, 1), 0)
    extra = jnp.zeros((128, L), F32)
    for h in range(2):
        for i in range(3):
            extra = jnp.where(sub == (1 - h) * 64 + 8 + i, rows[h][i].astype(F32), extra)
    a_ref[0, 0] = qa + extra.astype(BF).T


def attn_fwd(meta, q, k, v, qa, ka, D):
    R, L, W = q.shape
    T = k.shape[1]
    NP = W // 128
    col = lambda r, p, m: (r, 0, p)
    one = lambda r, p, m: (r, 0, 0)
    return pl.pallas_call(
        functools.partial(attn_fwd_kernel, L=L),
        grid_spec=pltpu.PrefetchScalarGridSpec(
            num_scalar_prefetch=1,
            grid=(R, NP),
            in_specs=[
                pl.BlockSpec((1, L, 128), col),
                pl.BlockSpec((1, T, 128), col),
                pl.BlockSpec((1, T, 128), col),
                pl.BlockSpec((1, L, 128), one),
                pl.BlockSpec((1, T, 128), one),
            ],
            out_specs=[pl.BlockSpec((1, L, 128), col), pl.BlockSpec((1, 1, L, 128), lambda r, p, m: (r, p, 0, 0))],
            scratch_shapes=[
                pltpu.VMEM((2, T, 128), BF),
                pltpu.VMEM((128, T), BF),
                pltpu.VMEM((2, L, L), F32),
                pltpu.VMEM((128, L), F32),
                pltpu.VMEM((2, 8, L), F32),
            ],
        ),
        out_shape=[jax.ShapeDtypeStruct((R, L, D), BF), jax.ShapeDtypeStruct((R, NP, L, 128), BF)],
        compiler_params=pltpu.CompilerParams(vmem_limit_bytes=48 << 20),
        cost_estimate=pl.CostEstimate(
            flops=R * 40 * L * T * W, bytes_accessed=R * (2 * L + 2 * T) * W * 2, transcendentals=R * L * T * 18
        ),
        name="attn_fwd",
    )(meta, q, k, v, qa, ka)


def attn_bwd_kernel(
    meta_ref, q_ref, k_ref, v_ref, do_ref, o_ref, a_ref, ka_ref, *refs, L, r0, D, first,
):
    dq_ref, dk_ref, dv_ref, kh_ref, vh_ref, kt_ref, s_ref, dp_ref, dqt_ref, dkt_ref, dvt_ref = refs[-11:]
    me = meta_ref[0]
    lo = meta_ref[1 + r0]
    lane = lax.broadcasted_iota(jnp.int32, (1, 128), 1)
    row = lax.broadcasted_iota(jnp.int32, (128, 1), 0)
    limit = D - (pl.program_id(0) + first) * 128
    ones = jnp.where((row % 64 >= 8) & (row % 64 < 11), 1.0, 0.0).astype(BF)
    do2 = jnp.where(lane < limit, do_ref[0], jnp.zeros((), BF))
    o2 = jnp.where(lane < limit, o_ref[0], jnp.zeros((), BF))
    q2 = q_ref[0]
    prod = do2.astype(F32) * o2.astype(F32)
    qh, dh = [], []
    for h in range(2):
        mine = lanes_of(h, lane)
        parts = thirds(-jnp.sum(jnp.where(mine, prod, 0.0), axis=1, keepdims=True))
        extra = jnp.zeros((1, 128), BF)
        for i in range(3):
            extra = jnp.where(lane == (1 - h) * 64 + 8 + i, parts[i], extra)
        dh.append(jnp.where(mine, do2, extra))
        qh.append(jnp.where(mine, q2, a_ref[0, 0]))
    qt, dot_ = q2.T, do2.T
    dqt_ref[...] = jnp.zeros_like(dqt_ref)

    def at(t):
        return pl.multiple_of((t ^ me) * L, L)

    def turn(t):
        here = pl.ds(at(t), L)
        kt = k_ref[0, here, :].T
        vt = v_ref[0, here, :].T
        kt_ref[:, here] = kt
        for h in range(2):
            kh_ref[h, :, here] = jnp.where(lanes_of(h, row), kt, ka_ref[0, :, here])
            vh_ref[h, :, here] = jnp.where(lanes_of(h, row), vt, ones)

    def scores(t, h):
        here = pl.ds(at(t), L)
        s_ref[h] = product(qh[h], kh_ref[h, :, here], 1, 0)
        dp_ref[h] = product(dh[h], vh_ref[h, :, here], 1, 0)

    def gather(t, h, diagonal):
        p = jnp.exp(s_ref[h])
        if diagonal:
            ok = lax.broadcasted_iota(jnp.int32, (L, L), 1) <= lax.broadcasted_iota(jnp.int32, (L, L), 0)
            p = jnp.where(ok, p, 0.0)
        ds = (p * dp_ref[h]).astype(BF)
        rows = slice(h * 64, (h + 1) * 64)
        dvt_ref[rows] = product(dot_[rows], p.astype(BF), 1, 0)
        dkt_ref[rows] = product(qt[rows], ds, 1, 0)
        dqt_ref[rows] += product(kt_ref[rows, pl.ds(at(t), L)], ds, 1, 1)

    def triangle(h):
        H = L // 2
        ok = lax.broadcasted_iota(jnp.int32, (H, H), 1) <= lax.broadcasted_iota(jnp.int32, (H, H), 0)
        p00 = jnp.where(ok, jnp.exp(s_ref[h, :H, :H]), 0.0)
        p10 = jnp.exp(s_ref[h, H:, :H])
        p11 = jnp.where(ok, jnp.exp(s_ref[h, H:, H:]), 0.0)
        ds00 = (p00 * dp_ref[h, :H, :H]).astype(BF)
        ds10 = (p10 * dp_ref[h, H:, :H]).astype(BF)
        ds11 = (p11 * dp_ref[h, H:, H:]).astype(BF)
        rows = slice(h * 64, (h + 1) * 64)
        do_h, q_h, k_h = dot_[rows], qt[rows], kt_ref[rows, :L]
        dvt_ref[rows, :H] = product(do_h[:, :H], p00.astype(BF), 1, 0) + product(do_h[:, H:], p10.astype(BF), 1, 0)
        dvt_ref[rows, H:] = product(do_h[:, H:], p11.astype(BF), 1, 0)
        dkt_ref[rows, :H] = product(q_h[:, :H], ds00, 1, 0) + product(q_h[:, H:], ds10, 1, 0)
        dkt_ref[rows, H:] = product(q_h[:, H:], ds11, 1, 0)
        dqt_ref[rows, :H] += product(k_h[:, :H], ds00, 1, 1)
        dqt_ref[rows, H:] += product(k_h[:, :H], ds10, 1, 1) + product(k_h[:, H:], ds11, 1, 1)

    def store(t):
        here = pl.ds(at(t), L)
        dk_ref[0, here, :] = dkt_ref[...].astype(BF).T
        dv_ref[0, here, :] = dvt_ref[...].astype(BF).T

    def none(t, carry):
        dk_ref[0, pl.ds(at(t), L), :] = jnp.zeros((L, 128), BF)
        dv_ref[0, pl.ds(at(t), L), :] = jnp.zeros((L, 128), BF)
        return carry

    lax.fori_loop(0, lo, none, 0)
    turn(lo)
    scores(lo, 0)

    def body(t, carry):
        scores(t, 1)
        turn(t + 1)
        gather(t, 0, False)
        scores(t + 1, 0)
        gather(t, 1, False)
        store(t)
        return carry

    lax.fori_loop(lo, me, body, 0)
    scores(me, 1)
    for h in range(2):
        if L % 256 == 0:
            triangle(h)
        else:
            gather(me, h, True)
    store(me)
    dq_ref[0] = dqt_ref[...].astype(BF).T * jnp.asarray(0.125, BF)


def attn_bwd(meta, q, k, v, do, o, extra, ka_t, r0, first, count, before=()):
    R, L, W = q.shape
    T, D = k.shape[1], do.shape[2]
    col = lambda p, m: (r0, 0, p + first)
    out = lambda p, m: (0, 0, p + first)
    return pl.pallas_call(
        functools.partial(attn_bwd_kernel, L=L, r0=r0, D=D, first=first),
        grid_spec=pltpu.PrefetchScalarGridSpec(
            num_scalar_prefetch=1,
            grid=(count,),
            in_specs=[
                pl.BlockSpec((1, L, 128), col),
                pl.BlockSpec((1, T, 128), col),
                pl.BlockSpec((1, T, 128), col),
                pl.BlockSpec((1, L, 128), col),
                pl.BlockSpec((1, L, 128), col),
                pl.BlockSpec((1, 1, L, 128), lambda p, m: (r0, p + first, 0, 0)),
                pl.BlockSpec((1, 128, T), lambda p, m: (r0, 0, 0)),
            ]
            + [pl.BlockSpec(memory_space=pl.ANY) for _ in before],
            out_specs=[pl.BlockSpec((1, L, 128), out), pl.BlockSpec((1, T, 128), out), pl.BlockSpec((1, T, 128), out)],
            scratch_shapes=[
                pltpu.VMEM((2, 128, T), BF),
                pltpu.VMEM((2, 128, T), BF),
                pltpu.VMEM((128, T), BF),
                pltpu.VMEM((2, L, L), F32),
                pltpu.VMEM((2, L, L), F32),
                pltpu.VMEM((128, L), F32),
                pltpu.VMEM((128, L), F32),
                pltpu.VMEM((128, L), F32),
            ],
        ),
        out_shape=[
            jax.ShapeDtypeStruct((1, L, W), BF),
            jax.ShapeDtypeStruct((1, T, W), BF),
            jax.ShapeDtypeStruct((1, T, W), BF),
        ],
        compiler_params=pltpu.CompilerParams(vmem_limit_bytes=48 << 20),
        input_output_aliases={8 + i: i for i in range(len(before))},
        cost_estimate=pl.CostEstimate(
            flops=60 * L * T * 128 * count, bytes_accessed=(3 * L + 4 * T) * 256 * count, transcendentals=L * T * 2 * count
        ),
        name="attn_bwd",
    )(meta, q, k, v, do, o, extra, ka_t, *before)


def document_lanes(seg_q, seg_k):
    number = jnp.arange(64, dtype=jnp.int32)
    two = lambda m: jnp.concatenate([m, m], -1).astype(BF)
    qa = jnp.where((number < 8) & (number != seg_q[..., None]), FAR, 0.0)
    ka = jnp.where((number == seg_k[..., None]) | ((number >= 8) & (number < 11)), 1.0, 0.0)
    return two(qa), two(ka)


def dot_nn(a, b):
    return lax.dot_general(a, b, (((1,), (0,)), ((), ())), preferred_element_type=F32)


def dot_nt(a, b):
    return lax.dot_general(a, b, (((1,), (1,)), ((), ())), preferred_element_type=F32)


def turned(x):
    rank = x.shape[1]
    eye = (
        lax.broadcasted_iota(jnp.int32, (rank, rank), 0) == lax.broadcasted_iota(jnp.int32, (rank, rank), 1)
    ).astype(F32).astype(BF)
    return dot_nt(eye, x).astype(BF)


def place(x, first, width):
    rank = x.shape[1]
    to = lax.broadcasted_iota(jnp.int32, (rank, width), 1) == lax.broadcasted_iota(jnp.int32, (rank, width), 0) + first
    return dot_nn(x, to.astype(F32).astype(BF)).astype(BF)


def taken(x, first, rank):
    width = x.shape[1]
    to = lax.broadcasted_iota(jnp.int32, (rank, width), 1) == lax.broadcasted_iota(jnp.int32, (rank, width), 0) + first
    return dot_nt(to.astype(F32).astype(BF), x).astype(BF)


def whole_spec(shape, **kw):
    return pl.BlockSpec(shape, lambda *_: (0,) * len(shape), pipeline_mode=pl.Buffered(1))


def unpack_kernel(g_ref, mix_ref, out_ref, rexp_ref, rshr_ref, *, cm, co, D, W, rem, per):
    S = g_ref.shape[0]
    rows = mix_ref.shape[2]
    half_width = cm + co
    for half in range(2):
        at = half * half_width
        mix = jnp.concatenate([g_ref[s, 0, :rows, at : at + cm] for s in range(S)], axis=1)
        out = jnp.concatenate([g_ref[s, 0, :rows, at + cm : at + half_width] for s in range(S)], axis=1)
        zero = jnp.zeros((mix.shape[0], W - D), mix.dtype)
        for i in range(3):
            mix_ref[0, half, :, i * W : (i + 1) * W] = jnp.concatenate([mix[:, i * D : (i + 1) * D], zero], axis=1)
        out_ref[0, half] = out
    for s in range(S):
        for i in range(rem // 8):
            rexp_ref[0, s * rem + i * 8 : s * rem + i * 8 + 8] = g_ref[
                s, 0, rows : rows + 8, i * 2 * rows : (i + 1) * 2 * rows
            ]
    for i in range(per * rem // 8):
        rshr_ref[0, i * 8 : i * 8 + 8] = jnp.concatenate(
            [g_ref[s, 0, rows + 8 : rows + 16, i * co : (i + 1) * co] for s in range(S)], axis=1
        )


def unpack(g, S, C, rows2, cm, co, D, W, rem, per):
    g = g.reshape(S, C, -1, 2 * (cm + co))
    shapes = [(C, 2, rows2, 3 * W), (C, 2, rows2, D), (C, S * rem, 2 * rows2), (C, per * rem, D)]
    mix, out, rexp, rshr = pl.pallas_call(
        functools.partial(unpack_kernel, cm=cm, co=co, D=D, W=W, rem=rem, per=per),
        grid=(C,),
        in_specs=[pl.BlockSpec((S, 1) + g.shape[2:], lambda c: (0, c, 0, 0))],
        out_specs=[pl.BlockSpec((1,) + s[1:], lambda c, n=len(s): (c,) + (0,) * (n - 1)) for s in shapes],
        out_shape=[jax.ShapeDtypeStruct(s, BF) for s in shapes],
        compiler_params=pltpu.CompilerParams(vmem_limit_bytes=48 << 20),
        cost_estimate=pl.CostEstimate(flops=0, bytes_accessed=4 * g.size, transcendentals=0),
        name="unpack",
    )(g)
    return mix.reshape(D, 3 * W), out.reshape(D, D), rexp, rshr.reshape(C * per * rem, D)


def qkv_kernel(meta_ref, *refs, count, W, R):
    n_refs = refs[:count]
    w_ref, m_ref, b_ref, q_ref, k_ref, v_ref, n_ref, wa_ref = refs[count:]
    j = pl.program_id(0)
    me = meta_ref[0]
    D = w_ref.shape[0]
    rank = m_ref.shape[1]
    for jj in range(count):

        @pl.when(j == jj)
        def _(jj=jj):
            n_ref[...] = n_refs[jj][...].reshape(n_ref.shape)

    @pl.when(j == 0)
    def _():
        wa_ref[:D] = w_ref[...]
        for r in range(R):
            wa_ref[D + r * rank : D + (r + 1) * rank] = m_ref[r]
        wa_ref[D + R * rank :] = jnp.zeros((W - D - R * rank, 3 * W), BF)

    def part(i):
        s = slice(i * W, (i + 1) * W)
        return (dot_nn(n_ref[...], wa_ref[:, s]) + b_ref[:, s]).reshape(R, -1, W)

    @pl.when(j == 0)
    def _():
        q_ref[...] = (part(0) * 0.125).astype(BF)

    @pl.when((me ^ j) <= me)
    def _():
        k_ref[...] = part(1).astype(BF)
        v_ref[...] = part(2).astype(BF)


def qkv(meta, n_parts, w, m, b):
    count = len(n_parts)
    R, L, W = n_parts[0].shape
    T = count * L
    row = pl.BlockSpec((R, L, W), lambda j, _: (0, j, 0))
    return pl.pallas_call(
        functools.partial(qkv_kernel, W=W, count=count, R=R),
        grid_spec=pltpu.PrefetchScalarGridSpec(
            num_scalar_prefetch=1,
            grid=(count,),
            in_specs=[whole_spec(x.shape) for x in (*n_parts, w, m, b)],
            out_specs=[whole_spec((R, L, W)), row, row],
            scratch_shapes=[pltpu.VMEM((R * L, W), BF), pltpu.VMEM((W, 3 * W), BF)],
        ),
        out_shape=[
            jax.ShapeDtypeStruct((R, L, W), BF),
            jax.ShapeDtypeStruct((R, T, W), BF),
            jax.ShapeDtypeStruct((R, T, W), BF),
        ],
        compiler_params=pltpu.CompilerParams(vmem_limit_bytes=60 << 20),
        cost_estimate=pl.CostEstimate(
            flops=4 * R * T * W * 2 * W, bytes_accessed=2 * (R * T * W + w.size + 2 * R * T * W), transcendentals=0
        ),
        name="qkv",
    )(meta, *n_parts, w, m, b)


def mid_kernel(
    o_ref, x_ref, dy_ref, wout_ref, e1_ref, e2_ref, x0_ref, x1_ref, gain_ref, shift_ref, xb_ref,
    res_ref, na_ref, da_ref, lo_ref,
):
    r = pl.program_id(0)
    D, W = o_ref.shape[2], na_ref.shape[2]
    rank = e1_ref.shape[1]
    o, dy = o_ref[0], dy_ref[0]
    lo = dot_nt(o, e1_ref[0]).astype(BF)
    lo_ref[0] = lo
    res = x_ref[0].astype(F32) + dot_nn(o, wout_ref[...]) + dot_nn(lo, x0_ref[0]) + xb_ref[...]
    res_ref[0] = res
    z, _ = layer_stats(res)
    n2 = (z * gain_ref[...] + shift_ref[...]).astype(BF)
    l3 = dot_nt(n2, e2_ref[0]).astype(BF)
    na_ref[0] = jnp.concatenate([n2, place(l3, r * rank, W - D)], axis=1)
    dl4 = dot_nt(dy, x1_ref[0]).astype(BF)
    da_ref[0] = jnp.concatenate([dy, place(dl4, r * rank, W - D)], axis=1)


def mid(o, x, dy, wout, e1, e2, x0, x1, gain, shift, xb, W):
    R, L, D = o.shape
    rank = e1.shape[1]
    row = pl.BlockSpec((1, L, D), lambda r: (r, 0, 0))
    wide = pl.BlockSpec((1, L, W), lambda r: (r, 0, 0))
    small = pl.BlockSpec((1, rank, D), lambda r: (r, 0, 0))
    return pl.pallas_call(
        mid_kernel,
        grid=(R,),
        in_specs=[row] * 3 + [whole_spec(wout.shape)] + [small] * 4 + [whole_spec((1, D))] * 3,
        out_specs=[row, wide, wide, pl.BlockSpec((1, L, rank), lambda r: (r, 0, 0))],
        out_shape=[
            jax.ShapeDtypeStruct((R, L, D), F32),
            jax.ShapeDtypeStruct((R, L, W), BF),
            jax.ShapeDtypeStruct((R, L, W), BF),
            jax.ShapeDtypeStruct((R, L, rank), BF),
        ],
        compiler_params=pltpu.CompilerParams(vmem_limit_bytes=48 << 20),
        cost_estimate=pl.CostEstimate(flops=2 * R * L * D * D, bytes_accessed=16 * R * L * D, transcendentals=0),
        name="mid",
    )(o, x, dy, wout, e1, e2, x0, x1, gain, shift, xb)


def ffn_kernel(
    na_ref, da_ref, res_ref, o_ref, lo_ref, wexp_ref, wshr_ref, rexp_ref, rshr_ref, eu_ref, eur_ref,
    hd_ref, hdr_ref, b_ref, br_ref, x0_ref, x1_ref, e1_ref, e2_ref, wout_ref, gain_ref, xb_ref,
    y_ref, dr_ref, do_ref, g1_ref, g2_ref, gx0_ref, gx1_ref, ge_ref, ger_ref, gh_ref, ghr_ref,
    out_acc, dn_acc, we_ref, ws_ref, l3_ref, dl4_ref, *, R, per, co,
):
    f = pl.program_id(0)
    last = pl.num_programs(0) - 1
    N, W = na_ref.shape
    L, D, rank = N // R, res_ref.shape[2], x0_ref.shape[1]

    @pl.when(f == 0)
    def _():
        out_acc[...] = jnp.zeros_like(out_acc)
        dn_acc[...] = jnp.zeros_like(dn_acc)
        we_ref[D:] = jnp.zeros((W - D, we_ref.shape[1]), BF)
        ws_ref[D:] = jnp.zeros((W - D, ws_ref.shape[1]), BF)
        for r in range(R):
            l3_ref[r] = taken(na_ref[r * L : (r + 1) * L, D // 128 * 128 :], D % 128 + r * rank, rank)
            dl4_ref[r] = taken(da_ref[r * L : (r + 1) * L, D // 128 * 128 :], D % 128 + r * rank, rank)

    def narrow(eu, hd, width):
        for r in range(R):
            we_ref[D + r * rank : D + (r + 1) * rank, :width] = eu[r]
            ws_ref[D + r * rank : D + (r + 1) * rank, :width] = hd[r]

    def block(width, b, ge, gh):
        we, ws = we_ref[:, :width], ws_ref[:, :width]
        h = dot_nn(na_ref[...], we) + b
        dg = dot_nn(da_ref[...], ws)
        c0, c1 = 0.7978845608028654, 0.7978845608028654 * 0.044715
        hh = h * h
        th = jnp.tanh(h * (c0 + c1 * hh))
        half = 0.5 + 0.5 * th
        g = (h * half).astype(BF)
        slope = half + (h * (0.5 - 0.5 * (th * th))) * (c0 + (3 * c1) * hh)
        dh = (dg * slope).astype(BF)
        out_acc[...] += dot_nt(g, ws)
        dn_acc[...] += dot_nt(dh, we)
        for r in range(R):
            gh[r] = dot_nn(dl4_ref[r], g[r * L : (r + 1) * L])
            ge[r] = dot_nn(l3_ref[r], dh[r * L : (r + 1) * L])

    we_ref[:D] = wexp_ref[...].reshape(D, -1)
    if per:
        for part in range(per):

            @pl.when(lax.rem(f, per) == part)
            def _(part=part):
                for s in range(wshr_ref.shape[0]):
                    ws_ref[s * co : (s + 1) * co] = wshr_ref[s, 0, part * co : (part + 1) * co]

    else:
        ws_ref[:D] = wshr_ref[0]
    narrow(eu_ref, hd_ref, we_ref.shape[1])
    block(we_ref.shape[1], b_ref[...], ge_ref, gh_ref)

    @pl.when(f == last)
    def _():
        width = rshr_ref.shape[0]
        we_ref[:D, :width] = jnp.concatenate([rexp_ref[c] for c in range(rexp_ref.shape[0])], axis=1).T
        ws_ref[:D, :width] = rshr_ref[...].T
        narrow(eur_ref, hdr_ref, width)
        block(width, br_ref[...], ger_ref, ghr_ref)

        def rows(r, carry):
            here = pl.ds(pl.multiple_of(r * L, L), L)
            edge = D // 128 * 128
            dy = da_ref[here, :D]
            l4_t = taken(out_acc[here, edge:].astype(BF), D % 128 + r * rank, rank)
            dl3_t = taken(dn_acc[here, edge:].astype(BF), D % 128 + r * rank, rank)
            gx1_ref[r] = dot_nn(l4_t, dy)
            g2_ref[r] = dot_nn(dl3_t, na_ref[here, :D])
            res = res_ref[r]
            low = lambda t, w: lax.dot_general(t, w, (((0,), (0,)), ((), ())), preferred_element_type=F32)
            y_ref[r] = (res + out_acc[here, :D] + low(l4_t, x1_ref[r]) + xb_ref[...]).astype(BF).T
            e = (dn_acc[here, :D] + low(dl3_t, e2_ref[r])) * gain_ref[...]
            z, inv = layer_stats(res)
            dr = dy.astype(F32) + norm_back(e, z, inv)
            dr_ref[r] = dr
            drb = dr.astype(BF)
            dl2 = dot_nt(drb, x0_ref[r]).astype(BF)
            do_ref[r] = (dot_nt(drb, wout_ref[...]) + dot_nn(dl2, e1_ref[r])).astype(BF)
            g1_ref[r] = dot_nn(turned(dl2), o_ref[r])
            gx0_ref[r] = dot_nn(turned(lo_ref[r]), drb)
            return carry

        lax.fori_loop(0, R, rows, 0)


def ffn(na, da, res, o, lo, wexp, wshr, rexp, rshr, eu, eur, hd, hdr, b, br, x0, x1, e1, e2, wout, gain, xb):
    R, L, D = res.shape
    N, W = na.shape
    rank = x0.shape[1]
    width, rem = wexp.shape[-1], rshr.shape[0]
    blocks = eu.shape[2] // width
    cols = lambda *lead: pl.BlockSpec(lead + (width,), lambda f: (0,) * len(lead) + (f,))
    if wexp.ndim == 4:
        S, C = wexp.shape[:2]
        per, co = S // C, D // S
        wexp_spec = pl.BlockSpec((1, C, D // C, width), lambda f: (f, 0, 0, 0))
        wshr_spec = pl.BlockSpec((S, 1, D // C, width), lambda f: (0, f // per, 1, 0))
    else:
        per = co = 0
        wexp_spec = wshr_spec = pl.BlockSpec((1, D, width), lambda f: (f, 0, 0))
    shapes = [
        ((R, D, L), BF), ((R, L, D), F32), ((R, L, D), BF),
        ((R, rank, D), F32), ((R, rank, D), F32), ((R, rank, D), F32), ((R, rank, D), F32),
        ((R, rank, blocks * width), F32), ((R, rank, rem), F32), ((R, rank, blocks * width), F32), ((R, rank, rem), F32),
    ]
    out_specs = [whole_spec(s) for s, _ in shapes]
    out_specs[7] = out_specs[9] = cols(R, rank)
    ff = blocks * width + rem
    return pl.pallas_call(
        functools.partial(ffn_kernel, R=R, per=per, co=co),
        grid=(blocks,),
        in_specs=[whole_spec(a.shape) for a in (na, da, res, o, lo)]
        + [wexp_spec, wshr_spec, whole_spec(rexp.shape), whole_spec(rshr.shape)]
        + [cols(R, rank), whole_spec(eur.shape), cols(R, rank), whole_spec(hdr.shape), cols(1), whole_spec(br.shape)]
        + [whole_spec(a.shape) for a in (x0, x1, e1, e2, wout, gain, xb)],
        out_specs=out_specs,
        out_shape=[jax.ShapeDtypeStruct(s, d) for s, d in shapes],
        scratch_shapes=[
            pltpu.VMEM((N, W), F32), pltpu.VMEM((N, W), F32), pltpu.VMEM((W, width), BF), pltpu.VMEM((W, width), BF),
            pltpu.VMEM((R, rank, L), BF), pltpu.VMEM((R, rank, L), BF),
        ],
        compiler_params=pltpu.CompilerParams(vmem_limit_bytes=60 << 20),
        cost_estimate=pl.CostEstimate(
            flops=16 * N * D * ff, bytes_accessed=4 * D * ff + 24 * N * D, transcendentals=N * ff
        ),
        name="ffn",
    )(na, da, res, o, lo, wexp, wshr, rexp, rshr, eu, eur, hd, hdr, b, br, x0, x1, e1, e2, wout, gain, xb)


def project_kernel(meta_ref, dq_ref, dk_ref, dv_ref, w_ref, m_ref, *refs, W, js, r):
    count = len(js)
    n_refs, o_refs = refs[:count], refs[count : 2 * count]
    g_ref, n_ref, t_ref, wa_ref = refs[2 * count :]
    step = pl.program_id(0)
    j = step + js[0]
    me = meta_ref[0]
    D = w_ref.shape[0]
    rank = m_ref.shape[1]
    edge = D // 128 * 128
    for i in range(count):

        @pl.when(step == i)
        def _(i=i):
            n_ref[...] = n_refs[i][0]

    @pl.when(step == 0)
    def _():
        g_ref[...] = jnp.zeros_like(g_ref)
        wa_ref[:D] = w_ref[...]
        wa_ref[D : D + rank] = m_ref[0]
        wa_ref[D + rank :] = jnp.zeros((W - D - rank, 3 * W), BF)

    def work(pieces):
        low_t = taken(n_ref[:, edge:], D % 128 + r * rank, rank)
        total = sum(dot_nt(d[0], wa_ref[:, i * W : (i + 1) * W]) for i, d in pieces)
        for i, d in pieces:
            g_ref[i] += dot_nn(low_t, d[0])
        g_ref[3] += dot_nn(taken(total[:, edge:].astype(BF), D % 128, rank), n_ref[...])
        return total

    if js[0] == 0:

        @pl.when(j == 0)
        def _():
            o_refs[0][...] = work([(0, dq_ref), (1, dk_ref), (2, dv_ref)])

    if js[-1] > 0:

        @pl.when((j > 0) & ((me ^ j) < me))
        def _():
            t_ref[...] = work([(1, dk_ref), (2, dv_ref)]).astype(BF)

    for i in range(count):
        if js[i] > 0:

            @pl.when(step == i)
            def _(i=i):
                o_refs[i][...] = t_ref[...]


def project(meta, dq, dk, dv, w, m, n_parts, r, js):
    _, L, W = dq.shape
    rank = m.shape[1]
    count = len(js)
    out = pl.pallas_call(
        functools.partial(project_kernel, W=W, js=tuple(js), r=r),
        grid_spec=pltpu.PrefetchScalarGridSpec(
            num_scalar_prefetch=1,
            grid=(count,),
            in_specs=[
                whole_spec(dq.shape),
                pl.BlockSpec((1, L, W), lambda j, _: (0, j + js[0], 0)),
                pl.BlockSpec((1, L, W), lambda j, _: (0, j + js[0], 0)),
                whole_spec(w.shape),
                pl.BlockSpec((1, rank, 3 * W), lambda j, _: (r, 0, 0)),
            ]
            + [pl.BlockSpec((1, L, W), lambda j, _: (r, 0, 0))] * count,
            out_specs=[whole_spec((L, W))] * count + [whole_spec((4, rank, W))],
            scratch_shapes=[pltpu.VMEM((L, W), BF), pltpu.VMEM((L, W), BF), pltpu.VMEM((W, 3 * W), BF)],
        ),
        out_shape=[jax.ShapeDtypeStruct((L, W), BF if j else F32) for j in js]
        + [jax.ShapeDtypeStruct((4, rank, W), F32)],
        compiler_params=pltpu.CompilerParams(vmem_limit_bytes=60 << 20),
        cost_estimate=pl.CostEstimate(
            flops=8 * count * L * W * 2 * W, bytes_accessed=2 * (w.size + 4 * count * L * W), transcendentals=0
        ),
        name="project",
    )(meta, dq, dk, dv, w, m, *[n_parts[j] for j in js])
    return list(out[:count]), out[count]


def norm_kernel(x_ref, dy_ref, gain_ref, shift_ref, e_ref, n_ref, xr_ref, dyr_ref):
    x = x_ref[0].astype(F32)
    centred = x - jnp.mean(x, axis=0, keepdims=True)
    inv = lax.rsqrt(jnp.mean(centred * centred, axis=0, keepdims=True) + EPS)
    n = (centred * inv * gain_ref[...] + shift_ref[...]).astype(BF).T
    low = dot_nt(n, e_ref[0]).astype(BF)
    narrow = place(low, pl.program_id(0) * low.shape[1], n_ref.shape[2] - n.shape[1])
    n_ref[0] = jnp.concatenate([n, narrow], axis=1)
    xr_ref[0] = x_ref[0].T
    dyr_ref[0] = dy_ref[0].T


def first_norm(x_t, dy_t, gain, shift, e_t, W):
    R, D, L = x_t.shape
    col = pl.BlockSpec((1, D, L), lambda r: (r, 0, 0))
    row = pl.BlockSpec((1, L, D), lambda r: (r, 0, 0))
    return pl.pallas_call(
        norm_kernel,
        grid=(R,),
        in_specs=[col, col, whole_spec((D, 1)), whole_spec((D, 1)), pl.BlockSpec((1,) + e_t.shape[1:], lambda r: (r, 0, 0))],
        out_specs=[pl.BlockSpec((1, L, W), lambda r: (r, 0, 0)), row, row],
        out_shape=[jax.ShapeDtypeStruct((R, L, W), BF)] + [jax.ShapeDtypeStruct((R, L, D), BF)] * 2,
        compiler_params=pltpu.CompilerParams(vmem_limit_bytes=48 << 20),
        cost_estimate=pl.CostEstimate(flops=10 * x_t.size, bytes_accessed=10 * x_t.size, transcendentals=0),
        name="first_norm",
    )(x_t, dy_t, gain[:, None], shift[:, None], e_t)


def last_kernel(*refs, count, alias):
    if alias:
        refs = refs[1:]
    terms, (dr_ref, x_ref, gain_ref, e_ref, o_ref) = refs[:count], refs[count:]
    D = x_ref.shape[2]
    dn = terms[0][...]
    for t in terms[1:]:
        dn = dn + t[...].astype(F32)
    edge = D // 128 * 128
    rank = e_ref.shape[1]
    low_t = taken(dn[:, edge:].astype(BF), D % 128, rank)
    dn = dn[:, :D] + lax.dot_general(low_t, e_ref[0], (((0,), (0,)), ((), ())), preferred_element_type=F32)
    z, inv = layer_stats(x_ref[0].astype(F32))
    o_ref[0] = (dr_ref[0] + norm_back(dn * gain_ref[...], z, inv)).astype(BF).T


def last(r, before, terms, dr, x, gain, e_t):
    R, L, D = x.shape
    alias = before is not None
    return pl.pallas_call(
        functools.partial(last_kernel, count=len(terms), alias=alias),
        grid=(1,),
        in_specs=[pl.BlockSpec(memory_space=pl.ANY)] * alias
        + [whole_spec(t.shape) for t in terms]
        + [pl.BlockSpec((1, L, D), lambda i: (r, 0, 0))] * 2
        + [whole_spec((1, D)), pl.BlockSpec((1,) + e_t.shape[1:], lambda i: (r, 0, 0))],
        out_specs=pl.BlockSpec((1, D, L), lambda i: (r, 0, 0)),
        out_shape=jax.ShapeDtypeStruct((R, D, L), BF),
        input_output_aliases={0: 0} if alias else {},
        compiler_params=pltpu.CompilerParams(vmem_limit_bytes=48 << 20),
        cost_estimate=pl.CostEstimate(flops=20 * L * D, bytes_accessed=12 * L * D, transcendentals=0),
        name="last",
    )(*([before] if alias else []), *terms, dr, x, gain, e_t)


def late_kernel(slot_ref, part_ref, *refs, R, parts, D, W):
    g_refs, base_ref, mix_ref, entry_ref, total = refs[:R], refs[R], refs[R + 2], refs[R + 3], refs[R + 4]
    total[...] = base_ref[...]
    count = g_refs[0].shape[0]
    for r in range(R):

        def one(i, carry):
            a = slot_ref[r * count + i]
            c = part_ref[i]
            total[a, c] = total[a, c] + g_refs[r][i].astype(F32)
            return carry

        lax.fori_loop(0, count, one, 0)
    per = parts // 4
    wide = [jnp.concatenate([total[:, i * per + p] for p in range(per)], axis=-1) for i in range(4)]
    mix_ref[...] = jnp.concatenate([w[:, :, :D] for w in wide[:3]], axis=-1)
    entry_ref[0] = wide[3][:, :, :D]


def base_kernel(slot_ref, *refs):
    g_refs, total = refs[:-1], refs[-1]
    total[...] = jnp.zeros_like(total)
    count = g_refs[0].shape[0]
    for r, g_ref in enumerate(g_refs):

        def one(i, carry):
            a = slot_ref[r * count + i]
            total[a] = total[a] + g_ref[i].astype(F32)
            return carry

        lax.fori_loop(0, count, one, 0)


def late_base(slot, gs, adapters):
    shape = (adapters,) + gs[0].shape[1:]
    return pl.pallas_call(
        base_kernel,
        grid_spec=pltpu.PrefetchScalarGridSpec(
            num_scalar_prefetch=1, grid=(1,), in_specs=[whole_spec(g.shape) for g in gs], out_specs=whole_spec(shape)
        ),
        out_shape=jax.ShapeDtypeStruct(shape, F32),
        compiler_params=pltpu.CompilerParams(vmem_limit_bytes=48 << 20),
        cost_estimate=pl.CostEstimate(flops=0, bytes_accessed=8 << 20, transcendentals=0),
        name="late_base",
    )(slot, *gs)


def late_slots(slot, part, gs, base, entry, D, W):
    R = len(gs)
    adapters = entry.shape[1]
    _, rank, width = gs[-1].shape
    parts = 4 * W // width
    return pl.pallas_call(
        functools.partial(late_kernel, R=R, parts=parts, D=D, W=W),
        grid_spec=pltpu.PrefetchScalarGridSpec(
            num_scalar_prefetch=2,
            grid=(1,),
            in_specs=[whole_spec(g.shape) for g in (*gs, base)] + [pl.BlockSpec(memory_space=pl.ANY)],
            out_specs=[
                whole_spec((adapters, rank, 3 * D)),
                pl.BlockSpec((1, adapters, rank, D), lambda i, *_: (0, 0, 0, 0)),
            ],
            scratch_shapes=[pltpu.VMEM((adapters, parts, rank, width), F32)],
        ),
        out_shape=[
            jax.ShapeDtypeStruct((adapters, rank, 3 * D), F32),
            jax.ShapeDtypeStruct(entry.shape, F32),
        ],
        input_output_aliases={3 + R: 1},
        compiler_params=pltpu.CompilerParams(vmem_limit_bytes=60 << 20),
        cost_estimate=pl.CostEstimate(flops=0, bytes_accessed=12 << 20, transcendentals=0),
        name="late_slots",
    )(slot, part, *gs, base, entry)


def mm(pattern, a, b):
    return jnp.einsum(pattern, a, b, preferred_element_type=F32)


def layer_stats(v):
    middle = jnp.mean(v, axis=-1, keepdims=True)
    centred = v - middle
    inv = lax.rsqrt(jnp.mean(centred * centred, axis=-1, keepdims=True) + EPS)
    return centred * inv, inv


def norm_back(e, z, inv):
    return (e - jnp.mean(e, -1, keepdims=True) - z * jnp.mean(e * z, -1, keepdims=True)) * inv


def swap(x, axis, bit, needed):
    n = lax.axis_size(axis)
    return lax.ppermute(x, axis, [(d ^ bit, d) for d in range(n) if needed(d)])


def blocks_of(x, bits):
    found = {0: x}
    for bit in reversed(bits):
        for j in sorted(found):
            found[j | bit] = swap(found[j], "ctx", bit, lambda d, k=j | bit: (d ^ k) < d)
    return [found[j] for j in sorted(found)]


def block_sum(terms):
    return terms[0] if len(terms) == 1 else sum(t.astype(F32) for t in terms).astype(BF)


def blocks_back(held, bit):
    held = dict(held)
    for j in sorted(held):
        if j & bit:
            sent = block_sum(held.pop(j))
            got = swap(sent, "ctx", bit, lambda d, k=j, b=bit: ((d ^ b) ^ k) < (d ^ b))
            held[j ^ bit] = held[j ^ bit] + [got]
    return held


def turned_order(bits):
    count = 2 * bits[-1]
    return sorted(range(count), key=lambda c: [c & b for b in bits])


def ctx_sum_stage(g, bit):
    n = lax.axis_size("ctx")
    half = g.shape[0] // 2
    mine = (lax.axis_index("ctx") & bit) != 0
    low, high = g[:half], g[half:]
    got = lax.ppermute(jnp.where(mine, low, high), "ctx", [(d, d ^ bit) for d in range(n)])
    return jnp.where(mine, high, low) + got


def gather_all(x, seq_count, ctx_count, at, beside):
    n = seq_count * ctx_count
    seq_bits = [ctx_count << i for i in range(seq_count.bit_length() - 1)]
    ctx_bits = [1 << i for i in range(ctx_count.bit_length() - 1)]
    steps = seq_bits[::-1] + ctx_bits[::-1]
    held, order, beside = x[None], [0], list(beside)
    for i, bit in enumerate(steps):
        k = i - at
        if 0 <= k < len(beside):
            if callable(beside[k]):
                beside[k] = beside[k](beside[k - 1])
            held, beside[k] = lax.optimization_barrier((held, beside[k]))
        got = lax.ppermute(held, BOTH, [(d, d ^ bit) for d in range(n)])
        held = jnp.concatenate([held, got], 0)
        order = order + [o ^ bit for o in order]
    return held, order, beside


def slots_kernel(index_ref, g_ref, *refs, count, spans):
    outs, total = refs[:-1], refs[-1]
    total[...] = jnp.zeros_like(total)

    def one(i, carry):
        a = index_ref[i]
        total[a] = total[a] + g_ref[i].astype(F32)
        return carry

    lax.fori_loop(0, count, one, 0)
    for out, layers in zip(outs, spans):
        for i, pieces in enumerate(layers):
            parts = [total[:, :, first : first + width] for first, width in pieces]
            if parts:
                out[i] = parts[0] if len(parts) == 1 else jnp.concatenate(parts, axis=-1)


def to_slots(index, g, adapters, spans):
    count, rank, wide = g.shape
    rows = 8
    shapes = [(len(layers), adapters, rank, sum(w for _, w in layers[-1])) for layers in spans]
    return pl.pallas_call(
        functools.partial(slots_kernel, count=count, spans=spans),
        grid_spec=pltpu.PrefetchScalarGridSpec(
            num_scalar_prefetch=1,
            grid=(rank // rows,),
            in_specs=[pl.BlockSpec((count, rows, wide), lambda i, m: (0, i, 0))],
            out_specs=[pl.BlockSpec(s[:2] + (rows, s[3]), lambda i, m: (0, 0, i, 0)) for s in shapes],
            scratch_shapes=[pltpu.VMEM((adapters, rows, wide), F32)],
        ),
        out_shape=[jax.ShapeDtypeStruct(s, F32) for s in shapes],
        compiler_params=pltpu.CompilerParams(vmem_limit_bytes=48 << 20),
        cost_estimate=pl.CostEstimate(
            flops=count * rank * wide, bytes_accessed=count * rank * wide * 2 + adapters * rank * wide * 4, transcendentals=0
        ),
        name="to_slots",
    )(index, g)


def per_device(
    tokens, segments, adapter_index, norm_gains, norm_shifts, head_biases, expand_bias, exit_biases,
    mixing_weight, output_weight, expand_weight, shrink_weight,
    entry_adapters, mixing_adapters, expand_adapters, hidden_adapters, exit_adapters, cotangent,
):
    micro, seqs, L, D = tokens.shape
    R = micro * seqs
    adapters, rank = mixing_adapters.shape[:2]
    FF = expand_bias.shape[0]
    C = lax.axis_size("ctx")
    S = lax.axis_size("seq")
    bits = [1 << i for i in range(C.bit_length() - 1)]
    me = lax.axis_index("ctx")
    T = C * L
    W = -(-D // 128) * 128
    pad = W - D

    flip = lambda m: jnp.swapaxes(m, -1, -2)
    rows = mixing_weight.shape[0]
    cm, co, ce = mixing_weight.shape[1], output_weight.shape[1], expand_weight.shape[1]
    first = jnp.concatenate([mixing_weight, output_weight], 1)
    first = jnp.concatenate([first[: rows // 2], first[rows // 2 :]], 1)
    main = ce // 128 * 128
    rem = ce - main
    per = S // C
    shr_t = shrink_weight.T.reshape(co, per, ce).transpose(1, 0, 2)
    wide = first.shape[1]
    folded = lambda m: jnp.pad(
        m.reshape(-1, 8, m.shape[1]).transpose(1, 0, 2).reshape(8, -1), ((0, 0), (0, wide - m.size // 8))
    )
    rest = [folded(expand_weight[:, main:].T), folded(flip(shr_t[:, :, main:]).reshape(per * rem, co))]
    rest = jnp.concatenate(rest, 0)
    first = jnp.concatenate([first, rest], 0)
    second = jnp.concatenate([expand_weight[:, :main], shr_t[:, :, :main].reshape(per * co, main)], 0)
    g1 = lax.all_gather(first, BOTH)
    g2 = lax.all_gather(second, BOTH).reshape(S, C, -1, main)
    w_mix, w_out, r_exp, r_shr = unpack(g1, S, C, rows // 2, cm, co, D, W, rem, per)
    if rows % 16 == 0 and per * co == rows and co % 8 == 0:
        w_exp = w_shr = g2
    else:
        w_exp = g2[:, :, :rows].reshape(S, D, main)
        w_shr = g2[:, :, rows:].reshape(S, C, per, co, main).transpose(1, 2, 0, 3, 4).reshape(S, D, main)

    def split_ff(m):
        m = m.reshape(m.shape[:-1] + (S, ce))
        return m[..., :main].reshape(m.shape[:-2] + (S * main,)), m[..., main:].reshape(m.shape[:-2] + (S * rem,))

    index = adapter_index.reshape(R)
    take = lambda table, axis: jnp.stack(
        [lax.dynamic_index_in_dim(table, index[r], axis, keepdims=False) for r in range(R)], axis
    )
    entry = take(entry_adapters, 1)
    mix_up = take(mixing_adapters, 0)
    exp_up = take(expand_adapters, 0)
    hid = take(hidden_adapters, 0)
    exit_up = take(exit_adapters, 1)
    pad_heads = lambda m: jnp.concatenate([padded(m[..., i * D : (i + 1) * D]) for i in range(3)], -1)
    padded = lambda m: jnp.pad(m, [(0, 0)] * (m.ndim - 1) + [(0, pad)])
    mix_up = pad_heads(mix_up)
    entry_t = flip(entry)
    exp_main, exp_rest = split_ff(exp_up)
    hid_main, hid_rest = split_ff(flip(hid))
    bias_main, bias_rest = split_ff(expand_bias[None])
    head_bias = pad_heads(jnp.concatenate([head_biases[0], jnp.zeros_like(head_biases[0]), head_biases[1]])[None])

    seg = segments.reshape(R, L)
    seg_blocks = blocks_of(seg, bits)
    first_block = me * jnp.ones((R,), jnp.int32)
    for j, other in enumerate(seg_blocks):
        reached = ((me ^ j) <= me) & jnp.any(other == seg[:, :1], axis=1)
        first_block = jnp.where(reached, jnp.minimum(first_block, me ^ j), first_block)
    meta = jnp.concatenate([me[None], first_block]).astype(jnp.int32)
    qa, ka = document_lanes(seg, jnp.concatenate(seg_blocks, 1))

    n1, x, dy = first_norm(
        flip(tokens.reshape(R, L, D)), flip(cotangent.reshape(R, L, D)), norm_gains[0], norm_shifts[0],
        entry_t[0], W,
    )
    n1_parts = blocks_of(n1, bits)
    q, k, v = qkv(meta, n1_parts, w_mix, mix_up, head_bias)
    o, extra = attn_fwd(meta, q, k, v, qa, ka, D)

    res, na, da, lo = mid(
        o, x, dy, w_out, entry_t[1], entry_t[2], exit_up[0], exit_up[1], norm_gains[1][None], norm_shifts[1][None],
        exit_biases[0][None], W,
    )
    y, dr, do, g1, g2_, gx0, gx1, ge, ger, gh, ghr = ffn(
        na.reshape(R * L, W), da.reshape(R * L, W), res, o, lo, w_exp, w_shr, r_exp, r_shr,
        exp_main, exp_rest, hid_main, hid_rest, bias_main, bias_rest,
        exit_up[0], exit_up[1], entry_t[1], entry_t[2], w_out, norm_gains[1][None], exit_biases[1][None],
    )
    layer_output = flip(y).reshape(tokens.shape)

    number = jnp.broadcast_to((index.astype(F32) / C)[:, None, None], (R, rank, 128))
    early = jnp.concatenate([g1, g2_, gx0, gx1, ge, ger, gh, ghr, number], -1).reshape(R * rank, -1)
    swapped = turned_order(bits)
    share = R * rank // C
    early = jnp.concatenate([early[c * share : (c + 1) * share] for c in swapped], 0)

    pairs = W // 128
    ka_t = flip(ka)
    late, terms, held = [], [], None
    everything = list(range(C))
    for r in range(R):
        grads = ()
        cuts = [i * pairs // (len(bits) if held is None else 2) for i in range(len(bits) + 1 if held is None else 3)]
        for i, (p0, p1) in enumerate(zip(cuts, cuts[1:])):
            grads = attn_bwd(meta, q, k, v, do, o, extra, ka_t, r, p0, p1 - p0, grads)
            if held is None:
                early = ctx_sum_stage(early, bits[i])
                if i + 1 < len(bits):
                    do, early = lax.optimization_barrier((do, early))
            if held is not None and i == 0:
                held = blocks_back(held, bits[0])
                held = {j: [block_sum(t)] if j else t for j, t in held.items()}
                do, held = lax.optimization_barrier((do, held))
                for bit in bits[1:]:
                    held = blocks_back(held, bit)
        dq, dk, dv = grads
        if held is None:
            dk, early = lax.optimization_barrier((dk, early))
            early = lax.all_gather(early.astype(BF), BOTH).reshape(S * R, rank, -1)
        if held is not None:
            dk, held = lax.optimization_barrier((dk, held))
            terms.append(held[0])
        if r + 1 < R:
            parts, g = project(meta, dq, dk, dv, w_mix, mix_up, n1_parts, r, everything)
            held = {j: [p] for j, p in enumerate(parts)}
            do, held = lax.optimization_barrier((do, held))
        else:
            parts, g = project(meta, dq, dk, dv, w_mix, mix_up, n1_parts, r, everything)
            held = {j: [p] for j, p in enumerate(parts)}
            held = blocks_back(held, bits[0])
            held = {j: [block_sum(t)] if j else t for j, t in held.items()}
        g = g.reshape(4, rank, C // 4, -1).transpose(0, 2, 1, 3).reshape(C, rank, -1)
        if r + 1 < R:
            late.append(lax.all_gather(g.astype(BF), BOTH))
        else:
            g = jnp.concatenate([g[c : c + 1] for c in swapped], 0)
            for bit in bits:
                g = ctx_sum_stage(g, bit)
            g, held = lax.optimization_barrier((g, held))
            for bit in bits[1:]:
                held = blocks_back(held, bit)
            terms.append(held[0])
            grad_of = lambda i, before: last(i, before, terms[i], dr, x, norm_gains[0][None], entry_t[0])
            input_grad = None
            for i in range(R - 1):
                input_grad = grad_of(i, input_grad)
            all_index = early[:, 0, -1].astype(jnp.int32)
            both = []
            for at in (4 * D, 4 * D + FF):
                both.append([p for i in range(S) for p in ((at + i * main, main), (at + S * main + i * rem, rem))])
            entry_g, exit_g, expand_g, hidden_g = to_slots(
                all_index, early, adapters,
                [[[], [(0, D)], [(D, D)]], [[(2 * D, D)], [(3 * D, D)]], [both[0]], [both[1]]],
            )
            early_g = (entry_g, exit_g, expand_g, hidden_g)
            by_row = all_index.reshape(S, R)
            slot = jnp.concatenate([jnp.repeat(by_row[:, i], C) for i in range(R - 1)])
            before = (*early_g, input_grad, late_base(slot, late, adapters))
            last_late, order, beside = gather_all(
                g[0].astype(BF), S, C, S.bit_length() - 1,
                [before, lambda done: grad_of(r, done[4])],
            )
            entry_g, exit_g, expand_g, hidden_g = beside[0][:4]
            base = beside[0][5]
            input_grad = beside[1]
            late.append(last_late)
    device = lax.axis_index("seq") * C + me
    order = device ^ jnp.array(order, jnp.int32)
    slot = jnp.sum(jnp.where((order // C)[:, None] == jnp.arange(S), by_row[:, R - 1], 0), 1)
    mixing_g, entry_g = late_slots(slot, order % C, late[-1:], base, entry_g, D, W)
    input_grad = flip(input_grad).reshape(tokens.shape)

    return (
        layer_output,
        input_grad,
        flip(entry_g),
        mixing_g,
        expand_g[0],
        flip(hidden_g[0]),
        exit_g,
    )


def solution(mesh):
    rows = P(None, "seq", "ctx", None)
    weight = P("ctx", "seq")
    in_specs = (
        (rows, P(None, "seq", "ctx"), P(None, "seq")) + (P(),) * 5 + (weight,) * 4 + (P(),) * 5 + (rows,)
    )
    out_specs = (rows, rows) + (P(),) * 5
    return jax.shard_map(per_device, mesh=mesh, in_specs=in_specs, out_specs=out_specs, check_vma=False)
```
